32 devices in a mesh: rows: 8 (over z, x), keys: 4 (over y, core).
Axes of the slice: x: 2, y: 2, z: 4, core: 2. Of those that a mesh axis runs over, the one named last changes fastest.
Arguments:
- tokens: bfloat16 [8, 512, 1024], P('rows'), may hold values from -6 to 6
- cotangent: bfloat16 [8, 512, 1024], P('rows'), may hold values from -6 to 6
- segment_ids: int32 [8, 512], P('rows'), may hold values from 0 to 15, never falling along the last dimension, each value on 1 to 128 neighbouring positions
- pad_mask: int32 [8, 512], P('rows'), may hold values 0 or 1
- prefix_keys: bfloat16 [2, 64, 1024], P(None, 'keys'), may hold values from -6 to 6
- prefix_values: bfloat16 [2, 64, 1024], P(None, 'keys'), may hold values from -6 to 6
- w_query: bfloat16 [2, 1024, 1024], P(None, 'rows'), may hold values from -0.1875 to 0.1875
- w_key: bfloat16 [2, 1024, 1024], P(None, 'rows'), may hold values from -0.1875 to 0.1875
- w_value: bfloat16 [2, 1024, 1024], P(None, 'rows'), may hold values from -0.1875 to 0.1875
- w_out: bfloat16 [2, 1024, 1024], P(None, 'rows'), may hold values from -1 to 1
- w_up: bfloat16 [2, 1024, 4096], P(None, 'rows', 'keys'), may hold values from -0.1875 to 0.1875
- w_down_t: bfloat16 [2, 1024, 4096], P(None, 'rows', 'keys'), may hold values from -0.09375 to 0.09375
- norm1_gain: float32 [2, 1024], replicated, may hold values from 0.5 to 1.5
- norm1_bias: float32 [2, 1024], replicated, may hold values from -1.2 to 1.2
- norm2_gain: float32 [2, 1024], replicated, may hold values from 0.5 to 1.5
- norm2_bias: float32 [2, 1024], replicated, may hold values from -1.2 to 1.2
Outputs:
- activations: bfloat16 [8, 512, 1024], P('rows')
- grad_tokens: float32 [8, 512, 1024], P('rows')
- grad_prefix_keys: float32 [2, 64, 1024], P(None, 'keys')
- grad_prefix_values: float32 [2, 64, 1024], P(None, 'keys')
The draws below stay inside these ranges and needn't reach their ends.
Inputs may be any that keep to these rules, and one draw needn't show every extreme that they name: `segment_ids`: in each row the ids never fall; every id of 0 to 15 covers 1 to 128 consecutive tokens, and some sentence covers exactly 128.
All inputs are finite; a program needn't handle non-finite values. No bound on the sum of `pad_mask` on one device may be relied on, other than what follows from the above.
Results may differ from the reference program's by a relative error of at most 0.03.
Values may be sent and summed in bfloat16 or wider, within the bound.
A program may use at most 192 MiB of HBM per device.

```python
import math
import jax
import jax.numpy as jnp
import numpy as np
from jax import lax

D = 1024
HEADS = 16
HEAD = 64
FF = 4096
PREFIX = 64
LAYERS = 2
ROW_LEN = 512
SEGS = 16
SEG_MOST = 128
ROWS = 8


def place_ends(array, key, least, largest):
    shape = array.shape
    spot = [jax.random.randint(jax.random.fold_in(key, axis), (), 0, shape[axis]) for axis in range(len(shape))]
    array = array.at[tuple(spot)].set(least)
    longest = shape.index(max(shape))
    spot[longest] = (spot[longest] + 1) % shape[longest]
    return array.at[tuple(spot)].set(largest)


def shard_levels(stream_key, shape, pieces, smallest, high):
    gain, own = 1.0, jax.random.fold_in(stream_key, 6)
    for axis_at, shards_of in pieces:
        draws = jnp.exp(jax.random.uniform(jax.random.fold_in(own, axis_at), (shards_of,), jnp.float32, smallest / len(pieces), high / len(pieces)))
        gain = gain * jnp.repeat(draws, shape[axis_at] // shards_of).reshape([-1 if axis == axis_at else 1 for axis in range(len(shape))])
    return gain


def length_profile(number_of, total, most, skew):
    portions = [(1 << 20) // math.isqrt(grade ** skew) + 1 for grade in range(2, number_of + 1)]
    surplus, counts = total - most - (number_of - 1), [1] * (number_of - 1)
    while surplus > 0:
        free = [i for i in range(number_of - 1) if counts[i] < most]
        pool, budget = sum([portions[i] for i in free]), surplus
        for i in free:
            more = min(most - counts[i], max(1, budget * portions[i] // pool), surplus)
            counts[i] = counts[i] + more
            surplus = surplus - more
    return np.array([most] + counts)


def ragged_sizes(own_key, count, total, limit, skew):
    if count == 2:
        one = jax.random.randint(own_key, (), max(1, total - limit), min(limit, total - 1) + 1)
        return jnp.stack([one, total - one])
    tallies = jnp.asarray(length_profile(count, total, limit, skew), jnp.int32)
    twos = (count - 1) // 2
    source_of, taker = tallies[1:1 + 2 * twos:2], tallies[2:2 + 2 * twos:2]
    margin = jnp.minimum(source_of - 1, limit - taker)
    passed = jax.random.randint(jax.random.fold_in(own_key, 1), (twos,), 0, 1 << 20) % (margin + 1)
    tallies = tallies.at[1:1 + 2 * twos:2].set(source_of - passed).at[2:2 + 2 * twos:2].set(taker + passed)
    return tallies[jax.random.permutation(jax.random.fold_in(own_key, 2), count)]


def noise(stream_key, extent, scale, bound, shards=(), kind=jnp.bfloat16):
    level = shard_levels(stream_key, extent, shards, -0.22, 0.18) if shards else 1.0
    entries = jax.random.normal(stream_key, extent, jnp.float32) * scale * level
    return jnp.minimum(jnp.maximum(entries, -bound), bound).astype(kind)


def setup_inputs(seed: int = 0) -> dict:
    key_of = jax.random.split(jax.random.key(seed), 17)
    tokens = noise(key_of[0], (ROWS, ROW_LEN, D), 1.0, 6.0, ((0, 8),))
    cotangent = noise(key_of[1], (ROWS, ROW_LEN, D), 1.0, 6.0, ((0, 8),))
    segment_ids = jax.vmap(lambda own: jnp.searchsorted(jnp.cumsum(ragged_sizes(own, SEGS, ROW_LEN, SEG_MOST, 2)), jnp.arange(ROW_LEN), side="right"))(jax.random.split(key_of[2], ROWS)).reshape((ROWS, ROW_LEN)).astype(jnp.int32)
    pad_mask = place_ends((jax.random.randint(key_of[3], (ROWS, ROW_LEN), 0, 8) < 7).astype(jnp.int32), jax.random.fold_in(key_of[3], 1), 0, 1)
    prefix_keys = noise(key_of[4], (LAYERS, PREFIX, D), 1.0, 6.0, ((1, 4),))
    prefix_values = noise(key_of[5], (LAYERS, PREFIX, D), 1.0, 6.0, ((1, 4),))
    w_query = noise(key_of[6], (LAYERS, D, D), D ** -0.5, 0.1875, ((1, 8),))
    w_key = noise(key_of[7], (LAYERS, D, D), D ** -0.5, 0.1875, ((1, 8),))
    w_value = noise(key_of[8], (LAYERS, D, D), D ** -0.5, 0.1875, ((1, 8),))
    w_out = noise(key_of[9], (LAYERS, D, D), (D // 32) ** -0.5, 1.0, ((1, 8),))
    w_up = noise(key_of[10], (LAYERS, D, FF), D ** -0.5, 0.1875, ((1, 8), (2, 4)))
    w_down_t = noise(key_of[11], (LAYERS, D, FF), FF ** -0.5, 0.09375, ((1, 8), (2, 4)))
    norm1_gain = jnp.clip(1.0 + 0.1 * jax.random.normal(key_of[12], (LAYERS, D), jnp.float32), 0.5, 1.5)
    norm1_bias = noise(key_of[13], (LAYERS, D), 0.2, 1.2, (), jnp.float32)
    norm2_gain = jnp.clip(1.0 + 0.1 * jax.random.normal(key_of[14], (LAYERS, D), jnp.float32), 0.5, 1.5)
    norm2_bias = noise(key_of[15], (LAYERS, D), 0.2, 1.2, (), jnp.float32)
    return {"tokens": tokens, "cotangent": cotangent, "segment_ids": segment_ids, "pad_mask": pad_mask, "prefix_keys": prefix_keys, "prefix_values": prefix_values, "w_query": w_query, "w_key": w_key, "w_value": w_value, "w_out": w_out, "w_up": w_up, "w_down_t": w_down_t, "norm1_gain": norm1_gain, "norm1_bias": norm1_bias, "norm2_gain": norm2_gain, "norm2_bias": norm2_bias}


@jax.custom_vjp
def low(v):
    return lax.optimization_barrier(v.astype(jnp.bfloat16)).astype(jnp.float32)

@jax.custom_vjp
def low_back(v):
    return v

def low_keep(v):
    return (low(v), None)

def low_pass(kept, grad):
    return (grad,)

def back_keep(v):
    return (v, None)

def back_low(kept, grad):
    return (low(grad),)
low.defvjp(low_keep, low_pass)
low_back.defvjp(back_keep, back_low)
EPSILON = 1e-05
NEGATIVE = -1000000000.0
HIGHEST = lax.Precision.HIGHEST

def normalize(inputs, gain_vec, shift_vec):
    centre = inputs - lax.optimization_barrier(jnp.mean(inputs, axis=-1, keepdims=True))
    spread = lax.optimization_barrier(jnp.mean(centre * centre, axis=-1, keepdims=True))
    return centre * lax.rsqrt(spread + EPSILON) * gain_vec + shift_vec

def matmul(left_side, right_side):
    return jnp.dot(left_side, right_side, precision=HIGHEST, preferred_element_type=jnp.float32)

def layer_forward(hidden, segment_row, pad_row, layer_params, prefix_key, prefix_value):
    w_query, w_key, w_value, w_out, w_up, w_down, gain_one, bias_one, gain_two, bias_two = layer_params
    token_count = hidden.shape[0]
    prefix_count = prefix_key.shape[0]
    hidden_low = low(hidden)
    queries = low_back(low(HEAD ** (-0.5) * matmul(hidden_low, w_query)))
    keys_row = low_back(low(matmul(hidden_low, w_key)))
    values_row = low_back(low(matmul(hidden_low, w_value)))
    key_heads = jnp.concatenate([prefix_key, keys_row], axis=0).reshape(prefix_count + token_count, HEADS, HEAD)
    value_heads = jnp.concatenate([prefix_value, values_row], axis=0).reshape(prefix_count + token_count, HEADS, HEAD)
    same_segment = (segment_row[:, None] == segment_row[None, :]) & (pad_row[None, :] == 1)
    visible = jnp.concatenate([jnp.ones((token_count, prefix_count), dtype=bool), same_segment], axis=1)
    scores = jnp.einsum('qhd,khd->hqk', queries.reshape(token_count, HEADS, HEAD), key_heads, precision=HIGHEST)
    scores = low_back(jnp.where(visible[None], scores, NEGATIVE))
    log_total = jax.nn.logsumexp(scores, axis=-1, keepdims=True)
    shares = low(jnp.exp(scores - log_total))
    attended = jnp.einsum('hqk,khd->qhd', shares, value_heads, precision=HIGHEST).reshape(token_count, HEADS * HEAD)
    attended = low_back(low(attended))
    branch = low_back(matmul(attended, w_out))
    middle = normalize(hidden + branch, gain_one, bias_one)
    up_proj = low_back(matmul(low(middle), w_up))
    activated = low(jax.nn.gelu(up_proj, approximate=False))
    feed_out = low_back(matmul(activated, w_down.T))
    return normalize(middle + feed_out, gain_two, bias_two)

def reference(tokens, cotangent, segment_ids, pad_mask, prefix_keys, prefix_values, w_query, w_key, w_value, w_out, w_up, w_down_t, norm1_gain, norm1_bias, norm2_gain, norm2_bias):
    stacks = [matrix.astype(jnp.float32) for matrix in (w_query, w_key, w_value, w_out, w_up, w_down_t)]
    params_by_layer = [tuple((matrix[layer_index] for matrix in stacks)) + (norm1_gain[layer_index], norm1_bias[layer_index], norm2_gain[layer_index], norm2_bias[layer_index]) for layer_index in range(LAYERS)]

    def forward(token_rows, keys_prefix, values_prefix):

        def one_row(row_items):
            hidden, segment_row, pad_row = row_items
            for layer_index in range(LAYERS):
                hidden = layer_forward(hidden, segment_row, pad_row, params_by_layer[layer_index], keys_prefix[layer_index], values_prefix[layer_index])
            return hidden
        return lax.map(jax.checkpoint(one_row), (token_rows, segment_ids, pad_mask))
    outputs, backward = jax.vjp(forward, tokens.astype(jnp.float32), prefix_keys.astype(jnp.float32), prefix_values.astype(jnp.float32))
    grad_tokens, grad_keys, grad_values = backward(cotangent.astype(jnp.float32))
    return (outputs.astype(jnp.bfloat16), grad_tokens, grad_keys, grad_values)
```

```python
import functools

import jax
import jax.numpy as jnp
from jax import lax
from jax.experimental import pallas as pl
from jax.experimental.pallas import tpu as pltpu
from jax.sharding import PartitionSpec as P

HEAD = 64
LAYERS = 2
KEYS = 4
EPSILON = 1e-05
NEGATIVE = -1000000000.0
MESH = pl.DeviceIdType.MESH
BF = jnp.bfloat16
F32 = jnp.float32

AG_M0, AG_X1, AG_M1, AG_GF1, AG_GA1, AG_GF0, AG_GA0, AG_GX, AG_ACT = range(9)
GATHERS = 9
RS_A0, RS_F0, RS_A1, RS_F1, RS_GM1, RS_GX1, RS_GM0, RS_GX0 = range(8)
SCATTERS = 8


def dot_nn(a, b):
    return lax.dot_general(a, b, (((1,), (0,)), ((), ())), preferred_element_type=F32)


def dot_nt(a, b):
    return lax.dot_general(a, b, (((1,), (1,)), ((), ())), preferred_element_type=F32)


def dot_tn(a, b):
    return lax.dot_general(a, b, (((0,), (0,)), ((), ())), preferred_element_type=F32)


def kernel(
    dims,
    tokens, cotangent, seg_row, key_code, pre_k, pre_v,
    w_query, w_key, w_value, w_out, w_up, w_down,
    g1, b1, g2, b2,
    act_out, gt_out, gpk_out, gpv_out,
    wqkv, wo, wu, wd, pk, pv,
    part, rc, ry, ys, full,
    qkv, prob, gelu_d, zhat, rinv,
    own_x, own_m, own_g, cot, att, gqkv, gk, gv, hid, go, bias,
    pg, pg_in,
    w_send, w_recv, w_fwd, loc, pre_send, pre_recv,
    rs_send, rs_recv, ag_send, ag_recv, pg_send, pg_recv, pgr_send, pgr_recv,
):
    rows, tok, width, local_ff = dims
    nz = rows // 2
    wide = width // KEYS
    heads = wide // HEAD
    own = tok // KEYS
    half = tok // 2
    depth = width // rows
    count = pre_k.shape[1]
    prefix = KEYS * count
    window = 3 * own
    col = 256

    r = lax.axis_index("rows")
    k = lax.axis_index("keys")
    z, x = r // 2, lax.rem(r, 2)
    y, c = k // 2, lax.rem(k, 2)
    sib = (r, k + 1 - 2 * c)
    across = (r, lax.rem(k + 2, KEYS))
    beside = (r + 1 - 2 * x, k)
    far, near = 1 - y, y

    def level(d):
        return lax.rem(z + d, nz)

    barrier = pltpu.get_barrier_semaphore()

    def greet(d, carry):
        pl.semaphore_signal(barrier, inc=1, device_id=(level(d) * 2 + x, k), device_id_type=MESH)
        return carry

    lax.fori_loop(1, nz, greet, 0)
    pl.semaphore_signal(barrier, inc=1, device_id=beside, device_id_type=MESH)
    for d in range(1, KEYS):
        pl.semaphore_signal(barrier, inc=1, device_id=(r, lax.rem(k + d, KEYS)), device_id_type=MESH)

    group = nz // KEYS
    first_row = k * (rows // KEYS)

    def spot(ref, layer, at):
        return ref.at[layer, pl.ds(pl.multiple_of(at * depth, depth), depth), :]

    def slot(p, zz, xx):
        layer, kind = divmod(p, 4)
        at = zz * 2 + xx
        if kind == 1:
            return spot(wo, layer, at - first_row)
        return spot((wqkv, None, wu, wd)[kind], layer, at)

    def active(p, zz):
        return None if p % 4 != 1 else (zz // group) == k

    def guarded(condition, action):
        if condition is None:
            action()
        else:
            pl.when(condition)(action)

    columns = pl.ds(pl.multiple_of(k * wide, wide), wide)

    def own_copies(p):
        layer, kind = divmod(p, 4)
        if kind == 0:
            place = pl.ds(pl.multiple_of(r * depth, depth), depth)
            return [
                pltpu.make_async_copy(
                    w.at[layer, :, columns], wqkv.at[layer, place, i * wide : (i + 1) * wide], loc.at[p, i]
                )
                for i, w in enumerate((w_query, w_key, w_value))
            ]
        source = (None, w_out, w_up, w_down)[kind]
        return [pltpu.make_async_copy(source.at[layer], slot(p, z, x), loc.at[p, 0])]

    def own_start(p):
        guarded(active(p, z), lambda: [copy.start() for copy in own_copies(p)] and None)

    def own_wait(p):
        guarded(active(p, z), lambda: [copy.wait() for copy in own_copies(p)] and None)

    def push(p, zz, xx, send_sem, target):
        place = slot(p, zz, xx)
        return pltpu.make_async_remote_copy(
            src_ref=place, dst_ref=place, send_sem=send_sem, recv_sem=w_recv.at[p, xx, zz],
            device_id=target, device_id_type=MESH,
        )

    def to_level(p, d):
        return push(p, z, x, w_send.at[p, d], (level(d) * 2 + x, k))

    def issue(p):
        def action():
            def one(d, carry):
                to_level(p, d).start()
                return carry

            lax.fori_loop(1, nz, one, 0)
            push(p, z, x, w_send.at[p, 0], beside).start()

        guarded(active(p, z), action)

    def forward(p):
        def one(d, carry):
            zz = level(d)

            def action():
                copy = push(p, zz, x, w_fwd.at[p, zz], beside)
                copy.wait_recv()
                copy.start()

            guarded(active(p, zz), action)
            return carry

        lax.fori_loop(1, nz, one, 0)

    def arrive(p):
        def one(zz, carry):
            guarded(active(p, zz), push(p, zz, 1 - x, w_fwd.at[p, zz], beside).wait_recv)
            return carry

        lax.fori_loop(0, nz, one, 0)

    def drain(p):
        def action():
            def one(d, carry):
                to_level(p, d).wait_send()
                return carry

            lax.fori_loop(1, nz, one, 0)
            push(p, z, x, w_send.at[p, 0], beside).wait_send()

        guarded(active(p, z), action)

        def passed(d, carry):
            zz = level(d)
            guarded(active(p, zz), push(p, zz, x, w_fwd.at[p, zz], beside).wait_send)
            return carry

        lax.fori_loop(1, nz, passed, 0)

    def pre_copy(i, d):
        kt = lax.rem(k + d, KEYS)
        source, target = ((pre_k, pk), (pre_v, pv))[i]
        return pltpu.make_async_remote_copy(
            src_ref=source.at[:, :, pl.ds(pl.multiple_of(kt * wide, wide), wide)],
            dst_ref=target.at[:, pl.ds(pl.multiple_of(k * count, count), count), :],
            send_sem=pre_send.at[i, d], recv_sem=pre_recv.at[i, d], device_id=(r, kt), device_id_type=MESH,
        )

    def pre_own(i):
        source, target = ((pre_k, pk), (pre_v, pv))[i]
        return pltpu.make_async_copy(
            source.at[:, :, columns],
            target.at[:, pl.ds(pl.multiple_of(k * count, count), count), :],
            pre_recv.at[i, 0],
        )

    own_block = pl.ds(pl.multiple_of(k * own, own), own)
    cot_copy = pltpu.make_async_copy(cotangent.at[own_block, :], cot, loc.at[1, 1])

    for p in range(4 * LAYERS):
        own_start(p)
    cot_copy.start()
    for i in range(2):
        pre_own(i).start()

    pl.semaphore_wait(barrier, nz - 1 + 1 + KEYS - 1)
    for p in range(4 * LAYERS):
        own_wait(p)
        issue(p)
        if p == 0:
            for i in range(2):
                for d in range(1, KEYS):
                    pre_copy(i, d).start()
    cot_copy.wait()

    def block(ref, at, *lead):
        return ref.at[(*lead, pl.ds(pl.multiple_of(at * own, own), own), slice(None))]

    def rs_copy(n, which):
        if which == 2:
            source, target, device = ys, ry.at[n], across
        else:
            at = 2 * (far, near)[which] + 1 - c
            source, target, device = block(part, at), rc.at[n, which], sib
        return pltpu.make_async_remote_copy(
            src_ref=source, dst_ref=target, send_sem=rs_send.at[n, which], recv_sem=rs_recv.at[n, which],
            device_id=device, device_id_type=MESH,
        )

    def chunks(total, body, size=16):
        def one(i, carry):
            body(pl.multiple_of(i * size, size))
            return carry

        lax.fori_loop(0, total // size, one, 0)

    def rs_far(n):
        rs_copy(n, 0).start()

    def rs_mid(n):
        rs_copy(n, 0).wait_recv()
        mine = (2 * far + c) * own

        def add(i):
            total = part[pl.ds(mine + i, 16), :].astype(F32) + rc[n, 0, pl.ds(i, 16), :].astype(F32)
            ys[pl.ds(i, 16), :] = total.astype(BF)

        chunks(own, add)
        rs_copy(n, 2).start()

    def rs_near(n):
        rs_copy(n, 1).start()

    def rs_wait(n):
        rs_copy(n, 1).wait_recv()
        rs_copy(n, 2).wait_recv()

    def rs_sum(n, i):
        mine = part[pl.ds(k * own + i, 16), :].astype(F32) + rc[n, 1, pl.ds(i, 16), :].astype(F32)
        return mine + ry[n, pl.ds(i, 16), :].astype(F32)

    def rs_end(n):
        for which in range(3):
            rs_copy(n, which).wait_send()

    def ag_copy(n, which):
        at = (k, k, lax.rem(k + 2, KEYS))[which]
        place = block(full, at, n)
        return pltpu.make_async_remote_copy(
            src_ref=place, dst_ref=place, send_sem=ag_send.at[n, which], recv_sem=ag_recv.at[n, which],
            device_id=(across, sib, sib)[which], device_id_type=MESH,
        )

    def ag_start(n):
        ag_copy(n, 0).start()
        ag_copy(n, 1).start()

    def ag_near(n):
        ag_copy(n, 1).wait_recv()

    def ag_far(n):
        ag_copy(n, 0).wait_recv()
        ag_copy(n, 2).start()
        ag_copy(n, 2).wait_recv()

    def tiles(total, body):
        def one(j, carry):
            body(pl.multiple_of(j * col, col))
            return carry

        lax.fori_loop(0, total // col, one, 0)

    def half_rows(which):
        return pl.ds(pl.multiple_of(which * half, half), half)

    def project(layer, source, which):
        hr = half_rows(which)

        def body(j):
            val = dot_nn(source[hr, :], wqkv[layer, :, pl.ds(j, col)])
            scale = jnp.where(j < wide, HEAD**-0.5, 1.0)
            qkv[layer, hr, pl.ds(j, col)] = (val * scale).astype(BF)

        tiles(3 * wide, body)

    lane_head = lax.broadcasted_iota(jnp.int32, (1, wide), 1) // HEAD
    masks = [jnp.where(lane_head == h, 1.0, 0.0).astype(BF) for h in range(heads)]

    def stacked(value):
        return jnp.concatenate([value * mask for mask in masks], axis=0)

    def place_of(i):
        return pl.multiple_of(i * own, own)

    def window_of(i):
        return pl.multiple_of(jnp.clip(i - 1, 0, KEYS - 3) * own, own)

    def unstacked(value):
        parts = [value[h * HEAD : (h + 1) * HEAD, h * own : (h + 1) * own] for h in range(heads)]
        return jnp.concatenate(parts, axis=0).T

    def attend(layer, i):
        q4 = stacked(qkv[layer, pl.ds(place_of(i), own), 0:wide])
        span = pl.ds(window_of(i), window)
        mask = bias[i]
        s_tok = dot_nt(qkv[layer, span, wide : 2 * wide], q4) + jnp.concatenate([mask] * heads, axis=1)
        s_pre = dot_nt(pk[layer], q4)
        top = jnp.maximum(jnp.max(s_tok, axis=0, keepdims=True), jnp.max(s_pre, axis=0, keepdims=True))
        e_tok, e_pre = jnp.exp(s_tok - top), jnp.exp(s_pre - top)
        inverse = 1.0 / (jnp.sum(e_tok, axis=0, keepdims=True) + jnp.sum(e_pre, axis=0, keepdims=True))
        p_tok, p_pre = e_tok * inverse, e_pre * inverse
        prob[layer, i, 0:prefix, :] = p_pre
        prob[layer, i, prefix : prefix + window, :] = p_tok
        out = dot_tn(qkv[layer, span, 2 * wide : 3 * wide], p_tok.astype(BF))
        out += dot_tn(pv[layer], p_pre.astype(BF))
        att[pl.ds(place_of(i), own), :] = unstacked(out).astype(BF)

    def attend_half(layer, which):
        def one(i, carry):
            attend(layer, 2 * which + i)
            return carry

        lax.fori_loop(0, 2, one, 0)

    def attend_back(layer, i):
        at = pl.ds(place_of(i), own)
        q4 = stacked(qkv[layer, at, 0:wide])
        go4 = stacked(go[at, :])
        start = window_of(i)
        span = pl.ds(start, window)
        p_pre = prob[layer, i, 0:prefix, :]
        p_tok = prob[layer, i, prefix : prefix + window, :]
        gp_tok = dot_nt(qkv[layer, span, 2 * wide : 3 * wide], go4)
        gp_pre = dot_nt(pv[layer], go4)
        dsum = jnp.sum(p_tok * gp_tok, axis=0, keepdims=True) + jnp.sum(p_pre * gp_pre, axis=0, keepdims=True)
        gs_tok = (p_tok * (gp_tok - dsum)).astype(BF)
        gs_pre = (p_pre * (gp_pre - dsum)).astype(BF)
        places = pl.ds(prefix + start, window)
        gk[places, :] += dot_nn(gs_tok, q4)
        gk[0:prefix, :] += dot_nn(gs_pre, q4)
        gv[places, :] += dot_nn(p_tok.astype(BF), go4)
        gv[0:prefix, :] += dot_nn(p_pre.astype(BF), go4)
        gq = dot_tn(qkv[layer, span, wide : 2 * wide], gs_tok) + dot_tn(pk[layer], gs_pre)
        gqkv[at, 0:wide] = (unstacked(gq).astype(BF).astype(F32) * HEAD**-0.5).astype(BF)

    def attend_back_half(layer, which):
        def one(i, carry):
            attend_back(layer, 2 * which + i)
            return carry

        lax.fori_loop(0, 2, one, 0)

    def out_half(layer, which):
        hr = half_rows(which)

        def body(j):
            part[hr, pl.ds(j, col)] = dot_nn(att[hr, :], wo[layer, :, pl.ds(j, col)]).astype(BF)

        tiles(width, body)

    def up_half(layer, n, which):
        hr = half_rows(which)

        def body(j):
            u = dot_nn(full[n, hr, :], wu[layer, :, pl.ds(j, col)])
            for s in range(0, half, 32):
                v = u[s : s + 32]
                phi_sum = 0.5 * (1.0 + lax.erf(v * 0.7071067811865476))
                density = jnp.exp(v * v * -0.5) * 0.3989422804014327
                at = pl.ds(pl.multiple_of(which * half, half) + s, 32)
                hid[at, pl.ds(j, col)] = (v * phi_sum).astype(BF)
                gelu_d[layer, at, pl.ds(j, col)] = phi_sum + v * density

        tiles(local_ff, body)

    def down_half(layer, which):
        hr = half_rows(which)

        def body(j):
            part[hr, pl.ds(j, col)] = dot_nt(hid[hr, :], wd[layer, pl.ds(j, col), :]).astype(BF)

        tiles(width, body)

    def down_back_half(layer, n, which):
        hr = half_rows(which)

        def body(j):
            gg = dot_nn(full[n, hr, :], wd[layer, :, pl.ds(j, col)])
            hid[hr, pl.ds(j, col)] = (gg * gelu_d[layer, hr, pl.ds(j, col)]).astype(BF)

        tiles(local_ff, body)

    def up_back_half(layer, which):
        hr = half_rows(which)

        def body(j):
            part[hr, pl.ds(j, col)] = dot_nt(hid[hr, :], wu[layer, pl.ds(j, col), :]).astype(BF)

        tiles(width, body)

    def out_back_half(layer, n, which):
        hr = half_rows(which)
        go[hr, :] = dot_nt(full[n, hr, :], wo[layer]).astype(BF)

    def project_back_half(layer, which):
        hr = half_rows(which)

        def body(j):
            part[hr, pl.ds(j, col)] = dot_nt(gqkv[hr, :], wqkv[layer, pl.ds(j, col), :]).astype(BF)

        tiles(width, body)

    def norm_into(n, residual, layer, which, gain, shift, result, target):
        index = 2 * layer + which
        g, b = gain[layer : layer + 1, :], shift[layer : layer + 1, :]

        def body(i):
            value = residual[pl.ds(i, 16), :] + rs_sum(n, i)
            centre = value - jnp.mean(value, axis=-1, keepdims=True)
            inv = lax.rsqrt(jnp.mean(centre * centre, axis=-1, keepdims=True) + EPSILON)
            hat = centre * inv
            done = hat * g + b
            zhat[index, pl.ds(i, 16), :] = hat
            rinv[index, pl.ds(i, 16), :] = inv
            result[pl.ds(i, 16), :] = done
            full[target, pl.ds(k * own + i, 16), :] = done.astype(BF)

        chunks(own, body)

    def norm_back(read, layer, which, gain, target):
        index = 2 * layer + which
        g = gain[layer : layer + 1, :]

        def body(i):
            scaled = read(i) * g
            hat = zhat[index, pl.ds(i, 16), :]
            inv = rinv[index, pl.ds(i, 16), :]
            first = jnp.mean(scaled, axis=-1, keepdims=True)
            second = jnp.mean(scaled * hat, axis=-1, keepdims=True)
            result = inv * (scaled - first - hat * second)
            own_g[pl.ds(i, 16), :] = result
            full[target, pl.ds(k * own + i, 16), :] = result.astype(BF)

        chunks(own, body)

    def mask_of(i, carry):
        queries = seg_row[:, pl.ds(place_of(i), own)]
        codes = key_code[pl.ds(window_of(i), window), :]
        bias[i] = jnp.where(codes == queries, 0.0, NEGATIVE)
        return carry

    lax.fori_loop(0, KEYS, mask_of, 0)

    def widen(i):
        own_x[pl.ds(i, 16), :] = tokens[pl.ds(k * own + i, 16), :].astype(F32)

    chunks(own, widen)

    for i in range(2):
        pre_own(i).wait()
        for d in range(1, KEYS):
            pre_copy(i, d).wait_recv()

    for layer in range(LAYERS):
        base = 4 * layer
        rs_a, rs_f = ((RS_A0, RS_F0), (RS_A1, RS_F1))[layer]
        ag_m = (AG_M0, AG_M1)[layer]
        forward(base)
        arrive(base)
        if layer == 0:
            project(layer, tokens, near)
        else:
            ag_near(AG_X1)
            project(layer, full.at[AG_X1], near)
            ag_far(AG_X1)
        project(layer, tokens if layer == 0 else full.at[AG_X1], far)
        forward(base + 1)
        attend_half(layer, far)
        arrive(base + 1)
        out_half(layer, far)
        rs_far(rs_a)
        rs_mid(rs_a)
        attend_half(layer, near)
        out_half(layer, near)
        rs_near(rs_a)
        rs_wait(rs_a)
        norm_into(rs_a, own_x, layer, 0, g1, b1, own_m, ag_m)
        ag_start(ag_m)
        rs_end(rs_a)
        forward(base + 2)
        arrive(base + 2)
        ag_near(ag_m)
        up_half(layer, ag_m, near)
        forward(base + 3)
        ag_far(ag_m)
        up_half(layer, ag_m, far)
        arrive(base + 3)
        down_half(layer, far)
        rs_far(rs_f)
        rs_mid(rs_f)
        down_half(layer, near)
        rs_near(rs_f)
        rs_wait(rs_f)
        ag_y = AG_X1 if layer == 0 else AG_ACT
        norm_into(rs_f, own_m, layer, 1, g2, b2, own_x, ag_y)
        if layer == 0:
            ag_start(ag_y)
        rs_end(rs_f)

    def prefix_copy(layer, i, d):
        kt = lax.rem(k + d, KEYS)
        source = (gk, gv)[i]
        return pltpu.make_async_remote_copy(
            src_ref=source.at[pl.ds(pl.multiple_of(kt * count, count), count), :],
            dst_ref=pg.at[layer, i, :, columns],
            send_sem=pg_send.at[layer, i, d], recv_sem=pg_recv.at[layer, i, d],
            device_id=(r, kt), device_id_type=MESH,
        )

    def prefix_own(layer, i):
        return pltpu.make_async_copy(
            (gk, gv)[i].at[pl.ds(pl.multiple_of(k * count, count), count), :],
            pg.at[layer, i, :, columns],
            pg_recv.at[layer, i, 0],
        )

    bits = rows.bit_length() - 1

    def row_copy(layer, b):
        bit = 1 << b
        partner = r + bit - 2 * bit * lax.rem(r // bit, 2)
        return pltpu.make_async_remote_copy(
            src_ref=pg.at[layer], dst_ref=pg_in.at[layer, b],
            send_sem=pgr_send.at[layer, b], recv_sem=pgr_recv.at[layer, b],
            device_id=(partner, k), device_id_type=MESH,
        )

    def row_step(layer, b):
        copy = row_copy(layer, b)
        copy.wait()
        pg[layer] += pg_in[layer, b]

    for layer in reversed(range(LAYERS)):
        rs_gm, rs_gx = ((RS_GM0, RS_GX0), (RS_GM1, RS_GX1))[layer]
        ag_gf, ag_ga = ((AG_GF0, AG_GA0), (AG_GF1, AG_GA1))[layer]
        if layer == LAYERS - 1:
            norm_back(lambda i: cot[pl.ds(i, 16), :].astype(F32), layer, 1, g2, ag_gf)
        else:
            norm_back(lambda i: own_g[pl.ds(i, 16), :] + rs_sum(RS_GX1, i), layer, 1, g2, ag_gf)
        ag_start(ag_gf)
        if layer == LAYERS - 1:
            ag_start(AG_ACT)
        else:
            rs_end(RS_GX1)
        ag_near(ag_gf)
        down_back_half(layer, ag_gf, near)
        ag_far(ag_gf)
        down_back_half(layer, ag_gf, far)
        up_back_half(layer, far)
        rs_far(rs_gm)
        rs_mid(rs_gm)
        up_back_half(layer, near)
        rs_near(rs_gm)
        rs_wait(rs_gm)
        norm_back(lambda i: own_g[pl.ds(i, 16), :] + rs_sum(rs_gm, i), layer, 0, g1, ag_ga)
        ag_start(ag_ga)
        rs_end(rs_gm)
        if layer == LAYERS - 1:
            ag_far(AG_ACT)
            ag_near(AG_ACT)
        else:
            for i in range(2):
                for d in range(1, KEYS):
                    prefix_copy(layer + 1, i, d).wait_send()
        ag_near(ag_ga)
        out_back_half(layer, ag_ga, near)
        gk[...] = jnp.zeros_like(gk)
        gv[...] = jnp.zeros_like(gv)
        attend_back_half(layer, near)
        ag_far(ag_ga)
        out_back_half(layer, ag_ga, far)
        attend_back_half(layer, far)

        def narrow(i):
            gqkv[pl.ds(i, 16), wide : 2 * wide] = gk[pl.ds(prefix + i, 16), :].astype(BF)
            gqkv[pl.ds(i, 16), 2 * wide : 3 * wide] = gv[pl.ds(prefix + i, 16), :].astype(BF)

        chunks(tok, narrow)
        project_back_half(layer, far)
        rs_far(rs_gx)
        rs_mid(rs_gx)
        for i in range(2):
            prefix_own(layer, i).start()
            for d in range(1, KEYS):
                prefix_copy(layer, i, d).start()
        project_back_half(layer, near)
        rs_near(rs_gx)
        for i in range(2):
            prefix_own(layer, i).wait()
            for d in range(1, KEYS):
                prefix_copy(layer, i, d).wait_recv()
        row_copy(layer, 0).start()
        rs_wait(rs_gx)

    act_copy = pltpu.make_async_copy(full.at[AG_ACT], act_out, loc.at[1, 2])
    act_copy.start()

    def last(i):
        full[AG_GX, pl.ds(k * own + i, 16), :] = (own_g[pl.ds(i, 16), :] + rs_sum(RS_GX0, i)).astype(BF)

    chunks(own, last)
    ag_start(AG_GX)
    rs_end(RS_GX0)
    for b in range(bits):
        for layer in range(LAYERS):
            row_step(layer, b)
            if b + 1 < bits:
                row_copy(layer, b + 1).start()
    gpk_out[...] = pg[:, 0]
    gpv_out[...] = pg[:, 1]
    for i in range(2):
        for d in range(1, KEYS):
            prefix_copy(0, i, d).wait_send()
            pre_copy(i, d).wait_send()
    for p in range(4 * LAYERS):
        drain(p)
    ag_near(AG_GX)

    def spread(which):
        def body(i):
            at = pl.ds(pl.multiple_of(which * half, half) + i, 16)
            gt_out[at, :] = full[AG_GX, at, :].astype(F32)

        chunks(half, body)

    spread(near)
    ag_far(AG_GX)
    spread(far)
    for n in range(GATHERS):
        for which in range(3):
            ag_copy(n, which).wait_send()
    act_copy.wait()


def per_device(
    tokens, cotangent, segment_ids, pad_mask, prefix_keys, prefix_values,
    w_query, w_key, w_value, w_out, w_up, w_down_t,
    norm1_gain, norm1_bias, norm2_gain, norm2_bias,
):
    rows, keys = lax.axis_size("rows"), lax.axis_size("keys")
    assert keys == KEYS and rows % (2 * KEYS) == 0 and rows & (rows - 1) == 0
    tok, width = tokens.shape[1:]
    count = prefix_keys.shape[1]
    prefix = count * keys
    local_ff = w_up.shape[2]
    wide, own, window = width // keys, tok // keys, 3 * tok // keys
    heads = wide // HEAD
    nz, bits, pieces = rows // 2, rows.bit_length() - 1, 4 * LAYERS
    seg_row = segment_ids
    key_code = jnp.where(pad_mask == 1, segment_ids, -1).reshape(tok, 1)
    vmem, anywhere = pl.BlockSpec(memory_space=pltpu.VMEM), pl.BlockSpec(memory_space=pl.ANY)
    dma = pltpu.SemaphoreType.DMA
    scratch = [
        pltpu.VMEM((LAYERS, width, 3 * wide), BF),
        pltpu.VMEM((LAYERS, wide, width), BF),
        pltpu.VMEM((LAYERS, width, local_ff), BF),
        pltpu.VMEM((LAYERS, width, local_ff), BF),
        pltpu.VMEM((LAYERS, prefix, wide), BF),
        pltpu.VMEM((LAYERS, prefix, wide), BF),
        pltpu.VMEM((tok, width), BF),
        pltpu.VMEM((SCATTERS, 2, own, width), BF),
        pltpu.VMEM((SCATTERS, own, width), BF),
        pltpu.VMEM((own, width), BF),
        pltpu.VMEM((GATHERS, tok, width), BF),
        pltpu.VMEM((LAYERS, tok, 3 * wide), BF),
        pltpu.VMEM((LAYERS, keys, prefix + window, heads * own), F32),
        pltpu.VMEM((LAYERS, tok, local_ff), F32),
        pltpu.VMEM((2 * LAYERS, own, width), F32),
        pltpu.VMEM((2 * LAYERS, own, 1), F32),
        pltpu.VMEM((own, width), F32),
        pltpu.VMEM((own, width), F32),
        pltpu.VMEM((own, width), F32),
        pltpu.VMEM((own, width), BF),
        pltpu.VMEM((tok, wide), BF),
        pltpu.VMEM((tok, 3 * wide), BF),
        pltpu.VMEM((prefix + tok, wide), F32),
        pltpu.VMEM((prefix + tok, wide), F32),
        pltpu.VMEM((tok, local_ff), BF),
        pltpu.VMEM((tok, wide), BF),
        pltpu.VMEM((keys, window, own), F32),
        pltpu.VMEM((LAYERS, 2, count, width), F32),
        pltpu.VMEM((LAYERS, bits, 2, count, width), F32),
        dma((pieces, nz)),
        dma((pieces, 2, nz)),
        dma((pieces, nz)),
        dma((pieces, 3)),
        dma((2, keys)),
        dma((2, keys)),
        dma((SCATTERS, 3)),
        dma((SCATTERS, 3)),
        dma((GATHERS, 3)),
        dma((GATHERS, 3)),
        dma((LAYERS, 2, keys)),
        dma((LAYERS, 2, keys)),
        dma((LAYERS, bits)),
        dma((LAYERS, bits)),
    ]
    act, grad, grad_keys, grad_values = pl.pallas_call(
        functools.partial(kernel, (rows, tok, width, local_ff)),
        out_shape=(
            jax.ShapeDtypeStruct((tok, width), BF),
            jax.ShapeDtypeStruct((tok, width), F32),
            jax.ShapeDtypeStruct((LAYERS, count, width), F32),
            jax.ShapeDtypeStruct((LAYERS, count, width), F32),
        ),
        in_specs=[vmem, anywhere, vmem, vmem] + [anywhere] * 8 + [vmem] * 4,
        out_specs=(anywhere, vmem, vmem, vmem),
        scratch_shapes=scratch,
        compiler_params=pltpu.CompilerParams(
            collective_id=0, has_side_effects=True, vmem_limit_bytes=62 * 1024 * 1024 - 512 * 1024
        ),
    )(
        tokens[0], cotangent[0], seg_row, key_code, prefix_keys, prefix_values,
        w_query, w_key, w_value, w_out, w_up, w_down_t,
        norm1_gain, norm1_bias, norm2_gain, norm2_bias,
    )
    return act[None], grad[None], grad_keys, grad_values


def solution(mesh):
    row3 = P("rows", None, None)
    weight = P(None, "rows", None)
    return jax.shard_map(
        per_device,
        mesh=mesh,
        in_specs=(
            row3,
            row3,
            P("rows", None),
            P("rows", None),
            P(None, "keys", None),
            P(None, "keys", None),
            weight,
            weight,
            weight,
            weight,
            P(None, "rows", "keys"),
            P(None, "rows", "keys"),
            P(),
            P(),
            P(),
            P(),
        ),
        out_specs=(row3, row3, P(None, "keys", None), P(None, "keys", None)),
        check_vma=False,
    )
```

```python
import functools

import jax
import jax.numpy as jnp
from jax import lax
from jax.experimental import pallas as pl
from jax.experimental.pallas import tpu as pltpu
from jax.sharding import PartitionSpec as P

HEAD = 64
LAYERS = 2
KEYS = 4
EPSILON = 1e-05
NEGATIVE = -1000000000.0
MESH = pl.DeviceIdType.MESH
BF = jnp.bfloat16
F32 = jnp.float32

AG_M0, AG_X1, AG_M1, AG_GF1, AG_GA1, AG_GF0, AG_GA0, AG_GX, AG_ACT = range(9)
GATHERS = 9
RS_A0, RS_F0, RS_A1, RS_F1, RS_GM1, RS_GX1, RS_GM0, RS_GX0 = range(8)
SCATTERS = 8


def dot_nn(a, b):
    return lax.dot_general(a, b, (((1,), (0,)), ((), ())), preferred_element_type=F32)


def dot_nt(a, b):
    return lax.dot_general(a, b, (((1,), (1,)), ((), ())), preferred_element_type=F32)


def dot_tn(a, b):
    return lax.dot_general(a, b, (((0,), (0,)), ((), ())), preferred_element_type=F32)


def kernel(
    dims,
    tokens, cotangent, seg_row, key_code, pre_k, pre_v,
    w_query, w_key, w_value, w_out, w_up, w_down,
    g1, b1, g2, b2,
    act_out, gt_out, gpk_out, gpv_out,
    wqkv, wo, wu, wd, pk, pv,
    part, rc, ry, ys, full,
    qkv, prob, gelu_d, zhat, rinv,
    own_x, own_m, own_g, cot, att, gqkv, gk, gv, hid, go, bias,
    pg, pg_in,
    w_send, w_recv, w_over, loc, pre_send, pre_recv,
    rs_send, rs_recv, ag_send, ag_recv, pg_send, pg_recv, pgr_send, pgr_recv,
):
    rows, tok, width, local_ff = dims
    nz = rows // 2
    wide = width // KEYS
    heads = wide // HEAD
    own = tok // KEYS
    half = tok // 2
    depth = width // rows
    count = pre_k.shape[1]
    prefix = KEYS * count
    window = 3 * own
    col = 256

    r = lax.axis_index("rows")
    k = lax.axis_index("keys")
    z, x = r // 2, lax.rem(r, 2)
    y, c = k // 2, lax.rem(k, 2)
    sib = (r, k + 1 - 2 * c)
    across = (r, lax.rem(k + 2, KEYS))
    beside = (r + 1 - 2 * x, k)
    far, near = 1 - y, y

    def level(d):
        return lax.rem(z + d, nz)

    barrier = pltpu.get_barrier_semaphore()

    def greet(d, carry):
        pl.semaphore_signal(barrier, inc=1, device_id=(level(d) * 2 + x, k), device_id_type=MESH)
        return carry

    lax.fori_loop(1, nz, greet, 0)
    pl.semaphore_signal(barrier, inc=1, device_id=beside, device_id_type=MESH)
    for d in range(1, KEYS):
        pl.semaphore_signal(barrier, inc=1, device_id=(r, lax.rem(k + d, KEYS)), device_id_type=MESH)

    group = nz // KEYS
    first_row = k * (rows // KEYS)

    def spot(ref, layer, at):
        return ref.at[layer, pl.ds(pl.multiple_of(at * depth, depth), depth), :]

    def slot(p, zz, xx):
        layer, kind = divmod(p, 4)
        at = zz * 2 + xx
        if kind == 1:
            return spot(wo, layer, at - first_row)
        return spot((wqkv, None, wu, wd)[kind], layer, at)

    def active(p, zz):
        return None if p % 4 != 1 else (zz // group) == k

    def guarded(condition, action):
        if condition is None:
            action()
        else:
            pl.when(condition)(action)

    columns = pl.ds(pl.multiple_of(k * wide, wide), wide)

    def own_copies(p):
        layer, kind = divmod(p, 4)
        if kind == 0:
            place = pl.ds(pl.multiple_of(r * depth, depth), depth)
            return [
                pltpu.make_async_copy(
                    w.at[layer, :, columns], wqkv.at[layer, place, i * wide : (i + 1) * wide], loc.at[p, i]
                )
                for i, w in enumerate((w_query, w_key, w_value))
            ]
        source = (None, w_out, w_up, w_down)[kind]
        return [pltpu.make_async_copy(source.at[layer], slot(p, z, x), loc.at[p, 0])]

    def own_start(p):
        guarded(active(p, z), lambda: [copy.start() for copy in own_copies(p)] and None)

    def own_wait(p):
        guarded(active(p, z), lambda: [copy.wait() for copy in own_copies(p)] and None)

    def push(p, zz, xx, send_sem, target):
        place = slot(p, zz, xx)
        return pltpu.make_async_remote_copy(
            src_ref=place, dst_ref=place, send_sem=send_sem, recv_sem=w_recv.at[p, xx, zz],
            device_id=target, device_id_type=MESH,
        )

    def straight(p):
        return p == 4 * LAYERS - 1

    def up(p, zz, xx):
        return push(p, zz, xx, w_send.at[p, xx, zz], (lax.rem(z + 1, nz) * 2 + x, k))

    def down(p, zz, xx):
        sem = w_send.at[p, xx, jnp.where(zz == z, nz, zz)]
        return push(p, zz, xx, sem, (lax.rem(z + nz - 1, nz) * 2 + x, k))

    def over(p, zz):
        return push(p, zz, x, w_over.at[p, zz], beside)

    not_top, not_bottom = z < nz - 1, z > 0

    def spread_own(p, xx, action):
        pl.when(not_top)(lambda: action(up(p, z, xx)))
        pl.when(not_bottom)(lambda: action(down(p, z, xx)))

    def begin(copy):
        copy.start()

    def sent(copy):
        copy.wait_send()

    def issue(p):
        def action():
            spread_own(p, x, begin)
            over(p, z).start()

        guarded(active(p, z), action)

    def swap(p):
        over_in = push(p, z, 1 - x, w_over.at[p, z], beside)
        over_in.wait_recv()
        spread_own(p, 1 - x, begin)

    def hops(group, action):
        bounds = [1 + (nz - 1) * i // 3 for i in range(4)]

        def one(j, carry):
            pl.when(z - j >= 0)(lambda: action(jnp.maximum(z - j, 0), True))
            pl.when(z + j < nz)(lambda: action(jnp.minimum(z + j, nz - 1), False))
            return carry

        lax.fori_loop(bounds[group], bounds[group + 1], one, 0)

    def onward(p, zz, xx, below, action):
        if below:
            pl.when(not_top)(lambda: action(up(p, zz, xx)))
        else:
            pl.when(not_bottom)(lambda: action(down(p, zz, xx)))

    def passes(p, group):
        def action(zz, below):
            def take():
                for xx in (x, 1 - x) if straight(p) else (x,):
                    push(p, zz, xx, w_over.at[p, zz], beside).wait_recv()
                    onward(p, zz, xx, below, begin)
                if not straight(p):
                    over(p, zz).start()

            guarded(active(p, zz), take)

        hops(group, action)

    def arrive(p):
        if straight(p):
            return

        def one(zz, carry):
            guarded(active(p, zz), push(p, zz, 1 - x, w_over.at[p, zz], beside).wait_recv)
            return carry

        lax.fori_loop(0, nz, one, 0)

    def drain(p):
        def mine():
            spread_own(p, x, sent)
            if straight(p):
                spread_own(p, 1 - x, sent)
            over(p, z).wait_send()

        guarded(active(p, z), mine)

        def action(zz, below):
            def passed():
                for xx in (x, 1 - x) if straight(p) else (x,):
                    onward(p, zz, xx, below, sent)
                if not straight(p):
                    over(p, zz).wait_send()

            guarded(active(p, zz), passed)

        for group_at in range(3):
            hops(group_at, action)

    def pre_copy(i, d):
        kt = lax.rem(k + d, KEYS)
        source, target = ((pre_k, pk), (pre_v, pv))[i]
        return pltpu.make_async_remote_copy(
            src_ref=source.at[:, :, pl.ds(pl.multiple_of(kt * wide, wide), wide)],
            dst_ref=target.at[:, pl.ds(pl.multiple_of(k * count, count), count), :],
            send_sem=pre_send.at[i, d], recv_sem=pre_recv.at[i, d], device_id=(r, kt), device_id_type=MESH,
        )

    def pre_own(i):
        source, target = ((pre_k, pk), (pre_v, pv))[i]
        return pltpu.make_async_copy(
            source.at[:, :, columns],
            target.at[:, pl.ds(pl.multiple_of(k * count, count), count), :],
            pre_recv.at[i, 0],
        )

    own_block = pl.ds(pl.multiple_of(k * own, own), own)
    cot_copy = pltpu.make_async_copy(cotangent.at[own_block, :], cot, loc.at[1, 1])

    for p in range(4 * LAYERS):
        own_start(p)
    cot_copy.start()
    for i in range(2):
        pre_own(i).start()

    pl.semaphore_wait(barrier, nz - 1 + 1 + KEYS - 1)
    own_wait(0)
    issue(0)
    for i in range(2):
        for d in range(1, KEYS):
            pre_copy(i, d).start()
    for p in range(1, 4 * LAYERS):
        own_wait(p)
    issue(1)
    issue(2)
    cot_copy.wait()

    def block(ref, at, *lead):
        return ref.at[(*lead, pl.ds(pl.multiple_of(at * own, own), own), slice(None))]

    def rs_copy(n, which):
        if which == 2:
            source, target, device = ys, ry.at[n], across
        else:
            at = 2 * (far, near)[which] + 1 - c
            source, target, device = block(part, at), rc.at[n, which], sib
        return pltpu.make_async_remote_copy(
            src_ref=source, dst_ref=target, send_sem=rs_send.at[n, which], recv_sem=rs_recv.at[n, which],
            device_id=device, device_id_type=MESH,
        )

    def chunks(total, body, size=16):
        def one(i, carry):
            body(pl.multiple_of(i * size, size))
            return carry

        lax.fori_loop(0, total // size, one, 0)

    def rs_far(n):
        rs_copy(n, 0).start()

    def rs_mid(n):
        rs_copy(n, 0).wait_recv()
        mine = (2 * far + c) * own

        def add(i):
            total = part[pl.ds(mine + i, 16), :].astype(F32) + rc[n, 0, pl.ds(i, 16), :].astype(F32)
            ys[pl.ds(i, 16), :] = total.astype(BF)

        chunks(own, add)
        rs_copy(n, 2).start()

    def rs_near(n):
        rs_copy(n, 1).start()

    def rs_wait(n):
        rs_copy(n, 1).wait_recv()
        rs_copy(n, 2).wait_recv()

    def rs_sum(n, i):
        mine = part[pl.ds(k * own + i, 16), :].astype(F32) + rc[n, 1, pl.ds(i, 16), :].astype(F32)
        return mine + ry[n, pl.ds(i, 16), :].astype(F32)

    def rs_end(n):
        for which in range(3):
            rs_copy(n, which).wait_send()

    def ag_copy(n, which):
        at = (k, k, lax.rem(k + 2, KEYS))[which]
        place = block(full, at, n)
        return pltpu.make_async_remote_copy(
            src_ref=place, dst_ref=place, send_sem=ag_send.at[n, which], recv_sem=ag_recv.at[n, which],
            device_id=(across, sib, sib)[which], device_id_type=MESH,
        )

    def ag_start(n):
        ag_copy(n, 0).start()
        ag_copy(n, 1).start()

    def ag_near(n):
        ag_copy(n, 1).wait_recv()

    def ag_far(n):
        ag_copy(n, 0).wait_recv()
        ag_copy(n, 2).start()
        ag_copy(n, 2).wait_recv()

    def tiles(total, body):
        def one(j, carry):
            body(pl.multiple_of(j * col, col))
            return carry

        lax.fori_loop(0, total // col, one, 0)

    def half_rows(which):
        return pl.ds(pl.multiple_of(which * half, half), half)

    def project(layer, source, which):
        hr = half_rows(which)

        def body(j):
            val = dot_nn(source[hr, :], wqkv[layer, :, pl.ds(j, col)])
            scale = jnp.where(j < wide, HEAD**-0.5, 1.0)
            qkv[layer, hr, pl.ds(j, col)] = (val * scale).astype(BF)

        tiles(3 * wide, body)

    lane_head = lax.broadcasted_iota(jnp.int32, (1, wide), 1) // HEAD
    masks = [jnp.where(lane_head == h, 1.0, 0.0).astype(BF) for h in range(heads)]

    def stacked(value):
        return jnp.concatenate([value * mask for mask in masks], axis=0)

    def place_of(i):
        return pl.multiple_of(i * own, own)

    def window_of(i):
        return pl.multiple_of(jnp.clip(i - 1, 0, KEYS - 3) * own, own)

    def unstacked(value):
        parts = [value[h * HEAD : (h + 1) * HEAD, h * own : (h + 1) * own] for h in range(heads)]
        return jnp.concatenate(parts, axis=0).T

    def attend(layer, i):
        q4 = stacked(qkv[layer, pl.ds(place_of(i), own), 0:wide])
        span = pl.ds(window_of(i), window)
        mask = bias[i]
        s_tok = dot_nt(qkv[layer, span, wide : 2 * wide], q4) + jnp.concatenate([mask] * heads, axis=1)
        s_pre = dot_nt(pk[layer], q4)
        top = jnp.maximum(jnp.max(s_tok, axis=0, keepdims=True), jnp.max(s_pre, axis=0, keepdims=True))
        e_tok, e_pre = jnp.exp(s_tok - top), jnp.exp(s_pre - top)
        inverse = 1.0 / (jnp.sum(e_tok, axis=0, keepdims=True) + jnp.sum(e_pre, axis=0, keepdims=True))
        p_tok, p_pre = e_tok * inverse, e_pre * inverse
        prob[layer, i, 0:prefix, :] = p_pre
        prob[layer, i, prefix : prefix + window, :] = p_tok
        out = dot_tn(qkv[layer, span, 2 * wide : 3 * wide], p_tok.astype(BF))
        out += dot_tn(pv[layer], p_pre.astype(BF))
        att[pl.ds(place_of(i), own), :] = unstacked(out).astype(BF)

    def attend_half(layer, which):
        def one(i, carry):
            attend(layer, 2 * which + i)
            return carry

        lax.fori_loop(0, 2, one, 0)

    def attend_back(layer, i):
        at = pl.ds(place_of(i), own)
        q4 = stacked(qkv[layer, at, 0:wide])
        go4 = stacked(go[at, :])
        start = window_of(i)
        span = pl.ds(start, window)
        p_pre = prob[layer, i, 0:prefix, :]
        p_tok = prob[layer, i, prefix : prefix + window, :]
        gp_tok = dot_nt(qkv[layer, span, 2 * wide : 3 * wide], go4)
        gp_pre = dot_nt(pv[layer], go4)
        dsum = jnp.sum(p_tok * gp_tok, axis=0, keepdims=True) + jnp.sum(p_pre * gp_pre, axis=0, keepdims=True)
        gs_tok = (p_tok * (gp_tok - dsum)).astype(BF)
        gs_pre = (p_pre * (gp_pre - dsum)).astype(BF)
        places = pl.ds(prefix + start, window)
        gk[places, :] += dot_nn(gs_tok, q4)
        gk[0:prefix, :] += dot_nn(gs_pre, q4)
        gv[places, :] += dot_nn(p_tok.astype(BF), go4)
        gv[0:prefix, :] += dot_nn(p_pre.astype(BF), go4)
        gq = dot_tn(qkv[layer, span, wide : 2 * wide], gs_tok) + dot_tn(pk[layer], gs_pre)
        gqkv[at, 0:wide] = (unstacked(gq).astype(BF).astype(F32) * HEAD**-0.5).astype(BF)

    def attend_back_half(layer, which):
        def one(i, carry):
            attend_back(layer, 2 * which + i)
            return carry

        lax.fori_loop(0, 2, one, 0)

    def out_half(layer, which):
        hr = half_rows(which)

        def body(j):
            part[hr, pl.ds(j, col)] = dot_nn(att[hr, :], wo[layer, :, pl.ds(j, col)]).astype(BF)

        tiles(width, body)

    def up_half(layer, n, which):
        hr = half_rows(which)

        def body(j):
            u = dot_nn(full[n, hr, :], wu[layer, :, pl.ds(j, col)])
            for s in range(0, half, 32):
                v = u[s : s + 32]
                phi_sum = 0.5 * (1.0 + lax.erf(v * 0.7071067811865476))
                density = jnp.exp(v * v * -0.5) * 0.3989422804014327
                at = pl.ds(pl.multiple_of(which * half, half) + s, 32)
                hid[at, pl.ds(j, col)] = (v * phi_sum).astype(BF)
                gelu_d[layer, at, pl.ds(j, col)] = phi_sum + v * density

        tiles(local_ff, body)

    def down_half(layer, which):
        hr = half_rows(which)

        def body(j):
            part[hr, pl.ds(j, col)] = dot_nt(hid[hr, :], wd[layer, pl.ds(j, col), :]).astype(BF)

        tiles(width, body)

    def down_back_half(layer, n, which):
        hr = half_rows(which)

        def body(j):
            gg = dot_nn(full[n, hr, :], wd[layer, :, pl.ds(j, col)])
            hid[hr, pl.ds(j, col)] = (gg * gelu_d[layer, hr, pl.ds(j, col)]).astype(BF)

        tiles(local_ff, body)

    def up_back_half(layer, which):
        hr = half_rows(which)

        def body(j):
            part[hr, pl.ds(j, col)] = dot_nt(hid[hr, :], wu[layer, pl.ds(j, col), :]).astype(BF)

        tiles(width, body)

    def out_back_half(layer, n, which):
        hr = half_rows(which)
        go[hr, :] = dot_nt(full[n, hr, :], wo[layer]).astype(BF)

    def project_back_half(layer, which):
        hr = half_rows(which)

        def body(j):
            part[hr, pl.ds(j, col)] = dot_nt(gqkv[hr, :], wqkv[layer, pl.ds(j, col), :]).astype(BF)

        tiles(width, body)

    def norm_into(n, residual, layer, which, gain, shift, result, target):
        index = 2 * layer + which
        g, b = gain[layer : layer + 1, :], shift[layer : layer + 1, :]

        def body(i):
            value = residual[pl.ds(i, 16), :] + rs_sum(n, i)
            centre = value - jnp.mean(value, axis=-1, keepdims=True)
            inv = lax.rsqrt(jnp.mean(centre * centre, axis=-1, keepdims=True) + EPSILON)
            hat = centre * inv
            done = hat * g + b
            zhat[index, pl.ds(i, 16), :] = hat
            rinv[index, pl.ds(i, 16), :] = inv
            result[pl.ds(i, 16), :] = done
            full[target, pl.ds(k * own + i, 16), :] = done.astype(BF)

        chunks(own, body)

    def norm_back(read, layer, which, gain, target):
        index = 2 * layer + which
        g = gain[layer : layer + 1, :]

        def body(i):
            scaled = read(i) * g
            hat = zhat[index, pl.ds(i, 16), :]
            inv = rinv[index, pl.ds(i, 16), :]
            first = jnp.mean(scaled, axis=-1, keepdims=True)
            second = jnp.mean(scaled * hat, axis=-1, keepdims=True)
            result = inv * (scaled - first - hat * second)
            own_g[pl.ds(i, 16), :] = result
            full[target, pl.ds(k * own + i, 16), :] = result.astype(BF)

        chunks(own, body)

    def mask_of(i, carry):
        queries = seg_row[:, pl.ds(place_of(i), own)]
        codes = key_code[pl.ds(window_of(i), window), :]
        bias[i] = jnp.where(codes == queries, 0.0, NEGATIVE)
        return carry

    lax.fori_loop(0, KEYS, mask_of, 0)

    def widen(i):
        own_x[pl.ds(i, 16), :] = tokens[pl.ds(k * own + i, 16), :].astype(F32)

    chunks(own, widen)

    for i in range(2):
        pre_own(i).wait()
        for d in range(1, KEYS):
            pre_copy(i, d).wait_recv()

    def forward_layer(layer, first, second, third, fourth, fifth):
        base = 4 * layer
        rs_a, rs_f = ((RS_A0, RS_F0), (RS_A1, RS_F1))[layer]
        ag_m = (AG_M0, AG_M1)[layer]
        source = tokens if layer == 0 else full.at[AG_X1]
        first()
        arrive(base)
        if layer > 0:
            ag_near(AG_X1)
        project(layer, source, near)
        if layer > 0:
            ag_far(AG_X1)
        project(layer, source, far)
        second()
        attend_half(layer, far)
        arrive(base + 1)
        out_half(layer, far)
        rs_far(rs_a)
        rs_mid(rs_a)
        attend_half(layer, near)
        out_half(layer, near)
        rs_near(rs_a)
        third()
        rs_wait(rs_a)
        norm_into(rs_a, own_x, layer, 0, g1, b1, own_m, ag_m)
        ag_start(ag_m)
        rs_end(rs_a)
        fourth()
        arrive(base + 2)
        ag_near(ag_m)
        up_half(layer, ag_m, near)
        ag_far(ag_m)
        up_half(layer, ag_m, far)
        fifth()
        arrive(base + 3)
        down_half(layer, far)
        rs_far(rs_f)
        rs_mid(rs_f)
        down_half(layer, near)
        rs_near(rs_f)

    def events(*calls):
        def run():
            for call in calls:
                if len(call) == 1:
                    issue(call[0])
                elif call[1] == 0:
                    swap(call[0])
                else:
                    passes(call[0], call[1] - 1)

        return run

    forward_layer(
        0,
        events((0, 1), (0, 2), (0, 3), (1, 1), (3,)),
        events((1, 2), (1, 3), (2, 1)),
        events((2, 2), (2, 3), (3, 1), (4,)),
        events((3, 2), (3, 3), (4, 1), (5,)),
        events((4, 2), (4, 3), (5, 1), (6,)),
    )
    events((5, 2), (5, 3), (6, 1), (7,))()
    rs_wait(RS_F0)
    norm_into(RS_F0, own_m, 0, 1, g2, b2, own_x, AG_X1)
    ag_start(AG_X1)
    rs_end(RS_F0)
    forward_layer(
        1,
        events((6, 2), (7, 0), (6, 3)),
        events(),
        events((7, 1)),
        events((7, 2)),
        events((7, 3)),
    )
    rs_wait(RS_F1)
    norm_into(RS_F1, own_m, 1, 1, g2, b2, own_x, AG_ACT)
    rs_end(RS_F1)

    def prefix_copy(layer, i, d):
        kt = lax.rem(k + d, KEYS)
        source = (gk, gv)[i]
        return pltpu.make_async_remote_copy(
            src_ref=source.at[pl.ds(pl.multiple_of(kt * count, count), count), :],
            dst_ref=pg.at[layer, i, :, columns],
            send_sem=pg_send.at[layer, i, d], recv_sem=pg_recv.at[layer, i, d],
            device_id=(r, kt), device_id_type=MESH,
        )

    def prefix_own(layer, i):
        return pltpu.make_async_copy(
            (gk, gv)[i].at[pl.ds(pl.multiple_of(k * count, count), count), :],
            pg.at[layer, i, :, columns],
            pg_recv.at[layer, i, 0],
        )

    bits = rows.bit_length() - 1

    def row_copy(layer, b):
        bit = 1 << b
        partner = r + bit - 2 * bit * lax.rem(r // bit, 2)
        return pltpu.make_async_remote_copy(
            src_ref=pg.at[layer], dst_ref=pg_in.at[layer, b],
            send_sem=pgr_send.at[layer, b], recv_sem=pgr_recv.at[layer, b],
            device_id=(partner, k), device_id_type=MESH,
        )

    def row_step(layer, b):
        copy = row_copy(layer, b)
        copy.wait()
        pg[layer] += pg_in[layer, b]

    for layer in reversed(range(LAYERS)):
        rs_gm, rs_gx = ((RS_GM0, RS_GX0), (RS_GM1, RS_GX1))[layer]
        ag_gf, ag_ga = ((AG_GF0, AG_GA0), (AG_GF1, AG_GA1))[layer]
        if layer == LAYERS - 1:
            norm_back(lambda i: cot[pl.ds(i, 16), :].astype(F32), layer, 1, g2, ag_gf)
        else:
            norm_back(lambda i: own_g[pl.ds(i, 16), :] + rs_sum(RS_GX1, i), layer, 1, g2, ag_gf)
        ag_start(ag_gf)
        if layer == LAYERS - 1:
            ag_start(AG_ACT)
        else:
            rs_end(RS_GX1)
        ag_near(ag_gf)
        down_back_half(layer, ag_gf, near)
        ag_far(ag_gf)
        down_back_half(layer, ag_gf, far)
        up_back_half(layer, far)
        rs_far(rs_gm)
        rs_mid(rs_gm)
        up_back_half(layer, near)
        rs_near(rs_gm)
        rs_wait(rs_gm)
        norm_back(lambda i: own_g[pl.ds(i, 16), :] + rs_sum(rs_gm, i), layer, 0, g1, ag_ga)
        ag_start(ag_ga)
        rs_end(rs_gm)
        if layer == LAYERS - 1:
            ag_far(AG_ACT)
            ag_near(AG_ACT)
        else:
            for i in range(2):
                for d in range(1, KEYS):
                    prefix_copy(layer + 1, i, d).wait_send()
        ag_near(ag_ga)
        out_back_half(layer, ag_ga, near)
        gk[...] = jnp.zeros_like(gk)
        gv[...] = jnp.zeros_like(gv)
        attend_back_half(layer, near)
        ag_far(ag_ga)
        out_back_half(layer, ag_ga, far)
        attend_back_half(layer, far)

        def narrow(i):
            gqkv[pl.ds(i, 16), wide : 2 * wide] = gk[pl.ds(prefix + i, 16), :].astype(BF)
            gqkv[pl.ds(i, 16), 2 * wide : 3 * wide] = gv[pl.ds(prefix + i, 16), :].astype(BF)

        chunks(tok, narrow)
        project_back_half(layer, far)
        rs_far(rs_gx)
        rs_mid(rs_gx)
        for i in range(2):
            prefix_own(layer, i).start()
            for d in range(1, KEYS):
                prefix_copy(layer, i, d).start()
        project_back_half(layer, near)
        rs_near(rs_gx)
        for i in range(2):
            prefix_own(layer, i).wait()
            for d in range(1, KEYS):
                prefix_copy(layer, i, d).wait_recv()
        row_copy(layer, 0).start()
        rs_wait(rs_gx)

    act_copy = pltpu.make_async_copy(full.at[AG_ACT], act_out, loc.at[1, 2])
    act_copy.start()

    def last(i):
        full[AG_GX, pl.ds(k * own + i, 16), :] = (own_g[pl.ds(i, 16), :] + rs_sum(RS_GX0, i)).astype(BF)

    chunks(own, last)
    ag_start(AG_GX)
    rs_end(RS_GX0)
    for b in range(bits):
        for layer in range(LAYERS):
            row_step(layer, b)
            if b + 1 < bits:
                row_copy(layer, b + 1).start()
    gpk_out[...] = pg[:, 0]
    gpv_out[...] = pg[:, 1]
    for i in range(2):
        for d in range(1, KEYS):
            prefix_copy(0, i, d).wait_send()
            pre_copy(i, d).wait_send()
    for p in range(4 * LAYERS):
        drain(p)
    ag_near(AG_GX)

    def spread(which):
        def body(i):
            at = pl.ds(pl.multiple_of(which * half, half) + i, 16)
            gt_out[at, :] = full[AG_GX, at, :].astype(F32)

        chunks(half, body)

    spread(near)
    ag_far(AG_GX)
    spread(far)
    for n in range(GATHERS):
        for which in range(3):
            ag_copy(n, which).wait_send()
    act_copy.wait()


def per_device(
    tokens, cotangent, segment_ids, pad_mask, prefix_keys, prefix_values,
    w_query, w_key, w_value, w_out, w_up, w_down_t,
    norm1_gain, norm1_bias, norm2_gain, norm2_bias,
):
    rows, keys = lax.axis_size("rows"), lax.axis_size("keys")
    assert keys == KEYS and rows % (2 * KEYS) == 0 and rows & (rows - 1) == 0
    tok, width = tokens.shape[1:]
    count = prefix_keys.shape[1]
    prefix = count * keys
    local_ff = w_up.shape[2]
    wide, own, window = width // keys, tok // keys, 3 * tok // keys
    heads = wide // HEAD
    nz, bits, pieces = rows // 2, rows.bit_length() - 1, 4 * LAYERS
    seg_row = segment_ids
    key_code = jnp.where(pad_mask == 1, segment_ids, -1).reshape(tok, 1)
    vmem, anywhere = pl.BlockSpec(memory_space=pltpu.VMEM), pl.BlockSpec(memory_space=pl.ANY)
    dma = pltpu.SemaphoreType.DMA
    scratch = [
        pltpu.VMEM((LAYERS, width, 3 * wide), BF),
        pltpu.VMEM((LAYERS, wide, width), BF),
        pltpu.VMEM((LAYERS, width, local_ff), BF),
        pltpu.VMEM((LAYERS, width, local_ff), BF),
        pltpu.VMEM((LAYERS, prefix, wide), BF),
        pltpu.VMEM((LAYERS, prefix, wide), BF),
        pltpu.VMEM((tok, width), BF),
        pltpu.VMEM((SCATTERS, 2, own, width), BF),
        pltpu.VMEM((SCATTERS, own, width), BF),
        pltpu.VMEM((own, width), BF),
        pltpu.VMEM((GATHERS, tok, width), BF),
        pltpu.VMEM((LAYERS, tok, 3 * wide), BF),
        pltpu.VMEM((LAYERS, keys, prefix + window, heads * own), F32),
        pltpu.VMEM((LAYERS, tok, local_ff), F32),
        pltpu.VMEM((2 * LAYERS, own, width), F32),
        pltpu.VMEM((2 * LAYERS, own, 1), F32),
        pltpu.VMEM((own, width), F32),
        pltpu.VMEM((own, width), F32),
        pltpu.VMEM((own, width), F32),
        pltpu.VMEM((own, width), BF),
        pltpu.VMEM((tok, wide), BF),
        pltpu.VMEM((tok, 3 * wide), BF),
        pltpu.VMEM((prefix + tok, wide), F32),
        pltpu.VMEM((prefix + tok, wide), F32),
        pltpu.VMEM((tok, local_ff), BF),
        pltpu.VMEM((tok, wide), BF),
        pltpu.VMEM((keys, window, own), F32),
        pltpu.VMEM((LAYERS, 2, count, width), F32),
        pltpu.VMEM((LAYERS, bits, 2, count, width), F32),
        dma((pieces, 2, nz + 1)),
        dma((pieces, 2, nz)),
        dma((pieces, nz)),
        dma((pieces, 3)),
        dma((2, keys)),
        dma((2, keys)),
        dma((SCATTERS, 3)),
        dma((SCATTERS, 3)),
        dma((GATHERS, 3)),
        dma((GATHERS, 3)),
        dma((LAYERS, 2, keys)),
        dma((LAYERS, 2, keys)),
        dma((LAYERS, bits)),
        dma((LAYERS, bits)),
    ]
    act, grad, grad_keys, grad_values = pl.pallas_call(
        functools.partial(kernel, (rows, tok, width, local_ff)),
        out_shape=(
            jax.ShapeDtypeStruct((tok, width), BF),
            jax.ShapeDtypeStruct((tok, width), F32),
            jax.ShapeDtypeStruct((LAYERS, count, width), F32),
            jax.ShapeDtypeStruct((LAYERS, count, width), F32),
        ),
        in_specs=[vmem, anywhere, vmem, vmem] + [anywhere] * 8 + [vmem] * 4,
        out_specs=(anywhere, vmem, vmem, vmem),
        scratch_shapes=scratch,
        compiler_params=pltpu.CompilerParams(
            collective_id=0, has_side_effects=True, vmem_limit_bytes=62 * 1024 * 1024 - 512 * 1024
        ),
    )(
        tokens[0], cotangent[0], seg_row, key_code, prefix_keys, prefix_values,
        w_query, w_key, w_value, w_out, w_up, w_down_t,
        norm1_gain, norm1_bias, norm2_gain, norm2_bias,
    )
    return act[None], grad[None], grad_keys, grad_values


def solution(mesh):
    row3 = P("rows", None, None)
    weight = P(None, "rows", None)
    return jax.shard_map(
        per_device,
        mesh=mesh,
        in_specs=(
            row3,
            row3,
            P("rows", None),
            P("rows", None),
            P(None, "keys", None),
            P(None, "keys", None),
            weight,
            weight,
            weight,
            weight,
            P(None, "rows", "keys"),
            P(None, "rows", "keys"),
            P(),
            P(),
            P(),
            P(),
        ),
        out_specs=(row3, row3, P(None, "keys", None), P(None, "keys", None)),
        check_vma=False,
    )
```

```python
import functools

import jax
import jax.numpy as jnp
from jax import lax
from jax.experimental import pallas as pl
from jax.experimental.pallas import tpu as pltpu
from jax.sharding import PartitionSpec as P

HEAD = 64
LAYERS = 2
KEYS = 4
EPSILON = 1e-05
NEGATIVE = -1000000000.0
MESH = pl.DeviceIdType.MESH
BF = jnp.bfloat16
F32 = jnp.float32

AG_M0, AG_X1, AG_M1, AG_GF1, AG_GA1, AG_GF0, AG_GA0, AG_GX, AG_ACT = range(9)
GATHERS = 9
RS_A0, RS_F0, RS_A1, RS_F1, RS_GM1, RS_GX1, RS_GM0, RS_GX0 = range(8)
SCATTERS = 8
GATHER_BEFORE = (None, AG_M0, AG_X1, AG_M1, AG_GF1, AG_GA1, AG_GF0, AG_GA0)
SUBS = 4


def dot_nn(a, b):
    return lax.dot_general(a, b, (((1,), (0,)), ((), ())), preferred_element_type=F32)


def dot_nt(a, b):
    return lax.dot_general(a, b, (((1,), (1,)), ((), ())), preferred_element_type=F32)


def dot_tn(a, b):
    return lax.dot_general(a, b, (((0,), (0,)), ((), ())), preferred_element_type=F32)


def kernel(
    dims,
    tokens, cotangent, segments, padding, pre_k, pre_v,
    w_query, w_key, w_value, w_out, w_up, w_down,
    g1, b1, g2, b2,
    low_out, prefix_out,
    wqkv, wo, wu, wd, pk, pv,
    part, rc, ry, ys, full,
    qkv, prob, gelu_d, zhat, rinv,
    own_x, own_m, own_g, cot, att, gqkv, gk, gv, hid, go, bias, codes,
    pg, pg_low, pg_in,
    w_send, w_recv, w_over, loc, pre_send, pre_recv,
    rs_send, rs_recv, ag_send, ag_recv, pg_send, pg_recv, pgr_send, pgr_recv,
):
    rows, tok, width, local_ff = dims
    nz = rows // 2
    wide = width // KEYS
    heads = wide // HEAD
    own = tok // KEYS
    half = tok // 2
    depth = width // rows
    count = pre_k.shape[1]
    prefix = KEYS * count
    window = 3 * own

    r = lax.axis_index("rows")
    k = lax.axis_index("keys")
    z, x = r // 2, lax.rem(r, 2)
    y, c = k // 2, lax.rem(k, 2)
    sib = (r, k + 1 - 2 * c)
    across = (r, lax.rem(k + 2, KEYS))
    beside = (r + 1 - 2 * x, k)
    far, near = 1 - y, y

    def level(d):
        return lax.rem(z + d, nz)

    barrier = pltpu.get_barrier_semaphore()

    def greet(d, carry):
        pl.semaphore_signal(barrier, inc=1, device_id=(level(d) * 2 + x, k), device_id_type=MESH)
        return carry

    lax.fori_loop(1, nz, greet, 0)
    pl.semaphore_signal(barrier, inc=1, device_id=beside, device_id_type=MESH)
    for d in range(1, KEYS):
        pl.semaphore_signal(barrier, inc=1, device_id=(r, lax.rem(k + d, KEYS)), device_id_type=MESH)

    group = nz // KEYS
    first_row = k * (rows // KEYS)

    def spot(ref, layer, at):
        return ref.at[layer, pl.ds(pl.multiple_of(at * depth, depth), depth), :]

    def slot(p, zz, xx):
        layer, kind = divmod(p, 4)
        at = zz * 2 + xx
        if kind == 1:
            return spot(wo, layer, at - first_row)
        return spot((wqkv, None, wu, wd)[kind], layer, at)

    def active(p, zz):
        return None if p % 4 != 1 else (zz // group) == k

    def guarded(condition, action):
        if condition is None:
            action()
        else:
            pl.when(condition)(action)

    columns = pl.ds(pl.multiple_of(k * wide, wide), wide)

    def own_copies(p):
        layer, kind = divmod(p, 4)
        if kind == 0:
            place = pl.ds(pl.multiple_of(r * depth, depth), depth)
            return [
                pltpu.make_async_copy(
                    w.at[layer, :, columns], wqkv.at[layer, place, i * wide : (i + 1) * wide], loc.at[6 * layer + i]
                )
                for i, w in enumerate((w_query, w_key, w_value))
            ]
        source = (None, w_out, w_up, w_down)[kind]
        return [pltpu.make_async_copy(source.at[layer], slot(p, z, x), loc.at[6 * layer + 2 + kind])]

    def own_start(p):
        guarded(active(p, z), lambda: [copy.start() for copy in own_copies(p)] and None)

    def own_wait(p):
        guarded(active(p, z), lambda: [copy.wait() for copy in own_copies(p)] and None)

    def push(p, zz, xx, send_sem, target):
        place = slot(p, zz, xx)
        return pltpu.make_async_remote_copy(
            src_ref=place, dst_ref=place, send_sem=send_sem, recv_sem=w_recv.at[p, xx, zz],
            device_id=target, device_id_type=MESH,
        )

    def straight(p):
        return p == 4 * LAYERS - 1

    def up(p, zz, xx):
        return push(p, zz, xx, w_send.at[p, xx, zz], (lax.rem(z + 1, nz) * 2 + x, k))

    def down(p, zz, xx):
        sem = w_send.at[p, xx, jnp.where(zz == z, nz, zz)]
        return push(p, zz, xx, sem, (lax.rem(z + nz - 1, nz) * 2 + x, k))

    def over(p, zz):
        return push(p, zz, x, w_over.at[p, zz], beside)

    not_top, not_bottom = z < nz - 1, z > 0

    def spread_own(p, xx, action):
        pl.when(not_top)(lambda: action(up(p, z, xx)))
        pl.when(not_bottom)(lambda: action(down(p, z, xx)))

    def begin(copy):
        copy.start()

    def sent(copy):
        copy.wait_send()

    def issue(p):
        guarded(active(p, z), lambda: spread_own(p, x, begin))

    def beside_own(p):
        guarded(active(p, z), lambda: over(p, z).start())

    def swap(p):
        over_in = push(p, z, 1 - x, w_over.at[p, z], beside)
        over_in.wait_recv()
        spread_own(p, 1 - x, begin)

    def hops(group, action, sides=(True, False)):
        bounds = [1 + (nz - 1) * i // 3 for i in range(4)]

        def one(j, carry):
            if True in sides:
                pl.when(z - j >= 0)(lambda: action(jnp.maximum(z - j, 0), True))
            if False in sides:
                pl.when(z + j < nz)(lambda: action(jnp.minimum(z + j, nz - 1), False))
            return carry

        lax.fori_loop(bounds[group], bounds[group + 1], one, 0)

    def onward(p, zz, xx, below, action):
        if below:
            pl.when(not_top)(lambda: action(up(p, zz, xx)))
        else:
            pl.when(not_bottom)(lambda: action(down(p, zz, xx)))

    def passes(p, group, sides):
        def action(zz, below):
            def take():
                for xx in (x, 1 - x) if straight(p) else (x,):
                    push(p, zz, xx, w_over.at[p, zz], beside).wait_recv()
                    onward(p, zz, xx, below, begin)
                if not straight(p):
                    over(p, zz).start()

            guarded(active(p, zz), take)

        hops(group, action, sides)

    def arrive(p):
        if straight(p):
            return

        def one(zz, carry):
            guarded(active(p, zz), push(p, zz, 1 - x, w_over.at[p, zz], beside).wait_recv)
            return carry

        lax.fori_loop(0, nz, one, 0)

    def drain(p):
        def mine():
            spread_own(p, x, sent)
            if straight(p):
                spread_own(p, 1 - x, sent)
            over(p, z).wait_send()

        guarded(active(p, z), mine)

        def action(zz, below):
            def passed():
                for xx in (x, 1 - x) if straight(p) else (x,):
                    onward(p, zz, xx, below, sent)
                if not straight(p):
                    over(p, zz).wait_send()

            guarded(active(p, zz), passed)

        for group_at in range(3):
            hops(group_at, action)

    def pre_copy(i, d):
        kt = lax.rem(k + d, KEYS)
        source, target = ((pre_k, pk), (pre_v, pv))[i]
        return pltpu.make_async_remote_copy(
            src_ref=source.at[:, :, pl.ds(pl.multiple_of(kt * wide, wide), wide)],
            dst_ref=target.at[:, pl.ds(pl.multiple_of(k * count, count), count), :],
            send_sem=pre_send.at[i, d], recv_sem=pre_recv.at[i, d], device_id=(r, kt), device_id_type=MESH,
        )

    def pre_own(i):
        source, target = ((pre_k, pk), (pre_v, pv))[i]
        return pltpu.make_async_copy(
            source.at[:, :, columns],
            target.at[:, pl.ds(pl.multiple_of(k * count, count), count), :],
            pre_recv.at[i, 0],
        )

    own_block = pl.ds(pl.multiple_of(k * own, own), own)
    cot_copy = pltpu.make_async_copy(cotangent.at[own_block, :], cot, loc.at[12])

    for p in range(4 * LAYERS):
        own_start(p)
    cot_copy.start()
    for i in range(2):
        pre_own(i).start()

    visible_code = jnp.where(padding[...] == 1, segments[...], -1).astype(F32)
    codes[...] = jnp.broadcast_to(visible_code, (own, tok)).T

    def mask_of(i, carry):
        queries = segments[:, pl.ds(pl.multiple_of(i * own, own), own)].astype(F32)
        keys_code = codes[pl.ds(pl.multiple_of(jnp.clip(i - 1, 0, KEYS - 3) * own, own), window), :]
        bias[i] = jnp.where(keys_code == queries, 0.0, NEGATIVE)
        return carry

    lax.fori_loop(0, KEYS, mask_of, 0)

    def widen(i, carry):
        at = pl.multiple_of(i * 16, 16)
        own_x[pl.ds(at, 16), :] = tokens[pl.ds(k * own + at, 16), :].astype(F32)
        return carry

    lax.fori_loop(0, own // 16, widen, 0)
    pl.semaphore_wait(barrier, nz - 1 + 1 + KEYS - 1)
    own_wait(0)
    issue(0)
    beside_own(0)
    for i in range(2):
        for d in range(1, KEYS):
            pre_copy(i, d).start()
    for p in range(1, 4 * LAYERS):
        own_wait(p)
    cot_copy.wait()

    sub = own // SUBS
    block_a, block_b = 2 * far + c, 2 * far + 1 - c

    def rows_at(at, size):
        return pl.ds(pl.multiple_of(at, 16), size)

    def rs_copy(n, i):
        if i < SUBS:
            source, target = part.at[rows_at(block_b * own + i * sub, sub), :], rc.at[n, 0, i * sub : (i + 1) * sub, :]
        elif i == SUBS:
            source, target = part.at[rows_at((2 * near + 1 - c) * own, own), :], rc.at[n, 1]
        else:
            at = slice((i - SUBS - 1) * sub, (i - SUBS) * sub)
            source, target = ys.at[at, :], ry.at[n, at, :]
        return pltpu.make_async_remote_copy(
            src_ref=source, dst_ref=target, send_sem=rs_send.at[i], recv_sem=rs_recv.at[i],
            device_id=sib if i <= SUBS else across, device_id_type=MESH,
        )

    def chunks(total, body, size=16):
        def one(i, carry):
            body(pl.multiple_of(i * size, size))
            return carry

        lax.fori_loop(0, total // size, one, 0)

    def rs_mid(n, i):
        rs_copy(n, i).wait_recv()
        for at in range(i * sub, (i + 1) * sub, 16):
            mine = part[rows_at(block_a * own + at, 16), :].astype(F32)
            ys[at : at + 16, :] = (mine + rc[n, 0, at : at + 16, :].astype(F32)).astype(BF)
        rs_copy(n, SUBS + 1 + i).start()

    def rs_near(n):
        rs_copy(n, SUBS).start()

    def rs_sum(n, at):
        mine = part[rows_at(k * own + at, 16), :].astype(F32) + rc[n, 1, at : at + 16, :].astype(F32)
        return mine + ry[n, at : at + 16, :].astype(F32)

    def rs_each(n, body, target):
        if n > 0:
            ag_end(GATHER_BEFORE[n])
        rs_copy(n, SUBS).wait_recv()
        for i in range(SUBS):
            rs_copy(n, SUBS + 1 + i).wait_recv()
            for at in range(i * sub, (i + 1) * sub, 16):
                body(at)
            ag_copy(target, i).start()
        ag_copy(target, SUBS).start()
        rs_end(n)

    def rs_end(n):
        for i in range(2 * SUBS + 1):
            rs_copy(n, i).wait_send()

    def ag_copy(n, i):
        if i < SUBS:
            place, device = full.at[n, rows_at(k * own + i * sub, sub), :], across
        elif i == SUBS:
            place, device = full.at[n, rows_at(k * own, own), :], sib
        else:
            place, device = full.at[n, rows_at(block_a * own + (i - SUBS - 1) * sub, sub), :], sib
        return pltpu.make_async_remote_copy(
            src_ref=place, dst_ref=place, send_sem=ag_send.at[n // AG_ACT, i], recv_sem=ag_recv.at[n // AG_ACT, i],
            device_id=device, device_id_type=MESH,
        )

    def ag_end(n):
        for i in range(2 * SUBS + 1):
            ag_copy(n, i).wait_send()

    def ag_near(n):
        ag_copy(n, SUBS).wait_recv()

    def ag_pass(n, i):
        ag_copy(n, i).wait_recv()
        ag_copy(n, SUBS + 1 + i).start()

    def ag_got(n, i):
        ag_copy(n, SUBS + 1 + i).wait_recv()

    def ag_far(n):
        for i in range(SUBS):
            ag_pass(n, i)
        for i in range(SUBS):
            ag_got(n, i)

    def half_rows(which):
        return pl.ds(pl.multiple_of(which * half, half), half)

    def far_rows(i):
        return rows_at(block_a * own + i * sub, sub), rows_at(block_b * own + i * sub, sub)

    def both(ref, *lead, at):
        return jnp.concatenate([ref[(*lead, rows, slice(None))] for rows in at], axis=0)

    def project(layer, source, which):
        hr = half_rows(which)
        xin = source[hr, :]
        for i in range(3):
            at = slice(i * wide, (i + 1) * wide)
            val = dot_nn(xin, wqkv[layer, :, at])
            qkv[layer, hr, at] = (val * HEAD**-0.5 if i == 0 else val).astype(BF)

    lane_head = lax.broadcasted_iota(jnp.int32, (1, wide), 1) // HEAD
    masks = [jnp.where(lane_head == h, 1.0, 0.0).astype(BF) for h in range(heads)]

    def stacked(value):
        return jnp.concatenate([value * mask for mask in masks], axis=0)

    def place_of(i):
        return pl.multiple_of(i * own, own)

    def window_of(i):
        return pl.multiple_of(jnp.clip(i - 1, 0, KEYS - 3) * own, own)

    def unstacked(value):
        parts = [value[h * HEAD : (h + 1) * HEAD, h * own : (h + 1) * own] for h in range(heads)]
        return jnp.concatenate(parts, axis=0).T

    def attend(layer, i):
        q4 = stacked(qkv[layer, pl.ds(place_of(i), own), 0:wide])
        span = pl.ds(window_of(i), window)
        mask = bias[i]
        s_tok = dot_nt(qkv[layer, span, wide : 2 * wide], q4) + jnp.concatenate([mask] * heads, axis=1)
        s_pre = dot_nt(pk[layer], q4)
        top = jnp.maximum(jnp.max(s_tok, axis=0, keepdims=True), jnp.max(s_pre, axis=0, keepdims=True))
        e_tok, e_pre = jnp.exp(s_tok - top), jnp.exp(s_pre - top)
        inverse = 1.0 / (jnp.sum(e_tok, axis=0, keepdims=True) + jnp.sum(e_pre, axis=0, keepdims=True))
        p_tok, p_pre = e_tok * inverse, e_pre * inverse
        prob[layer, i, 0:prefix, :] = p_pre
        prob[layer, i, prefix : prefix + window, :] = p_tok
        out = dot_tn(qkv[layer, span, 2 * wide : 3 * wide], p_tok.astype(BF))
        out += dot_tn(pv[layer], p_pre.astype(BF))
        att[pl.ds(place_of(i), own), :] = unstacked(out).astype(BF)

    def attend_back(layer, i):
        at = pl.ds(place_of(i), own)
        q4 = stacked(qkv[layer, at, 0:wide])
        go4 = stacked(go[at, :])
        start = window_of(i)
        span = pl.ds(start, window)
        p_pre = prob[layer, i, 0:prefix, :]
        p_tok = prob[layer, i, prefix : prefix + window, :]
        gp_tok = dot_nt(qkv[layer, span, 2 * wide : 3 * wide], go4)
        gp_pre = dot_nt(pv[layer], go4)
        dsum = jnp.sum(p_tok * gp_tok, axis=0, keepdims=True) + jnp.sum(p_pre * gp_pre, axis=0, keepdims=True)
        gs_tok = (p_tok * (gp_tok - dsum)).astype(BF)
        gs_pre = (p_pre * (gp_pre - dsum)).astype(BF)
        places = pl.ds(prefix + start, window)
        gk[places, :] += dot_nn(gs_tok, q4)
        gk[0:prefix, :] += dot_nn(gs_pre, q4)
        gv[places, :] += dot_nn(p_tok.astype(BF), go4)
        gv[0:prefix, :] += dot_nn(p_pre.astype(BF), go4)
        gq = dot_tn(qkv[layer, span, wide : 2 * wide], gs_tok) + dot_tn(pk[layer], gs_pre)
        gqkv[at, 0:wide] = (unstacked(gq).astype(BF).astype(F32) * HEAD**-0.5).astype(BF)

    def two(body, which):
        def one(i, carry):
            body(2 * which + i)
            return carry

        lax.fori_loop(0, 2, one, 0)

    def out_rows(layer, at, size):
        rows_here = rows_at(at, size)
        part[rows_here, :] = dot_nn(att[rows_here, :], wo[layer]).astype(BF)

    def up_half(layer, n, which):
        hr = half_rows(which)
        u = dot_nn(full[n, hr, :], wu[layer])
        for at in range(0, half, 16):
            v = u[at : at + 16]
            phi_sum = 0.5 * (1.0 + lax.erf(v * 0.7071067811865476))
            density = jnp.exp(v * v * -0.5) * 0.3989422804014327
            here = rows_at(which * half + at, 16)
            hid[here, :] = (v * phi_sum).astype(BF)
            gelu_d[layer, here, :] = phi_sum + v * density

    def ff_back(layer, gradient, slope):
        gu = (dot_nn(gradient, wd[layer]) * slope).astype(BF)
        return dot_nt(gu, wu[layer]).astype(BF)

    def scatter_far(n, step):
        for i in range(SUBS):
            value = step(i)
            at_a, at_b = far_rows(i)
            part[at_b, :] = value[sub:]
            rs_copy(n, i).start()
            part[at_a, :] = value[:sub]
            if i > 0:
                rs_mid(n, i - 1)
        rs_mid(n, SUBS - 1)

    def project_back(layer, at, size):
        rows_here = rows_at(at, size)
        part[rows_here, :] = dot_nt(gqkv[rows_here, :], wqkv[layer]).astype(BF)

    def norm_into(n, residual, layer, which, gain, shift, result, target):
        index = 2 * layer + which
        g, b = gain[layer : layer + 1, :], shift[layer : layer + 1, :]

        def body(i):
            value = residual[i : i + 16, :] + rs_sum(n, i)
            centre = value - jnp.mean(value, axis=-1, keepdims=True)
            inv = lax.rsqrt(jnp.mean(centre * centre, axis=-1, keepdims=True) + EPSILON)
            hat = centre * inv
            done = hat * g + b
            zhat[index, i : i + 16, :] = hat
            rinv[index, i : i + 16, :] = inv
            result[i : i + 16, :] = done
            full[target, rows_at(k * own + i, 16), :] = done.astype(BF)

        return body

    def norm_back(read, layer, which, gain, target):
        index = 2 * layer + which
        g = gain[layer : layer + 1, :]

        def body(i):
            scaled = read(i) * g
            hat = zhat[index, i : i + 16, :]
            inv = rinv[index, i : i + 16, :]
            first = jnp.mean(scaled, axis=-1, keepdims=True)
            second = jnp.mean(scaled * hat, axis=-1, keepdims=True)
            result = inv * (scaled - first - hat * second)
            own_g[i : i + 16, :] = result
            full[target, rows_at(k * own + i, 16), :] = result.astype(BF)

        return body

    for i in range(2):
        pre_own(i).wait()
        for d in range(1, KEYS):
            pre_copy(i, d).wait_recv()

    def forward_layer(layer, first, second, third, fourth, fifth):
        base = 4 * layer
        rs_a, rs_f = ((RS_A0, RS_F0), (RS_A1, RS_F1))[layer]
        ag_m = (AG_M0, AG_M1)[layer]
        source = tokens if layer == 0 else full.at[AG_X1]
        first()
        arrive(base)
        if layer > 0:
            ag_near(AG_X1)
        project(layer, source, near)
        if layer > 0:
            ag_far(AG_X1)
        project(layer, source, far)
        second()
        attend(layer, block_b)
        arrive(base + 1)
        out_rows(layer, block_b * own, own)
        for i in range(SUBS):
            rs_copy(rs_a, i).start()
        attend(layer, block_a)
        out_rows(layer, block_a * own, own)
        for i in range(SUBS):
            rs_mid(rs_a, i)
        two(functools.partial(attend, layer), near)
        out_rows(layer, near * half, half)
        rs_near(rs_a)
        third()
        rs_each(rs_a, norm_into(rs_a, own_x, layer, 0, g1, b1, own_m, ag_m), ag_m)
        fourth()
        arrive(base + 2)
        ag_near(ag_m)
        up_half(layer, ag_m, near)
        ag_far(ag_m)
        up_half(layer, ag_m, far)
        fifth()
        arrive(base + 3)
        scatter_far(rs_f, lambda i: dot_nt(both(hid, at=far_rows(i)), wd[layer]).astype(BF))
        part[half_rows(near), :] = dot_nt(hid[half_rows(near), :], wd[layer]).astype(BF)
        rs_near(rs_f)

    def events(*calls):
        def run():
            for call in calls:
                if len(call) == 1:
                    issue(call[0])
                    beside_own(call[0])
                elif call[1] == 0:
                    swap(call[0])
                else:
                    passes(call[0], call[1] - 1, (True, False))

        return run

    events((1,), (2,))()
    forward_layer(
        0,
        events((0, 1), (0, 2), (0, 3), (1, 1), (3,)),
        events((1, 2), (1, 3), (2, 1)),
        events((2, 2), (2, 3), (3, 1), (4,)),
        events((3, 2), (3, 3), (4, 1), (5,)),
        events((4, 2), (4, 3), (5, 1), (6,)),
    )
    events((5, 2), (5, 3), (6, 1), (7,))()
    rs_each(RS_F0, norm_into(RS_F0, own_m, 0, 1, g2, b2, own_x, AG_X1), AG_X1)
    forward_layer(
        1,
        events((6, 2), (7, 0), (6, 3)),
        events(),
        events((7, 1)),
        events((7, 2)),
        events((7, 3)),
    )

    def prefix_copy(layer, i, d):
        kt = lax.rem(k + d, KEYS)
        source = (gk, gv)[i]
        return pltpu.make_async_remote_copy(
            src_ref=source.at[pl.ds(pl.multiple_of(kt * count, count), count), :],
            dst_ref=pg.at[layer, i, :, columns],
            send_sem=pg_send.at[i, d], recv_sem=pg_recv.at[i, d],
            device_id=(r, kt), device_id_type=MESH,
        )

    def prefix_own(layer, i):
        return pltpu.make_async_copy(
            (gk, gv)[i].at[pl.ds(pl.multiple_of(k * count, count), count), :],
            pg.at[layer, i, :, columns],
            pg_recv.at[i, 0],
        )

    bits = rows.bit_length() - 1

    def row_copy(layer, b):
        bit = 1 << b
        partner = r + bit - 2 * bit * lax.rem(r // bit, 2)
        return pltpu.make_async_remote_copy(
            src_ref=pg_low.at[layer], dst_ref=pg_in.at[layer, b],
            send_sem=pgr_send.at[layer, b], recv_sem=pgr_recv.at[layer, b],
            device_id=(partner, k), device_id_type=MESH,
        )

    def row_start(layer, b):
        low = pg[layer].astype(BF)
        pg_low[layer] = low
        pg[layer] = low.astype(F32)
        row_copy(layer, b).start()

    def row_step(layer, b):
        row_copy(layer, b).wait()
        pg[layer] += pg_in[layer, b].astype(F32)
        if b + 1 < bits:
            row_start(layer, b + 1)

    def prefix_start(layer):
        for i in range(2):
            prefix_own(layer, i).start()
            for d in range(1, KEYS):
                prefix_copy(layer, i, d).start()

    def prefix_take(layer):
        for i in range(2):
            prefix_own(layer, i).wait()
            for d in range(1, KEYS):
                prefix_copy(layer, i, d).wait_recv()
        row_start(layer, 0)

    def prefix_sent(layer):
        for i in range(2):
            for d in range(1, KEYS):
                prefix_copy(layer, i, d).wait_send()

    for layer in reversed(range(LAYERS)):
        rs_gm, rs_gx = ((RS_GM0, RS_GX0), (RS_GM1, RS_GX1))[layer]
        ag_gf, ag_ga = ((AG_GF0, AG_GA0), (AG_GF1, AG_GA1))[layer]
        if layer == LAYERS - 1:
            forth = norm_into(RS_F1, own_m, 1, 1, g2, b2, own_x, AG_ACT)
            back = norm_back(lambda i: cot[i : i + 16, :].astype(F32), layer, 1, g2, ag_gf)

            def turn(i):
                forth(i)
                back(i)

            rs_each(RS_F1, turn, ag_gf)
        else:
            rs_each(RS_GX1, norm_back(lambda i: own_g[i : i + 16, :] + rs_sum(RS_GX1, i), layer, 1, g2, ag_gf), ag_gf)
            prefix_take(layer + 1)
        ag_near(ag_gf)
        part[half_rows(near), :] = ff_back(layer, full[ag_gf, half_rows(near), :], gelu_d[layer, half_rows(near), :])
        rs_near(rs_gm)

        def step(i):
            ag_pass(ag_gf, i)
            ag_got(ag_gf, i)
            at = far_rows(i)
            return ff_back(layer, both(full, ag_gf, at=at), both(gelu_d, layer, at=at))

        scatter_far(rs_gm, step)
        if layer == 0:
            row_step(1, 0)
        gk[...] = jnp.zeros_like(gk)
        gv[...] = jnp.zeros_like(gv)
        rs_each(rs_gm, norm_back(lambda i: own_g[i : i + 16, :] + rs_sum(rs_gm, i), layer, 0, g1, ag_ga), ag_ga)
        if layer == LAYERS - 1:
            for i in range(SUBS + 1):
                ag_copy(AG_ACT, i).start()
        ag_near(ag_ga)
        go[half_rows(near), :] = dot_nt(full[ag_ga, half_rows(near), :], wo[layer]).astype(BF)
        two(functools.partial(attend_back, layer), near)
        if layer == 0:
            row_step(1, 1)
        ag_far(ag_ga)
        go[half_rows(far), :] = dot_nt(full[ag_ga, half_rows(far), :], wo[layer]).astype(BF)
        two(functools.partial(attend_back, layer), far)
        prefix_start(layer)

        def narrow(which):
            def body(i):
                i = which * half + i
                gqkv[rows_at(i, 16), wide : 2 * wide] = gk[rows_at(prefix + i, 16), :].astype(BF)
                gqkv[rows_at(i, 16), 2 * wide : 3 * wide] = gv[rows_at(prefix + i, 16), :].astype(BF)

            chunks(half, body)

        narrow(far)
        project_back(layer, block_b * own, own)
        for i in range(SUBS):
            rs_copy(rs_gx, i).start()
        project_back(layer, block_a * own, own)
        for i in range(SUBS):
            rs_mid(rs_gx, i)
        narrow(near)
        project_back(layer, near * half, half)
        rs_near(rs_gx)
        if layer == LAYERS - 1:
            ag_far(AG_ACT)
            ag_near(AG_ACT)
        else:
            for b in range(2, bits):
                row_step(1, b)
            prefix_take(0)
        prefix_sent(layer)

    act_copy = pltpu.make_async_copy(full.at[AG_ACT], low_out.at[1], loc.at[13])
    act_copy.start()

    def last(i):
        full[AG_GX, rows_at(k * own + i, 16), :] = (own_g[i : i + 16, :] + rs_sum(RS_GX0, i)).astype(BF)

    rs_each(RS_GX0, last, AG_GX)
    for p in range(4 * LAYERS):
        drain(p)
    for i in range(2):
        for d in range(1, KEYS):
            pre_copy(i, d).wait_send()
    row_step(0, 0)
    ag_near(AG_GX)

    def grad_copy(which):
        return pltpu.make_async_copy(
            full.at[AG_GX, half_rows(which), :], low_out.at[0, half_rows(which), :], loc.at[14 + (which is far)]
        )

    grad_copy(near).start()
    ag_far(AG_GX)
    grad_copy(far).start()
    for b in range(1, bits):
        row_step(0, b)
    for i in range(2):
        for layer in range(LAYERS):
            prefix_out[i, layer] = pg[layer, i]
    ag_end(AG_GX)
    ag_end(AG_ACT)
    act_copy.wait()
    grad_copy(near).wait()
    grad_copy(far).wait()


def results(low, grads, act, gt, gpk, gpv, narrow, broad, act_held, grads_held, sems):
    parts, size = narrow.shape[:2]

    def taken(i):
        return pltpu.make_async_copy(low.at[0, i * size : (i + 1) * size, :], narrow.at[i], sems.at[0, i])

    def given(i):
        return pltpu.make_async_copy(broad.at[i], gt.at[0, i * size : (i + 1) * size, :], sems.at[1, i])

    in_act = pltpu.make_async_copy(low.at[1], act_held, sems.at[2, 0])
    out_act = pltpu.make_async_copy(act_held, act.at[0], sems.at[2, 0])
    in_grads = pltpu.make_async_copy(grads, grads_held, sems.at[2, 1])
    out_grads = [pltpu.make_async_copy(grads_held.at[i], (gpk, gpv)[i], sems.at[2, 2 + i]) for i in range(2)]
    for i in range(parts):
        taken(i).start()
    in_act.start()
    in_grads.start()
    for i in range(parts):
        taken(i).wait()
        broad[i] = narrow[i].astype(F32)
        given(i).start()
    in_act.wait()
    out_act.start()
    in_grads.wait()
    for copy in out_grads:
        copy.start()
    for i in range(parts):
        given(i).wait()
    out_act.wait()
    for copy in out_grads:
        copy.wait()


def per_device(
    tokens, cotangent, segment_ids, pad_mask, prefix_keys, prefix_values,
    w_query, w_key, w_value, w_out, w_up, w_down_t,
    norm1_gain, norm1_bias, norm2_gain, norm2_bias,
):
    rows, keys = lax.axis_size("rows"), lax.axis_size("keys")
    assert keys == KEYS and rows % (2 * KEYS) == 0 and rows & (rows - 1) == 0
    tok, width = tokens.shape[1:]
    count = prefix_keys.shape[1]
    prefix = count * keys
    local_ff = w_up.shape[2]
    wide, own, window = width // keys, tok // keys, 3 * tok // keys
    heads = wide // HEAD
    nz, bits, pieces = rows // 2, rows.bit_length() - 1, 4 * LAYERS
    vmem, anywhere = pl.BlockSpec(memory_space=pltpu.VMEM), pl.BlockSpec(memory_space=pl.ANY)
    dma = pltpu.SemaphoreType.DMA
    scratch = [
        pltpu.VMEM((LAYERS, width, 3 * wide), BF),
        pltpu.VMEM((LAYERS, wide, width), BF),
        pltpu.VMEM((LAYERS, width, local_ff), BF),
        pltpu.VMEM((LAYERS, width, local_ff), BF),
        pltpu.VMEM((LAYERS, prefix, wide), BF),
        pltpu.VMEM((LAYERS, prefix, wide), BF),
        pltpu.VMEM((tok, width), BF),
        pltpu.VMEM((SCATTERS, 2, own, width), BF),
        pltpu.VMEM((SCATTERS, own, width), BF),
        pltpu.VMEM((own, width), BF),
        pltpu.VMEM((GATHERS, tok, width), BF),
        pltpu.VMEM((LAYERS, tok, 3 * wide), BF),
        pltpu.VMEM((LAYERS, keys, prefix + window, heads * own), F32),
        pltpu.VMEM((LAYERS, tok, local_ff), F32),
        pltpu.VMEM((2 * LAYERS, own, width), F32),
        pltpu.VMEM((2 * LAYERS, own, 1), F32),
        pltpu.VMEM((own, width), F32),
        pltpu.VMEM((own, width), F32),
        pltpu.VMEM((own, width), F32),
        pltpu.VMEM((own, width), BF),
        pltpu.VMEM((tok, wide), BF),
        pltpu.VMEM((tok, 3 * wide), BF),
        pltpu.VMEM((prefix + tok, wide), F32),
        pltpu.VMEM((prefix + tok, wide), F32),
        pltpu.VMEM((tok, local_ff), BF),
        pltpu.VMEM((tok, wide), BF),
        pltpu.VMEM((keys, window, own), F32),
        pltpu.VMEM((tok, own), F32),
        pltpu.VMEM((LAYERS, 2, count, width), F32),
        pltpu.VMEM((LAYERS, 2, count, width), BF),
        pltpu.VMEM((LAYERS, bits, 2, count, width), BF),
        dma((pieces, 2, nz + 1)),
        dma((pieces, 2, nz)),
        dma((pieces, nz)),
        dma((16,)),
        dma((2, keys)),
        dma((2, keys)),
        dma((2 * SUBS + 1,)),
        dma((2 * SUBS + 1,)),
        dma((2, 2 * SUBS + 1)),
        dma((2, 2 * SUBS + 1)),
        dma((2, keys)),
        dma((2, keys)),
        dma((LAYERS, bits)),
        dma((LAYERS, bits)),
    ]
    low, grads = pl.pallas_call(
        functools.partial(kernel, (rows, tok, width, local_ff)),
        out_shape=(
            jax.ShapeDtypeStruct((2, tok, width), BF),
            jax.ShapeDtypeStruct((2, LAYERS, count, width), F32),
        ),
        in_specs=[vmem, anywhere, vmem, vmem] + [anywhere] * 8 + [vmem] * 4,
        out_specs=(anywhere, vmem),
        scratch_shapes=scratch,
        compiler_params=pltpu.CompilerParams(
            collective_id=0, has_side_effects=True, vmem_limit_bytes=62 * 1024 * 1024 - 512 * 1024
        ),
    )(
        tokens[0], cotangent[0], segment_ids, pad_mask, prefix_keys, prefix_values,
        w_query, w_key, w_value, w_out, w_up, w_down_t,
        norm1_gain, norm1_bias, norm2_gain, norm2_bias,
    )
    whole = (LAYERS, count, width)
    return pl.pallas_call(
        results,
        out_shape=(
            jax.ShapeDtypeStruct((1, tok, width), BF),
            jax.ShapeDtypeStruct((1, tok, width), F32),
            jax.ShapeDtypeStruct(whole, F32),
            jax.ShapeDtypeStruct(whole, F32),
        ),
        in_specs=[anywhere] * 2,
        out_specs=(anywhere,) * 4,
        scratch_shapes=[
            pltpu.VMEM((keys, own, width), BF),
            pltpu.VMEM((keys, own, width), F32),
            pltpu.VMEM((tok, width), BF),
            pltpu.VMEM((2, *whole), F32),
            dma((3, keys)),
        ],
    )(low, grads)


def solution(mesh):
    row3 = P("rows", None, None)
    weight = P(None, "rows", None)
    return jax.shard_map(
        per_device,
        mesh=mesh,
        in_specs=(
            row3,
            row3,
            P("rows", None),
            P("rows", None),
            P(None, "keys", None),
            P(None, "keys", None),
            weight,
            weight,
            weight,
            weight,
            P(None, "rows", "keys"),
            P(None, "rows", "keys"),
            P(),
            P(),
            P(),
            P(),
        ),
        out_specs=(row3, row3, P(None, "keys", None), P(None, "keys", None)),
        check_vma=False,
    )
```

```python
import functools

import jax
import jax.numpy as jnp
from jax import lax
from jax.experimental import pallas as pl
from jax.experimental.pallas import tpu as pltpu
from jax.sharding import PartitionSpec as P

HEAD = 64
LAYERS = 2
KEYS = 4
EPSILON = 1e-05
NEGATIVE = -1000000000.0
MESH = pl.DeviceIdType.MESH
BF = jnp.bfloat16
F32 = jnp.float32

AG_M0, AG_X1, AG_M1, AG_GF1, AG_GA1, AG_GF0, AG_GA0, AG_GX, AG_ACT = range(9)
GATHERS = 9
RS_A0, RS_F0, RS_A1, RS_F1, RS_GM1, RS_GX1, RS_GM0, RS_GX0 = range(8)
SCATTERS = 8
GATHER_BEFORE = (None, AG_M0, AG_X1, AG_M1, AG_GF1, AG_GA1, AG_GF0, AG_GA0)
SUBS = 4

SCHEDULE = {
    (0, "start"): (
        ("beside", 1, 0),
        ("beside", 7, 0),
        ("along", 1, 0),
        ("beside", 2, 0),
        ("along", 0, 0),
        ("down", 1, 1),
        ("along", 4, 0),
        ("up", 1, 1),
        ("down", 0, 1),
        ("up", 0, 1),
        ("up", 1, 2),
        ("down", 1, 2),
        ("along", 2, 0),
        ("up", 0, 2),
        ("up", 1, 3),
        ("beside", 0, 0),
        ("down", 0, 2),
        ("up", 2, 1),
        ("down", 1, 3),
        ("down", 2, 1),
        ("up", 0, 3),
        ("along", 5, 0),
        ("up", 2, 2),
        ("down", 0, 3),
        ("along", 3, 0),
        ("down", 2, 2),
        ("up", 2, 3),
        ("down", 3, 1),
        ("down", 5, 1),
        ("up", 3, 1),
        ("up", 3, 2),
    ),
    (0, "attended b"): (
        ("up", 5, 2),
    ),
    (0, "out b"): (
        ("beside", 5, 0),
        ("up", 5, 1),
        ("along", 6, 0),
    ),
    (0, "out a"): (
        ("beside", 3, 0),
        ("down", 3, 2),
        ("down", 5, 2),
        ("down", 2, 3),
    ),
    (0, "norm 3"): (
        ("up", 4, 1),
        ("up", 3, 3),
        ("up", 4, 2),
        ("down", 4, 1),
    ),
    (0, "normed"): (
        ("up", 4, 3),
        ("swap", 7, 0),
    ),
    (0, "up"): (
        ("down", 3, 3),
        ("down", 4, 2),
    ),
    (0, "up far"): (
        ("along", 7, 0),
    ),
    (0, "down 0"): (
        ("beside", 4, 0),
    ),
    (0, "down 1"): (
        ("up", 6, 1),
    ),
    (0, "down 2"): (
        ("down", 5, 3),
        ("up", 5, 3),
    ),
    (0, "last norm 1"): (
        ("down", 4, 3),
        ("down", 6, 1),
    ),
    (0, "last norm 2"): (
        ("up", 6, 2),
        ("down", 6, 2),
    ),
    (1, "start"): (
        ("beside", 6, 0),
        ("down", 7, 1),
    ),
    (1, "projected near"): (
        ("up", 7, 1),
    ),
    (1, "out b"): (
        ("up", 6, 3),
    ),
    (1, "out a"): (
        ("down", 6, 3),
    ),
    (1, "norm 1"): (
        ("down", 7, 2),
    ),
    (1, "norm 2"): (
        ("up", 7, 2),
    ),
    (1, "up far"): (
        ("up", 7, 3),
        ("down", 7, 3),
    ),
}
STRAIGHT = (7,)


def dot_nn(a, b):
    return lax.dot_general(a, b, (((1,), (0,)), ((), ())), preferred_element_type=F32)


def dot_nt(a, b):
    return lax.dot_general(a, b, (((1,), (1,)), ((), ())), preferred_element_type=F32)


def dot_tn(a, b):
    return lax.dot_general(a, b, (((0,), (0,)), ((), ())), preferred_element_type=F32)


def kernel(
    dims,
    tokens, cotangent, segments, padding, pre_k, pre_v,
    w_query, w_key, w_value, w_out, w_up, w_down,
    g1, b1, g2, b2,
    low_out, prefix_out,
    wqkv, wo, wu, wd, pk, pv,
    part, rc, ry, ys, full,
    qkv, prob, gelu_d, zhat, rinv,
    own_x, own_m, own_g, cot, att, gqkv, gk, gv, hid, go, bias, codes,
    pg, pg_low, pg_in,
    w_send, w_recv, w_over, loc, pre_send, pre_recv,
    rs_send, rs_recv, ag_send, ag_recv, pg_send, pg_recv, pgr_send, pgr_recv,
):
    rows, tok, width, local_ff = dims
    nz = rows // 2
    wide = width // KEYS
    heads = wide // HEAD
    own = tok // KEYS
    half = tok // 2
    depth = width // rows
    count = pre_k.shape[1]
    prefix = KEYS * count
    window = 3 * own

    r = lax.axis_index("rows")
    k = lax.axis_index("keys")
    z, x = r // 2, lax.rem(r, 2)
    y, c = k // 2, lax.rem(k, 2)
    sib = (r, k + 1 - 2 * c)
    across = (r, lax.rem(k + 2, KEYS))
    beside = (r + 1 - 2 * x, k)
    far, near = 1 - y, y

    def level(d):
        return lax.rem(z + d, nz)

    barrier = pltpu.get_barrier_semaphore()

    def greet(d, carry):
        pl.semaphore_signal(barrier, inc=1, device_id=(level(d) * 2 + x, k), device_id_type=MESH)
        return carry

    lax.fori_loop(1, nz, greet, 0)
    pl.semaphore_signal(barrier, inc=1, device_id=beside, device_id_type=MESH)
    for d in range(1, KEYS):
        pl.semaphore_signal(barrier, inc=1, device_id=(r, lax.rem(k + d, KEYS)), device_id_type=MESH)

    group = nz // KEYS
    first_row = k * (rows // KEYS)

    def spot(ref, layer, at):
        return ref.at[layer, pl.ds(pl.multiple_of(at * depth, depth), depth), :]

    def slot(p, zz, xx):
        layer, kind = divmod(p, 4)
        at = zz * 2 + xx
        if kind == 1:
            return spot(wo, layer, at - first_row)
        return spot((wqkv, None, wu, wd)[kind], layer, at)

    def active(p, zz):
        return None if p % 4 != 1 else (zz // group) == k

    def guarded(condition, action):
        if condition is None:
            action()
        else:
            pl.when(condition)(action)

    columns = pl.ds(pl.multiple_of(k * wide, wide), wide)

    def own_copies(p):
        layer, kind = divmod(p, 4)
        if kind == 0:
            place = pl.ds(pl.multiple_of(r * depth, depth), depth)
            return [
                pltpu.make_async_copy(
                    w.at[layer, :, columns], wqkv.at[layer, place, i * wide : (i + 1) * wide], loc.at[6 * layer + i]
                )
                for i, w in enumerate((w_query, w_key, w_value))
            ]
        source = (None, w_out, w_up, w_down)[kind]
        return [pltpu.make_async_copy(source.at[layer], slot(p, z, x), loc.at[6 * layer + 2 + kind])]

    def own_start(p):
        guarded(active(p, z), lambda: [copy.start() for copy in own_copies(p)] and None)

    def own_wait(p):
        guarded(active(p, z), lambda: [copy.wait() for copy in own_copies(p)] and None)

    def push(p, zz, xx, send_sem, target):
        place = slot(p, zz, xx)
        return pltpu.make_async_remote_copy(
            src_ref=place, dst_ref=place, send_sem=send_sem, recv_sem=w_recv.at[p, xx, zz],
            device_id=target, device_id_type=MESH,
        )

    def straight(p):
        return p in STRAIGHT

    def up(p, zz, xx):
        return push(p, zz, xx, w_send.at[p, xx, zz], (lax.rem(z + 1, nz) * 2 + x, k))

    def down(p, zz, xx):
        sem = w_send.at[p, xx, jnp.where(zz == z, nz, zz)]
        return push(p, zz, xx, sem, (lax.rem(z + nz - 1, nz) * 2 + x, k))

    def over(p, zz):
        return push(p, zz, x, w_over.at[p, zz], beside)

    not_top, not_bottom = z < nz - 1, z > 0

    def spread_own(p, xx, action):
        pl.when(not_top)(lambda: action(up(p, z, xx)))
        pl.when(not_bottom)(lambda: action(down(p, z, xx)))

    def begin(copy):
        copy.start()

    def sent(copy):
        copy.wait_send()

    def issue(p):
        guarded(active(p, z), lambda: spread_own(p, x, begin))

    def beside_own(p):
        guarded(active(p, z), lambda: over(p, z).start())

    def swap(p):
        over_in = push(p, z, 1 - x, w_over.at[p, z], beside)
        over_in.wait_recv()
        spread_own(p, 1 - x, begin)

    def hops(group, action, sides=(True, False)):
        bounds = [1 + (nz - 1) * i // 3 for i in range(4)]

        def one(j, carry):
            if True in sides:
                pl.when(z - j >= 0)(lambda: action(jnp.maximum(z - j, 0), True))
            if False in sides:
                pl.when(z + j < nz)(lambda: action(jnp.minimum(z + j, nz - 1), False))
            return carry

        lax.fori_loop(bounds[group], bounds[group + 1], one, 0)

    def onward(p, zz, xx, below, action):
        if below:
            pl.when(not_top)(lambda: action(up(p, zz, xx)))
        else:
            pl.when(not_bottom)(lambda: action(down(p, zz, xx)))

    def passes(p, group, sides):
        def action(zz, below):
            def take():
                for xx in (x, 1 - x) if straight(p) else (x,):
                    push(p, zz, xx, w_over.at[p, zz], beside).wait_recv()
                    onward(p, zz, xx, below, begin)
                if not straight(p):
                    over(p, zz).start()

            guarded(active(p, zz), take)

        hops(group, action, sides)

    def arrive(p):
        if straight(p):
            return

        def one(zz, carry):
            guarded(active(p, zz), push(p, zz, 1 - x, w_over.at[p, zz], beside).wait_recv)
            return carry

        lax.fori_loop(0, nz, one, 0)

    def drain(p):
        def mine():
            spread_own(p, x, sent)
            if straight(p):
                spread_own(p, 1 - x, sent)
            over(p, z).wait_send()

        guarded(active(p, z), mine)

        def action(zz, below):
            def passed():
                for xx in (x, 1 - x) if straight(p) else (x,):
                    onward(p, zz, xx, below, sent)
                if not straight(p):
                    over(p, zz).wait_send()

            guarded(active(p, zz), passed)

        for group_at in range(3):
            hops(group_at, action)

    def pre_copy(i, d):
        kt = lax.rem(k + d, KEYS)
        source, target = ((pre_k, pk), (pre_v, pv))[i]
        return pltpu.make_async_remote_copy(
            src_ref=source.at[:, :, pl.ds(pl.multiple_of(kt * wide, wide), wide)],
            dst_ref=target.at[:, pl.ds(pl.multiple_of(k * count, count), count), :],
            send_sem=pre_send.at[i, d], recv_sem=pre_recv.at[i, d], device_id=(r, kt), device_id_type=MESH,
        )

    def pre_own(i):
        source, target = ((pre_k, pk), (pre_v, pv))[i]
        return pltpu.make_async_copy(
            source.at[:, :, columns],
            target.at[:, pl.ds(pl.multiple_of(k * count, count), count), :],
            pre_recv.at[i, 0],
        )

    own_block = pl.ds(pl.multiple_of(k * own, own), own)
    cot_copy = pltpu.make_async_copy(cotangent.at[own_block, :], cot, loc.at[12])

    for p in range(4 * LAYERS):
        own_start(p)
    cot_copy.start()
    for i in range(2):
        pre_own(i).start()

    visible_code = jnp.where(padding[...] == 1, segments[...], -1).astype(F32)
    codes[...] = jnp.broadcast_to(visible_code, (own, tok)).T

    def mask_of(i, carry):
        queries = segments[:, pl.ds(pl.multiple_of(i * own, own), own)].astype(F32)
        keys_code = codes[pl.ds(pl.multiple_of(jnp.clip(i - 1, 0, KEYS - 3) * own, own), window), :]
        bias[i] = jnp.where(keys_code == queries, 0.0, NEGATIVE)
        return carry

    lax.fori_loop(0, KEYS, mask_of, 0)

    def widen(i, carry):
        at = pl.multiple_of(i * 16, 16)
        own_x[pl.ds(at, 16), :] = tokens[pl.ds(k * own + at, 16), :].astype(F32)
        return carry

    lax.fori_loop(0, own // 16, widen, 0)
    pl.semaphore_wait(barrier, nz - 1 + 1 + KEYS - 1)
    own_wait(0)
    for i in range(2):
        for d in range(1, KEYS):
            pre_copy(i, d).start()
    for p in range(1, 4 * LAYERS):
        own_wait(p)
    cot_copy.wait()

    sub = own // SUBS
    block_a, block_b = 2 * far + c, 2 * far + 1 - c

    def rows_at(at, size):
        return pl.ds(pl.multiple_of(at, 16), size)

    def rs_copy(n, i):
        if i < SUBS:
            source, target = part.at[rows_at(block_b * own + i * sub, sub), :], rc.at[n, 0, i * sub : (i + 1) * sub, :]
        elif i == SUBS:
            source, target = part.at[rows_at((2 * near + 1 - c) * own, own), :], rc.at[n, 1]
        else:
            at = slice((i - SUBS - 1) * sub, (i - SUBS) * sub)
            source, target = ys.at[at, :], ry.at[n, at, :]
        return pltpu.make_async_remote_copy(
            src_ref=source, dst_ref=target, send_sem=rs_send.at[i], recv_sem=rs_recv.at[i],
            device_id=sib if i <= SUBS else across, device_id_type=MESH,
        )

    def chunks(total, body, size=16):
        def one(i, carry):
            body(pl.multiple_of(i * size, size))
            return carry

        lax.fori_loop(0, total // size, one, 0)

    def rs_mid(n, i):
        rs_copy(n, i).wait_recv()
        for at in range(i * sub, (i + 1) * sub, 16):
            mine = part[rows_at(block_a * own + at, 16), :].astype(F32)
            ys[at : at + 16, :] = (mine + rc[n, 0, at : at + 16, :].astype(F32)).astype(BF)
        rs_copy(n, SUBS + 1 + i).start()

    def rs_near(n):
        rs_copy(n, SUBS).start()

    def rs_sum(n, at):
        mine = part[rows_at(k * own + at, 16), :].astype(F32) + rc[n, 1, at : at + 16, :].astype(F32)
        return mine + ry[n, at : at + 16, :].astype(F32)

    def rs_each(n, body, target, between=lambda i: None):
        if n > 0:
            ag_end(GATHER_BEFORE[n])
        rs_copy(n, SUBS).wait_recv()
        for i in range(SUBS):
            between(i)
            rs_copy(n, SUBS + 1 + i).wait_recv()
            for at in range(i * sub, (i + 1) * sub, 16):
                body(at)
            ag_copy(target, i).start()
        ag_copy(target, SUBS).start()
        rs_end(n)

    def rs_end(n):
        for i in range(2 * SUBS + 1):
            rs_copy(n, i).wait_send()

    def ag_copy(n, i):
        if i < SUBS:
            place, device = full.at[n, rows_at(k * own + i * sub, sub), :], across
        elif i == SUBS:
            place, device = full.at[n, rows_at(k * own, own), :], sib
        else:
            place, device = full.at[n, rows_at(block_a * own + (i - SUBS - 1) * sub, sub), :], sib
        return pltpu.make_async_remote_copy(
            src_ref=place, dst_ref=place, send_sem=ag_send.at[n // AG_ACT, i], recv_sem=ag_recv.at[n // AG_ACT, i],
            device_id=device, device_id_type=MESH,
        )

    def ag_end(n):
        for i in range(2 * SUBS + 1):
            ag_copy(n, i).wait_send()

    def ag_near(n):
        ag_copy(n, SUBS).wait_recv()

    def ag_pass(n, i):
        ag_copy(n, i).wait_recv()
        ag_copy(n, SUBS + 1 + i).start()

    def ag_got(n, i):
        ag_copy(n, SUBS + 1 + i).wait_recv()

    def ag_far(n):
        for i in range(SUBS):
            ag_pass(n, i)
        for i in range(SUBS):
            ag_got(n, i)

    def half_rows(which):
        return pl.ds(pl.multiple_of(which * half, half), half)

    def far_rows(i):
        return rows_at(block_a * own + i * sub, sub), rows_at(block_b * own + i * sub, sub)

    def both(ref, *lead, at):
        return jnp.concatenate([ref[(*lead, rows, slice(None))] for rows in at], axis=0)

    def project(layer, source, which):
        hr = half_rows(which)
        xin = source[hr, :]
        for i in range(3):
            at = slice(i * wide, (i + 1) * wide)
            val = dot_nn(xin, wqkv[layer, :, at])
            qkv[layer, hr, at] = (val * HEAD**-0.5 if i == 0 else val).astype(BF)

    lane_head = lax.broadcasted_iota(jnp.int32, (1, wide), 1) // HEAD
    masks = [jnp.where(lane_head == h, 1.0, 0.0).astype(BF) for h in range(heads)]

    def stacked(value):
        return jnp.concatenate([value * mask for mask in masks], axis=0)

    def place_of(i):
        return pl.multiple_of(i * own, own)

    def window_of(i):
        return pl.multiple_of(jnp.clip(i - 1, 0, KEYS - 3) * own, own)

    def unstacked(value):
        parts = [value[h * HEAD : (h + 1) * HEAD, h * own : (h + 1) * own] for h in range(heads)]
        return jnp.concatenate(parts, axis=0).T

    def attend(layer, i):
        q4 = stacked(qkv[layer, pl.ds(place_of(i), own), 0:wide])
        span = pl.ds(window_of(i), window)
        mask = bias[i]
        s_tok = dot_nt(qkv[layer, span, wide : 2 * wide], q4) + jnp.concatenate([mask] * heads, axis=1)
        s_pre = dot_nt(pk[layer], q4)
        top = jnp.maximum(jnp.max(s_tok, axis=0, keepdims=True), jnp.max(s_pre, axis=0, keepdims=True))
        e_tok, e_pre = jnp.exp(s_tok - top), jnp.exp(s_pre - top)
        inverse = 1.0 / (jnp.sum(e_tok, axis=0, keepdims=True) + jnp.sum(e_pre, axis=0, keepdims=True))
        p_tok, p_pre = e_tok * inverse, e_pre * inverse
        prob[layer, i, 0:prefix, :] = p_pre
        prob[layer, i, prefix : prefix + window, :] = p_tok
        out = dot_tn(qkv[layer, span, 2 * wide : 3 * wide], p_tok.astype(BF))
        out += dot_tn(pv[layer], p_pre.astype(BF))
        att[pl.ds(place_of(i), own), :] = unstacked(out).astype(BF)

    def attend_back(layer, i):
        at = pl.ds(place_of(i), own)
        q4 = stacked(qkv[layer, at, 0:wide])
        go4 = stacked(go[at, :])
        start = window_of(i)
        span = pl.ds(start, window)
        p_pre = prob[layer, i, 0:prefix, :]
        p_tok = prob[layer, i, prefix : prefix + window, :]
        gp_tok = dot_nt(qkv[layer, span, 2 * wide : 3 * wide], go4)
        gp_pre = dot_nt(pv[layer], go4)
        dsum = jnp.sum(p_tok * gp_tok, axis=0, keepdims=True) + jnp.sum(p_pre * gp_pre, axis=0, keepdims=True)
        gs_tok = (p_tok * (gp_tok - dsum)).astype(BF)
        gs_pre = (p_pre * (gp_pre - dsum)).astype(BF)
        places = pl.ds(prefix + start, window)
        gk[places, :] += dot_nn(gs_tok, q4)
        gk[0:prefix, :] += dot_nn(gs_pre, q4)
        gv[places, :] += dot_nn(p_tok.astype(BF), go4)
        gv[0:prefix, :] += dot_nn(p_pre.astype(BF), go4)
        gq = dot_tn(qkv[layer, span, wide : 2 * wide], gs_tok) + dot_tn(pk[layer], gs_pre)
        gqkv[at, 0:wide] = (unstacked(gq).astype(BF).astype(F32) * HEAD**-0.5).astype(BF)

    def two(body, which):
        def one(i, carry):
            body(2 * which + i)
            return carry

        lax.fori_loop(0, 2, one, 0)

    def out_rows(layer, at, size):
        rows_here = rows_at(at, size)
        part[rows_here, :] = dot_nn(att[rows_here, :], wo[layer]).astype(BF)

    def up_half(layer, n, which):
        hr = half_rows(which)
        u = dot_nn(full[n, hr, :], wu[layer])
        for at in range(0, half, 16):
            v = u[at : at + 16]
            phi_sum = 0.5 * (1.0 + lax.erf(v * 0.7071067811865476))
            density = jnp.exp(v * v * -0.5) * 0.3989422804014327
            here = rows_at(which * half + at, 16)
            hid[here, :] = (v * phi_sum).astype(BF)
            gelu_d[layer, here, :] = phi_sum + v * density

    def ff_back(layer, gradient, slope):
        gu = (dot_nn(gradient, wd[layer]) * slope).astype(BF)
        return dot_nt(gu, wu[layer]).astype(BF)

    def scatter_far(n, step, between=lambda i: None):
        for i in range(SUBS):
            between(i)
            value = step(i)
            at_a, at_b = far_rows(i)
            part[at_b, :] = value[sub:]
            rs_copy(n, i).start()
            part[at_a, :] = value[:sub]
            if i > 0:
                rs_mid(n, i - 1)
        rs_mid(n, SUBS - 1)

    def project_back(layer, at, size):
        rows_here = rows_at(at, size)
        part[rows_here, :] = dot_nt(gqkv[rows_here, :], wqkv[layer]).astype(BF)

    def norm_into(n, residual, layer, which, gain, shift, result, target):
        index = 2 * layer + which
        g, b = gain[layer : layer + 1, :], shift[layer : layer + 1, :]

        def body(i):
            value = residual[i : i + 16, :] + rs_sum(n, i)
            centre = value - jnp.mean(value, axis=-1, keepdims=True)
            inv = lax.rsqrt(jnp.mean(centre * centre, axis=-1, keepdims=True) + EPSILON)
            hat = centre * inv
            done = hat * g + b
            zhat[index, i : i + 16, :] = hat
            rinv[index, i : i + 16, :] = inv
            result[i : i + 16, :] = done
            full[target, rows_at(k * own + i, 16), :] = done.astype(BF)

        return body

    def norm_back(read, layer, which, gain, target):
        index = 2 * layer + which
        g = gain[layer : layer + 1, :]

        def body(i):
            scaled = read(i) * g
            hat = zhat[index, i : i + 16, :]
            inv = rinv[index, i : i + 16, :]
            first = jnp.mean(scaled, axis=-1, keepdims=True)
            second = jnp.mean(scaled * hat, axis=-1, keepdims=True)
            result = inv * (scaled - first - hat * second)
            own_g[i : i + 16, :] = result
            full[target, rows_at(k * own + i, 16), :] = result.astype(BF)

        return body

    def weights_at(layer, point):
        for kind, p, distance in SCHEDULE.get((layer, point), ()):
            if kind == "along":
                issue(p)
            elif kind == "beside":
                beside_own(p)
            elif kind == "swap":
                swap(p)
            else:
                passes(p, distance - 1, (kind == "up",))

    def forward_layer(layer):
        base = 4 * layer
        rs_a, rs_f = ((RS_A0, RS_F0), (RS_A1, RS_F1))[layer]
        ag_m = (AG_M0, AG_M1)[layer]
        source = tokens if layer == 0 else full.at[AG_X1]
        here = functools.partial(weights_at, layer)
        here("start")
        arrive(base)
        if layer > 0:
            ag_near(AG_X1)
        project(layer, source, near)
        here("projected near")
        if layer == 0:
            for i in range(2):
                pre_own(i).wait()
                for d in range(1, KEYS):
                    pre_copy(i, d).wait_recv()
        if layer > 0:
            ag_far(AG_X1)
        project(layer, source, far)
        here("projected")
        attend(layer, block_b)
        here("attended b")
        arrive(base + 1)
        out_rows(layer, block_b * own, own)
        for i in range(SUBS):
            rs_copy(rs_a, i).start()
        here("out b")
        attend(layer, block_a)
        out_rows(layer, block_a * own, own)
        for i in range(SUBS):
            rs_mid(rs_a, i)
        here("out a")
        two(functools.partial(attend, layer), near)
        out_rows(layer, near * half, half)
        rs_near(rs_a)
        here("out near")
        rs_each(
            rs_a,
            norm_into(rs_a, own_x, layer, 0, g1, b1, own_m, ag_m),
            ag_m,
            lambda i: here(f"norm {i}"),
        )
        here("normed")
        arrive(base + 2)
        ag_near(ag_m)
        here("up")
        up_half(layer, ag_m, near)
        here("up near")
        ag_far(ag_m)
        up_half(layer, ag_m, far)
        here("up far")
        arrive(base + 3)
        here("down")
        scatter_far(
            rs_f,
            lambda i: dot_nt(both(hid, at=far_rows(i)), wd[layer]).astype(BF),
            lambda i: here(f"down {i}"),
        )
        part[half_rows(near), :] = dot_nt(hid[half_rows(near), :], wd[layer]).astype(BF)
        rs_near(rs_f)
        here("down near")

    forward_layer(0)
    rs_each(
        RS_F0,
        norm_into(RS_F0, own_m, 0, 1, g2, b2, own_x, AG_X1),
        AG_X1,
        lambda i: weights_at(0, f"last norm {i}"),
    )
    forward_layer(1)

    def prefix_copy(layer, i, d):
        kt = lax.rem(k + d, KEYS)
        source = (gk, gv)[i]
        return pltpu.make_async_remote_copy(
            src_ref=source.at[pl.ds(pl.multiple_of(kt * count, count), count), :],
            dst_ref=pg.at[layer, i, :, columns],
            send_sem=pg_send.at[i, d], recv_sem=pg_recv.at[i, d],
            device_id=(r, kt), device_id_type=MESH,
        )

    def prefix_own(layer, i):
        return pltpu.make_async_copy(
            (gk, gv)[i].at[pl.ds(pl.multiple_of(k * count, count), count), :],
            pg.at[layer, i, :, columns],
            pg_recv.at[i, 0],
        )

    bits = rows.bit_length() - 1

    def row_copy(layer, b):
        bit = 1 << b
        partner = r + bit - 2 * bit * lax.rem(r // bit, 2)
        return pltpu.make_async_remote_copy(
            src_ref=pg_low.at[layer], dst_ref=pg_in.at[layer, b],
            send_sem=pgr_send.at[layer, b], recv_sem=pgr_recv.at[layer, b],
            device_id=(partner, k), device_id_type=MESH,
        )

    def row_start(layer, b):
        low = pg[layer].astype(BF)
        pg_low[layer] = low
        pg[layer] = low.astype(F32)
        row_copy(layer, b).start()

    def row_step(layer, b):
        row_copy(layer, b).wait()
        pg[layer] += pg_in[layer, b].astype(F32)
        if b + 1 < bits:
            row_start(layer, b + 1)

    def prefix_start(layer):
        for i in range(2):
            prefix_own(layer, i).start()
            for d in range(1, KEYS):
                prefix_copy(layer, i, d).start()

    def prefix_take(layer):
        for i in range(2):
            prefix_own(layer, i).wait()
            for d in range(1, KEYS):
                prefix_copy(layer, i, d).wait_recv()
        row_start(layer, 0)

    def prefix_sent(layer):
        for i in range(2):
            for d in range(1, KEYS):
                prefix_copy(layer, i, d).wait_send()

    for layer in reversed(range(LAYERS)):
        rs_gm, rs_gx = ((RS_GM0, RS_GX0), (RS_GM1, RS_GX1))[layer]
        ag_gf, ag_ga = ((AG_GF0, AG_GA0), (AG_GF1, AG_GA1))[layer]
        if layer == LAYERS - 1:
            forth = norm_into(RS_F1, own_m, 1, 1, g2, b2, own_x, AG_ACT)
            back = norm_back(lambda i: cot[i : i + 16, :].astype(F32), layer, 1, g2, ag_gf)

            def turn(i):
                forth(i)
                back(i)

            rs_each(RS_F1, turn, ag_gf)
        else:
            rs_each(RS_GX1, norm_back(lambda i: own_g[i : i + 16, :] + rs_sum(RS_GX1, i), layer, 1, g2, ag_gf), ag_gf)
            prefix_take(layer + 1)
        ag_near(ag_gf)
        part[half_rows(near), :] = ff_back(layer, full[ag_gf, half_rows(near), :], gelu_d[layer, half_rows(near), :])
        rs_near(rs_gm)

        def step(i):
            ag_pass(ag_gf, i)
            ag_got(ag_gf, i)
            at = far_rows(i)
            return ff_back(layer, both(full, ag_gf, at=at), both(gelu_d, layer, at=at))

        scatter_far(rs_gm, step)
        if layer == 0:
            row_step(1, 0)
        gk[...] = jnp.zeros_like(gk)
        gv[...] = jnp.zeros_like(gv)
        rs_each(rs_gm, norm_back(lambda i: own_g[i : i + 16, :] + rs_sum(rs_gm, i), layer, 0, g1, ag_ga), ag_ga)
        if layer == LAYERS - 1:
            for i in range(SUBS + 1):
                ag_copy(AG_ACT, i).start()
        ag_near(ag_ga)
        go[half_rows(near), :] = dot_nt(full[ag_ga, half_rows(near), :], wo[layer]).astype(BF)
        two(functools.partial(attend_back, layer), near)
        if layer == 0:
            row_step(1, 1)
        ag_far(ag_ga)
        go[half_rows(far), :] = dot_nt(full[ag_ga, half_rows(far), :], wo[layer]).astype(BF)
        two(functools.partial(attend_back, layer), far)
        prefix_start(layer)

        def narrow(which):
            def body(i):
                i = which * half + i
                gqkv[rows_at(i, 16), wide : 2 * wide] = gk[rows_at(prefix + i, 16), :].astype(BF)
                gqkv[rows_at(i, 16), 2 * wide : 3 * wide] = gv[rows_at(prefix + i, 16), :].astype(BF)

            chunks(half, body)

        narrow(far)
        project_back(layer, block_b * own, own)
        for i in range(SUBS):
            rs_copy(rs_gx, i).start()
        project_back(layer, block_a * own, own)
        for i in range(SUBS):
            rs_mid(rs_gx, i)
        narrow(near)
        project_back(layer, near * half, half)
        rs_near(rs_gx)
        if layer == LAYERS - 1:
            ag_far(AG_ACT)
            ag_near(AG_ACT)
        else:
            for b in range(2, bits):
                row_step(1, b)
            prefix_take(0)
        prefix_sent(layer)

    act_copy = pltpu.make_async_copy(full.at[AG_ACT], low_out.at[1], loc.at[13])
    act_copy.start()

    def last(i):
        full[AG_GX, rows_at(k * own + i, 16), :] = (own_g[i : i + 16, :] + rs_sum(RS_GX0, i)).astype(BF)

    rs_each(RS_GX0, last, AG_GX)
    for p in range(4 * LAYERS):
        drain(p)
    for i in range(2):
        for d in range(1, KEYS):
            pre_copy(i, d).wait_send()
    row_step(0, 0)
    ag_near(AG_GX)

    def grad_copy(which):
        return pltpu.make_async_copy(
            full.at[AG_GX, half_rows(which), :], low_out.at[0, half_rows(which), :], loc.at[14 + (which is far)]
        )

    grad_copy(near).start()
    ag_far(AG_GX)
    grad_copy(far).start()
    for b in range(1, bits):
        row_step(0, b)
    for i in range(2):
        for layer in range(LAYERS):
            prefix_out[i, layer] = pg[layer, i]
    ag_end(AG_GX)
    ag_end(AG_ACT)
    act_copy.wait()
    grad_copy(near).wait()
    grad_copy(far).wait()


def results(low, grads, act, gt, gpk, gpv, narrow, broad, act_held, grads_held, sems):
    parts, size = narrow.shape[:2]

    def taken(i):
        return pltpu.make_async_copy(low.at[0, i * size : (i + 1) * size, :], narrow.at[i], sems.at[0, i])

    def given(i):
        return pltpu.make_async_copy(broad.at[i], gt.at[0, i * size : (i + 1) * size, :], sems.at[1, i])

    in_act = pltpu.make_async_copy(low.at[1], act_held, sems.at[2, 0])
    out_act = pltpu.make_async_copy(act_held, act.at[0], sems.at[2, 0])
    in_grads = pltpu.make_async_copy(grads, grads_held, sems.at[2, 1])
    out_grads = [pltpu.make_async_copy(grads_held.at[i], (gpk, gpv)[i], sems.at[2, 2 + i]) for i in range(2)]
    for i in range(parts):
        taken(i).start()
    in_act.start()
    in_grads.start()
    for i in range(parts):
        taken(i).wait()
        broad[i] = narrow[i].astype(F32)
        given(i).start()
    in_act.wait()
    out_act.start()
    in_grads.wait()
    for copy in out_grads:
        copy.start()
    for i in range(parts):
        given(i).wait()
    out_act.wait()
    for copy in out_grads:
        copy.wait()


def per_device(
    tokens, cotangent, segment_ids, pad_mask, prefix_keys, prefix_values,
    w_query, w_key, w_value, w_out, w_up, w_down_t,
    norm1_gain, norm1_bias, norm2_gain, norm2_bias,
):
    rows, keys = lax.axis_size("rows"), lax.axis_size("keys")
    assert keys == KEYS and rows % (2 * KEYS) == 0 and rows & (rows - 1) == 0
    tok, width = tokens.shape[1:]
    count = prefix_keys.shape[1]
    prefix = count * keys
    local_ff = w_up.shape[2]
    wide, own, window = width // keys, tok // keys, 3 * tok // keys
    heads = wide // HEAD
    nz, bits, pieces = rows // 2, rows.bit_length() - 1, 4 * LAYERS
    vmem, anywhere = pl.BlockSpec(memory_space=pltpu.VMEM), pl.BlockSpec(memory_space=pl.ANY)
    dma = pltpu.SemaphoreType.DMA
    scratch = [
        pltpu.VMEM((LAYERS, width, 3 * wide), BF),
        pltpu.VMEM((LAYERS, wide, width), BF),
        pltpu.VMEM((LAYERS, width, local_ff), BF),
        pltpu.VMEM((LAYERS, width, local_ff), BF),
        pltpu.VMEM((LAYERS, prefix, wide), BF),
        pltpu.VMEM((LAYERS, prefix, wide), BF),
        pltpu.VMEM((tok, width), BF),
        pltpu.VMEM((SCATTERS, 2, own, width), BF),
        pltpu.VMEM((SCATTERS, own, width), BF),
        pltpu.VMEM((own, width), BF),
        pltpu.VMEM((GATHERS, tok, width), BF),
        pltpu.VMEM((LAYERS, tok, 3 * wide), BF),
        pltpu.VMEM((LAYERS, keys, prefix + window, heads * own), F32),
        pltpu.VMEM((LAYERS, tok, local_ff), F32),
        pltpu.VMEM((2 * LAYERS, own, width), F32),
        pltpu.VMEM((2 * LAYERS, own, 1), F32),
        pltpu.VMEM((own, width), F32),
        pltpu.VMEM((own, width), F32),
        pltpu.VMEM((own, width), F32),
        pltpu.VMEM((own, width), BF),
        pltpu.VMEM((tok, wide), BF),
        pltpu.VMEM((tok, 3 * wide), BF),
        pltpu.VMEM((prefix + tok, wide), F32),
        pltpu.VMEM((prefix + tok, wide), F32),
        pltpu.VMEM((tok, local_ff), BF),
        pltpu.VMEM((tok, wide), BF),
        pltpu.VMEM((keys, window, own), F32),
        pltpu.VMEM((tok, own), F32),
        pltpu.VMEM((LAYERS, 2, count, width), F32),
        pltpu.VMEM((LAYERS, 2, count, width), BF),
        pltpu.VMEM((LAYERS, bits, 2, count, width), BF),
        dma((pieces, 2, nz + 1)),
        dma((pieces, 2, nz)),
        dma((pieces, nz)),
        dma((16,)),
        dma((2, keys)),
        dma((2, keys)),
        dma((2 * SUBS + 1,)),
        dma((2 * SUBS + 1,)),
        dma((2, 2 * SUBS + 1)),
        dma((2, 2 * SUBS + 1)),
        dma((2, keys)),
        dma((2, keys)),
        dma((LAYERS, bits)),
        dma((LAYERS, bits)),
    ]
    low, grads = pl.pallas_call(
        functools.partial(kernel, (rows, tok, width, local_ff)),
        out_shape=(
            jax.ShapeDtypeStruct((2, tok, width), BF),
            jax.ShapeDtypeStruct((2, LAYERS, count, width), F32),
        ),
        in_specs=[vmem, anywhere, vmem, vmem] + [anywhere] * 8 + [vmem] * 4,
        out_specs=(anywhere, vmem),
        scratch_shapes=scratch,
        compiler_params=pltpu.CompilerParams(
            collective_id=0, has_side_effects=True, vmem_limit_bytes=62 * 1024 * 1024 - 512 * 1024
        ),
    )(
        tokens[0], cotangent[0], segment_ids, pad_mask, prefix_keys, prefix_values,
        w_query, w_key, w_value, w_out, w_up, w_down_t,
        norm1_gain, norm1_bias, norm2_gain, norm2_bias,
    )
    whole = (LAYERS, count, width)
    return pl.pallas_call(
        results,
        out_shape=(
            jax.ShapeDtypeStruct((1, tok, width), BF),
            jax.ShapeDtypeStruct((1, tok, width), F32),
            jax.ShapeDtypeStruct(whole, F32),
            jax.ShapeDtypeStruct(whole, F32),
        ),
        in_specs=[anywhere] * 2,
        out_specs=(anywhere,) * 4,
        scratch_shapes=[
            pltpu.VMEM((keys, own, width), BF),
            pltpu.VMEM((keys, own, width), F32),
            pltpu.VMEM((tok, width), BF),
            pltpu.VMEM((2, *whole), F32),
            dma((3, keys)),
        ],
    )(low, grads)


def solution(mesh):
    row3 = P("rows", None, None)
    weight = P(None, "rows", None)
    return jax.shard_map(
        per_device,
        mesh=mesh,
        in_specs=(
            row3,
            row3,
            P("rows", None),
            P("rows", None),
            P(None, "keys", None),
            P(None, "keys", None),
            weight,
            weight,
            weight,
            weight,
            P(None, "rows", "keys"),
            P(None, "rows", "keys"),
            P(),
            P(),
            P(),
            P(),
        ),
        out_specs=(row3, row3, P(None, "keys", None), P(None, "keys", None)),
        check_vma=False,
    )
```

```python
import functools

import jax
import jax.numpy as jnp
from jax import lax
from jax.experimental import pallas as pl
from jax.experimental.pallas import tpu as pltpu
from jax.sharding import PartitionSpec as P

HEAD = 64
LAYERS = 2
KEYS = 4
EPSILON = 1e-05
NEGATIVE = -1000000000.0
MESH = pl.DeviceIdType.MESH
BF = jnp.bfloat16
F32 = jnp.float32

AG_M0, AG_X1, AG_M1, AG_GF1, AG_GF0, AG_GX, AG_ACT = range(7)
GATHERS = 7
RS_A0, RS_F0, RS_A1, RS_F1, RS_GM1, RS_GX1, RS_GM0, RS_GX0 = range(8)
SCATTERS = 8
GATHER_BEFORE = (None, AG_M0, AG_X1, AG_M1, AG_GF1, None, AG_GF0, None)
SUBS = 2

SCHEDULE = {
    (0, "start"): (
        ("beside", 1, 0),
        ("beside", 7, 0),
        ("along", 1, 0),
        ("beside", 2, 0),
        ("along", 0, 0),
        ("down", 1, 1),
        ("along", 4, 0),
        ("up", 1, 1),
        ("down", 0, 1),
        ("up", 0, 1),
        ("up", 1, 2),
        ("down", 1, 2),
        ("along", 2, 0),
        ("up", 0, 2),
        ("up", 1, 3),
        ("beside", 0, 0),
        ("down", 0, 2),
        ("up", 2, 1),
        ("down", 1, 3),
        ("down", 2, 1),
        ("up", 0, 3),
        ("along", 5, 0),
        ("up", 2, 2),
        ("down", 0, 3),
        ("along", 3, 0),
        ("down", 2, 2),
        ("up", 2, 3),
        ("down", 3, 1),
        ("down", 5, 1),
        ("up", 3, 1),
        ("up", 3, 2),
    ),
    (0, "attended b"): (
        ("up", 5, 2),
    ),
    (0, "out b"): (
        ("beside", 5, 0),
        ("up", 5, 1),
        ("along", 6, 0),
    ),
    (0, "out a"): (
        ("beside", 3, 0),
        ("down", 3, 2),
        ("down", 5, 2),
        ("down", 2, 3),
    ),
    (0, "norm 1"): (
        ("up", 4, 1),
        ("up", 3, 3),
        ("up", 4, 2),
        ("down", 4, 1),
    ),
    (0, "normed"): (
        ("up", 4, 3),
        ("swap", 7, 0),
    ),
    (0, "up"): (
        ("down", 3, 3),
        ("down", 4, 2),
    ),
    (0, "up far"): (
        ("along", 7, 0),
    ),
    (0, "down 0"): (
        ("beside", 4, 0),
        ("up", 6, 1),
    ),
    (0, "down 1"): (
        ("down", 5, 3),
        ("up", 5, 3),
    ),
    (0, "last norm 0"): (
        ("down", 4, 3),
        ("down", 6, 1),
    ),
    (0, "last norm 1"): (
        ("up", 6, 2),
        ("down", 6, 2),
    ),
    (1, "start"): (
        ("beside", 6, 0),
        ("down", 7, 1),
    ),
    (1, "projected near"): (
        ("up", 7, 1),
    ),
    (1, "out b"): (
        ("up", 6, 3),
    ),
    (1, "out a"): (
        ("down", 6, 3),
    ),
    (1, "norm 0"): (
        ("down", 7, 2),
    ),
    (1, "norm 1"): (
        ("up", 7, 2),
    ),
    (1, "up far"): (
        ("up", 7, 3),
        ("down", 7, 3),
    ),
}
STRAIGHT = (7,)


def dot_nn(a, b):
    return lax.dot_general(a, b, (((1,), (0,)), ((), ())), preferred_element_type=F32)


def dot_nt(a, b):
    return lax.dot_general(a, b, (((1,), (1,)), ((), ())), preferred_element_type=F32)


def dot_tn(a, b):
    return lax.dot_general(a, b, (((0,), (0,)), ((), ())), preferred_element_type=F32)


def kernel(
    dims,
    tokens, cotangent, segments, padding, pre_k, pre_v,
    w_query, w_key, w_value, w_out, w_up, w_down,
    g1, b1, g2, b2,
    low_out, prefix_out,
    wqkv, wo, wu, wd, pk, pv,
    part, rc, ry, ys, full,
    qkv, prob, gelu_d, zhat, rinv,
    own_x, own_m, own_g, cot, att, gqkv, gk, gv, hid, ga, go_all, go, bias, codes,
    pg, pg_low, pg_in,
    w_send, w_recv, w_over, loc, pre_send, pre_recv,
    wq_send, wq_recv, go_send, go_recv,
    rs_send, rs_recv, ag_send, ag_recv, pg_send, pg_recv, pgr_send, pgr_recv,
):
    rows, tok, width, local_ff = dims
    nz = rows // 2
    wide = width // KEYS
    heads = wide // HEAD
    own = tok // KEYS
    half = tok // 2
    depth = width // rows
    count = pre_k.shape[1]
    prefix = KEYS * count
    window = 3 * own

    r = lax.axis_index("rows")
    k = lax.axis_index("keys")
    z, x = r // 2, lax.rem(r, 2)
    y, c = k // 2, lax.rem(k, 2)
    sib = (r, k + 1 - 2 * c)
    across = (r, lax.rem(k + 2, KEYS))
    beside = (r + 1 - 2 * x, k)
    far, near = 1 - y, y

    def level(d):
        return lax.rem(z + d, nz)

    barrier = pltpu.get_barrier_semaphore()

    def greet(d, carry):
        pl.semaphore_signal(barrier, inc=1, device_id=(level(d) * 2 + x, k), device_id_type=MESH)
        return carry

    lax.fori_loop(1, nz, greet, 0)
    pl.semaphore_signal(barrier, inc=1, device_id=beside, device_id_type=MESH)
    for d in range(1, KEYS):
        pl.semaphore_signal(barrier, inc=1, device_id=(r, lax.rem(k + d, KEYS)), device_id_type=MESH)

    group = nz // KEYS

    def spot(ref, layer, at):
        return ref.at[layer, pl.ds(pl.multiple_of(at * depth, depth), depth), :]

    def slot(p, zz, xx):
        layer, kind = divmod(p, 4)
        at = zz * 2 + xx
        return spot((wqkv, wo, wu, wd)[kind], layer, at)

    def active(p, zz):
        return None if p % 4 != 1 else (zz // group) == k

    def guarded(condition, action):
        if condition is None:
            action()
        else:
            pl.when(condition)(action)

    columns = pl.ds(pl.multiple_of(k * wide, wide), wide)

    def own_copies(p):
        layer, kind = divmod(p, 4)
        if kind == 0:
            place = pl.ds(pl.multiple_of(r * depth, depth), depth)
            return [
                pltpu.make_async_copy(
                    w.at[layer, :, columns], wqkv.at[layer, place, i * wide : (i + 1) * wide], loc.at[6 * layer + i]
                )
                for i, w in enumerate((w_query, w_key, w_value))
            ]
        source = (None, w_out, w_up, w_down)[kind]
        return [pltpu.make_async_copy(source.at[layer], slot(p, z, x), loc.at[6 * layer + 2 + kind])]

    def own_start(p):
        guarded(active(p, z), lambda: [copy.start() for copy in own_copies(p)] and None)

    def own_wait(p):
        guarded(active(p, z), lambda: [copy.wait() for copy in own_copies(p)] and None)

    def push(p, zz, xx, send_sem, target):
        place = slot(p, zz, xx)
        return pltpu.make_async_remote_copy(
            src_ref=place, dst_ref=place, send_sem=send_sem, recv_sem=w_recv.at[p, xx, zz],
            device_id=target, device_id_type=MESH,
        )

    def straight(p):
        return p in STRAIGHT

    def up(p, zz, xx):
        return push(p, zz, xx, w_send.at[p, xx, zz], (lax.rem(z + 1, nz) * 2 + x, k))

    def down(p, zz, xx):
        sem = w_send.at[p, xx, jnp.where(zz == z, nz, zz)]
        return push(p, zz, xx, sem, (lax.rem(z + nz - 1, nz) * 2 + x, k))

    def over(p, zz):
        return push(p, zz, x, w_over.at[p, zz], beside)

    not_top, not_bottom = z < nz - 1, z > 0

    def spread_own(p, xx, action):
        pl.when(not_top)(lambda: action(up(p, z, xx)))
        pl.when(not_bottom)(lambda: action(down(p, z, xx)))

    def begin(copy):
        copy.start()

    def sent(copy):
        copy.wait_send()

    def issue(p):
        guarded(active(p, z), lambda: spread_own(p, x, begin))

    def beside_own(p):
        guarded(active(p, z), lambda: over(p, z).start())

    def swap(p):
        over_in = push(p, z, 1 - x, w_over.at[p, z], beside)
        over_in.wait_recv()
        spread_own(p, 1 - x, begin)

    def hops(group, action, sides=(True, False)):
        bounds = [1 + (nz - 1) * i // 3 for i in range(4)]

        def one(j, carry):
            if True in sides:
                pl.when(z - j >= 0)(lambda: action(jnp.maximum(z - j, 0), True))
            if False in sides:
                pl.when(z + j < nz)(lambda: action(jnp.minimum(z + j, nz - 1), False))
            return carry

        lax.fori_loop(bounds[group], bounds[group + 1], one, 0)

    def onward(p, zz, xx, below, action):
        if below:
            pl.when(not_top)(lambda: action(up(p, zz, xx)))
        else:
            pl.when(not_bottom)(lambda: action(down(p, zz, xx)))

    def passes(p, group, sides):
        def action(zz, below):
            def take():
                for xx in (x, 1 - x) if straight(p) else (x,):
                    push(p, zz, xx, w_over.at[p, zz], beside).wait_recv()
                    onward(p, zz, xx, below, begin)
                if not straight(p):
                    over(p, zz).start()

            guarded(active(p, zz), take)

        hops(group, action, sides)

    def arrive(p):
        if straight(p):
            return

        def one(zz, carry):
            guarded(active(p, zz), push(p, zz, 1 - x, w_over.at[p, zz], beside).wait_recv)
            return carry

        lax.fori_loop(0, nz, one, 0)

    def drain(p):
        def mine():
            spread_own(p, x, sent)
            if straight(p):
                spread_own(p, 1 - x, sent)
            over(p, z).wait_send()

        guarded(active(p, z), mine)

        def action(zz, below):
            def passed():
                for xx in (x, 1 - x) if straight(p) else (x,):
                    onward(p, zz, xx, below, sent)
                if not straight(p):
                    over(p, zz).wait_send()

            guarded(active(p, zz), passed)

        for group_at in range(3):
            hops(group_at, action)

    def pre_copy(i, d):
        kt = lax.rem(k + d, KEYS)
        source, target = ((pre_k, pk), (pre_v, pv))[i]
        return pltpu.make_async_remote_copy(
            src_ref=source.at[:, :, pl.ds(pl.multiple_of(kt * wide, wide), wide)],
            dst_ref=target.at[:, pl.ds(pl.multiple_of(k * count, count), count), :],
            send_sem=pre_send.at[i, d], recv_sem=pre_recv.at[i, d], device_id=(r, kt), device_id_type=MESH,
        )

    def pre_own(i):
        source, target = ((pre_k, pk), (pre_v, pv))[i]
        return pltpu.make_async_copy(
            source.at[:, :, columns],
            target.at[:, pl.ds(pl.multiple_of(k * count, count), count), :],
            pre_recv.at[i, 0],
        )

    own_block = pl.ds(pl.multiple_of(k * own, own), own)
    cot_copy = pltpu.make_async_copy(cotangent.at[own_block, :], cot, loc.at[12])

    for p in range(4 * LAYERS):
        own_start(p)
    cot_copy.start()
    for i in range(2):
        pre_own(i).start()

    visible_code = jnp.where(padding[...] == 1, segments[...], -1).astype(F32)
    codes[...] = jnp.broadcast_to(visible_code, (own, tok)).T

    def mask_of(i, carry):
        queries = segments[:, pl.ds(pl.multiple_of(i * own, own), own)].astype(F32)
        keys_code = codes[pl.ds(pl.multiple_of(jnp.clip(i - 1, 0, KEYS - 3) * own, own), window), :]
        bias[i] = jnp.where(keys_code == queries, 0.0, NEGATIVE)
        return carry

    lax.fori_loop(0, KEYS, mask_of, 0)

    def widen(i, carry):
        at = pl.multiple_of(i * 16, 16)
        own_x[pl.ds(at, 16), :] = tokens[pl.ds(k * own + at, 16), :].astype(F32)
        return carry

    lax.fori_loop(0, own // 16, widen, 0)
    pl.semaphore_wait(barrier, nz - 1 + 1 + KEYS - 1)
    own_wait(0)
    for i in range(2):
        for d in range(1, KEYS):
            pre_copy(i, d).start()
    for p in range(1, 4 * LAYERS):
        own_wait(p)
    cot_copy.wait()

    sub = own // SUBS
    block_a, block_b = 2 * far + c, 2 * far + 1 - c

    def rows_at(at, size):
        return pl.ds(pl.multiple_of(at, 16), size)

    def rs_copy(n, i):
        if i < SUBS:
            source, target = part.at[rows_at(block_b * own + i * sub, sub), :], rc.at[n, 0, i * sub : (i + 1) * sub, :]
        elif i == SUBS:
            source, target = part.at[rows_at((2 * near + 1 - c) * own, own), :], rc.at[n, 1]
        else:
            at = slice((i - SUBS - 1) * sub, (i - SUBS) * sub)
            source, target = ys.at[at, :], ry.at[n, at, :]
        return pltpu.make_async_remote_copy(
            src_ref=source, dst_ref=target, send_sem=rs_send.at[i], recv_sem=rs_recv.at[i],
            device_id=sib if i <= SUBS else across, device_id_type=MESH,
        )

    def chunks(total, body, size=16):
        def one(i, carry):
            body(pl.multiple_of(i * size, size))
            return carry

        lax.fori_loop(0, total // size, one, 0)

    def rs_mid(n, i):
        rs_copy(n, i).wait_recv()
        for at in range(i * sub, (i + 1) * sub, 16):
            mine = part[rows_at(block_a * own + at, 16), :].astype(F32)
            ys[at : at + 16, :] = (mine + rc[n, 0, at : at + 16, :].astype(F32)).astype(BF)
        rs_copy(n, SUBS + 1 + i).start()

    def rs_near(n):
        rs_copy(n, SUBS).start()

    def rs_sum(n, at):
        mine = part[rows_at(k * own + at, 16), :].astype(F32) + rc[n, 1, at : at + 16, :].astype(F32)
        return mine + ry[n, at : at + 16, :].astype(F32)

    def rs_each(n, body, leave, between=lambda i: None):
        if GATHER_BEFORE[n] is not None:
            ag_end(GATHER_BEFORE[n])
        rs_copy(n, SUBS).wait_recv()
        for i in range(SUBS):
            between(i)
            rs_copy(n, SUBS + 1 + i).wait_recv()
            for at in range(i * sub, (i + 1) * sub, 16):
                body(at)
            leave(i)
        rs_end(n)

    def gather(n):
        def leave(i):
            ag_copy(n, i).start()
            if i == SUBS - 1:
                ag_copy(n, SUBS).start()

        return leave

    def rs_end(n):
        for i in range(2 * SUBS + 1):
            rs_copy(n, i).wait_send()

    def ag_copy(n, i):
        if i < SUBS:
            place, device = full.at[n, rows_at(k * own + i * sub, sub), :], across
        elif i == SUBS:
            place, device = full.at[n, rows_at(k * own, own), :], sib
        else:
            place, device = full.at[n, rows_at(block_a * own + (i - SUBS - 1) * sub, sub), :], sib
        return pltpu.make_async_remote_copy(
            src_ref=place, dst_ref=place, send_sem=ag_send.at[n // AG_ACT, i], recv_sem=ag_recv.at[n // AG_ACT, i],
            device_id=device, device_id_type=MESH,
        )

    def ag_end(n):
        for i in range(2 * SUBS + 1):
            ag_copy(n, i).wait_send()

    def ag_near(n):
        ag_copy(n, SUBS).wait_recv()

    def ag_pass(n, i):
        ag_copy(n, i).wait_recv()
        ag_copy(n, SUBS + 1 + i).start()

    def ag_got(n, i):
        ag_copy(n, SUBS + 1 + i).wait_recv()

    def ag_far(n):
        for i in range(SUBS):
            ag_pass(n, i)
        for i in range(SUBS):
            ag_got(n, i)

    def half_rows(which):
        return pl.ds(pl.multiple_of(which * half, half), half)

    def far_rows(i):
        return rows_at(block_a * own + i * sub, sub), rows_at(block_b * own + i * sub, sub)

    def both(ref, *lead, at):
        return jnp.concatenate([ref[(*lead, rows, slice(None))] for rows in at], axis=0)

    def project(layer, source, which):
        hr = half_rows(which)
        xin = source[hr, :]
        for i in range(3):
            at = slice(i * wide, (i + 1) * wide)
            val = dot_nn(xin, wqkv[layer, :, at])
            qkv[layer, hr, at] = (val * HEAD**-0.5 if i == 0 else val).astype(BF)

    lane_head = lax.broadcasted_iota(jnp.int32, (1, wide), 1) // HEAD
    masks = [jnp.where(lane_head == h, 1.0, 0.0).astype(BF) for h in range(heads)]

    def stacked(value):
        return jnp.concatenate([value * mask for mask in masks], axis=0)

    def place_of(i):
        return pl.multiple_of(i * own, own)

    def window_of(i):
        return pl.multiple_of(jnp.clip(i - 1, 0, KEYS - 3) * own, own)

    def unstacked(value):
        parts = [value[h * HEAD : (h + 1) * HEAD, h * own : (h + 1) * own] for h in range(heads)]
        return jnp.concatenate(parts, axis=0).T

    def attend(layer, i):
        q4 = stacked(qkv[layer, pl.ds(place_of(i), own), 0:wide])
        span = pl.ds(window_of(i), window)
        mask = bias[i]
        s_tok = dot_nt(qkv[layer, span, wide : 2 * wide], q4) + jnp.concatenate([mask] * heads, axis=1)
        s_pre = dot_nt(pk[layer], q4)
        top = jnp.maximum(jnp.max(s_tok, axis=0, keepdims=True), jnp.max(s_pre, axis=0, keepdims=True))
        e_tok, e_pre = jnp.exp(s_tok - top), jnp.exp(s_pre - top)
        inverse = 1.0 / (jnp.sum(e_tok, axis=0, keepdims=True) + jnp.sum(e_pre, axis=0, keepdims=True))
        p_tok, p_pre = e_tok * inverse, e_pre * inverse
        prob[layer, i, 0:prefix, :] = p_pre
        prob[layer, i, prefix : prefix + window, :] = p_tok
        out = dot_tn(qkv[layer, span, 2 * wide : 3 * wide], p_tok.astype(BF))
        out += dot_tn(pv[layer], p_pre.astype(BF))
        att[pl.ds(place_of(i), own), :] = unstacked(out).astype(BF)

    def attend_back(layer, i):
        at = pl.ds(place_of(i), own)
        q4 = stacked(qkv[layer, at, 0:wide])
        go4 = stacked(go[at, :])
        start = window_of(i)
        span = pl.ds(start, window)
        p_pre = prob[layer, i, 0:prefix, :]
        p_tok = prob[layer, i, prefix : prefix + window, :]
        gp_tok = dot_nt(qkv[layer, span, 2 * wide : 3 * wide], go4)
        gp_pre = dot_nt(pv[layer], go4)
        dsum = jnp.sum(p_tok * gp_tok, axis=0, keepdims=True) + jnp.sum(p_pre * gp_pre, axis=0, keepdims=True)
        gs_tok = (p_tok * (gp_tok - dsum)).astype(BF)
        gs_pre = (p_pre * (gp_pre - dsum)).astype(BF)
        places = pl.ds(prefix + start, window)
        gk[places, :] += dot_nn(gs_tok, q4)
        gk[0:prefix, :] += dot_nn(gs_pre, q4)
        gv[places, :] += dot_nn(p_tok.astype(BF), go4)
        gv[0:prefix, :] += dot_nn(p_pre.astype(BF), go4)
        gq = dot_tn(qkv[layer, span, wide : 2 * wide], gs_tok) + dot_tn(pk[layer], gs_pre)
        gqkv[at, 0:wide] = (unstacked(gq).astype(BF).astype(F32) * HEAD**-0.5).astype(BF)

    def two(body, which):
        def one(i, carry):
            body(2 * which + i)
            return carry

        lax.fori_loop(0, 2, one, 0)

    def out_rows(layer, at, size):
        rows_here = rows_at(at, size)
        part[rows_here, :] = dot_nn(att[rows_here, :], wo[layer, columns, :]).astype(BF)

    def up_half(layer, n, which):
        hr = half_rows(which)
        u = dot_nn(full[n, hr, :], wu[layer])
        for at in range(0, half, 16):
            v = u[at : at + 16]
            phi_sum = 0.5 * (1.0 + lax.erf(v * 0.7071067811865476))
            density = jnp.exp(v * v * -0.5) * 0.3989422804014327
            here = rows_at(which * half + at, 16)
            hid[here, :] = (v * phi_sum).astype(BF)
            gelu_d[layer, here, :] = phi_sum + v * density

    def ff_back(layer, gradient, slope):
        gu = (dot_nn(gradient, wd[layer]) * slope).astype(BF)
        return dot_nt(gu, wu[layer]).astype(BF)

    def scatter_far(n, step, between=lambda i: None):
        for i in range(SUBS):
            between(i)
            value = step(i)
            at_a, at_b = far_rows(i)
            part[at_b, :] = value[sub:]
            rs_copy(n, i).start()
            part[at_a, :] = value[:sub]
            if i > 0:
                rs_mid(n, i - 1)
        rs_mid(n, SUBS - 1)

    def project_back(layer, at, size):
        rows_here = rows_at(at, size)
        part[rows_here, :] = dot_nt(gqkv[rows_here, :], wqkv[layer]).astype(BF)

    def norm_into(n, residual, layer, which, gain, shift, result, target):
        index = 2 * layer + which
        g, b = gain[layer : layer + 1, :], shift[layer : layer + 1, :]

        def body(i):
            value = residual[i : i + 16, :] + rs_sum(n, i)
            centre = value - jnp.mean(value, axis=-1, keepdims=True)
            inv = lax.rsqrt(jnp.mean(centre * centre, axis=-1, keepdims=True) + EPSILON)
            hat = centre * inv
            done = hat * g + b
            zhat[index, i : i + 16, :] = hat
            rinv[index, i : i + 16, :] = inv
            result[i : i + 16, :] = done
            full[target, rows_at(k * own + i, 16), :] = done.astype(BF)

        return body

    def into(n):
        def store(i, low):
            full[n, rows_at(k * own + i, 16), :] = low

        return store

    def norm_back(read, layer, which, gain, store):
        index = 2 * layer + which
        g = gain[layer : layer + 1, :]

        def body(i):
            scaled = read(i) * g
            hat = zhat[index, i : i + 16, :]
            inv = rinv[index, i : i + 16, :]
            first = jnp.mean(scaled, axis=-1, keepdims=True)
            second = jnp.mean(scaled * hat, axis=-1, keepdims=True)
            result = inv * (scaled - first - hat * second)
            own_g[i : i + 16, :] = result
            store(i, result.astype(BF))

        return body

    quarter = width // KEYS

    def quarter_copy(layer, i):
        at = (k, k, lax.rem(k + 2, KEYS))[i]
        place = wo.at[layer, pl.ds(pl.multiple_of(at * quarter, quarter), quarter), :]
        return pltpu.make_async_remote_copy(
            src_ref=place, dst_ref=place, send_sem=wq_send.at[layer, i], recv_sem=wq_recv.at[layer, i],
            device_id=(across, sib, sib)[i], device_id_type=MESH,
        )

    def quarter_start(layer):
        quarter_copy(layer, 0).start()
        quarter_copy(layer, 1).start()

    def quarter_pass(layer):
        quarter_copy(layer, 0).wait_recv()
        quarter_copy(layer, 2).start()

    def quarter_got(layer):
        quarter_copy(layer, 1).wait_recv()
        quarter_copy(layer, 2).wait_recv()

    def go_copy(d, i):
        kt = lax.rem(k + d, KEYS)
        return pltpu.make_async_remote_copy(
            src_ref=go_all.at[i * sub : (i + 1) * sub, pl.ds(pl.multiple_of(kt * wide, wide), wide)],
            dst_ref=go.at[rows_at(k * own + i * sub, sub), :],
            send_sem=go_send.at[d, i], recv_sem=go_recv.at[d, i], device_id=(r, kt), device_id_type=MESH,
        )

    def go_leave(layer):
        def leave(i):
            at = slice(i * sub, (i + 1) * sub)
            go_all[at, :] = dot_nt(ga[at, :], wo[layer]).astype(BF)
            for d in (2, *range(1, KEYS, 2)):
                go_copy(d, i).start()
            go[rows_at(k * own + i * sub, sub), :] = go_all[at, columns]

        return leave

    def go_wait(d):
        for i in range(SUBS):
            go_copy(d, i).wait_recv()

    def weights_at(layer, point):
        for kind, p, distance in SCHEDULE.get((layer, point), ()):
            if kind == "along":
                issue(p)
            elif kind == "beside":
                beside_own(p)
            elif kind == "swap":
                swap(p)
            else:
                passes(p, distance - 1, (kind == "up",))

    def forward_layer(layer):
        base = 4 * layer
        rs_a, rs_f = ((RS_A0, RS_F0), (RS_A1, RS_F1))[layer]
        ag_m = (AG_M0, AG_M1)[layer]
        source = tokens if layer == 0 else full.at[AG_X1]
        here = functools.partial(weights_at, layer)
        here("start")
        arrive(base)
        if layer > 0:
            ag_near(AG_X1)
        project(layer, source, near)
        here("projected near")
        if layer == 0:
            for i in range(2):
                pre_own(i).wait()
                for d in range(1, KEYS):
                    pre_copy(i, d).wait_recv()
        if layer > 0:
            ag_far(AG_X1)
        project(layer, source, far)
        here("projected")
        attend(layer, block_b)
        here("attended b")
        arrive(base + 1)
        out_rows(layer, block_b * own, own)
        for i in range(SUBS):
            rs_copy(rs_a, i).start()
        here("out b")
        attend(layer, block_a)
        out_rows(layer, block_a * own, own)
        for i in range(SUBS):
            rs_mid(rs_a, i)
        here("out a")
        two(functools.partial(attend, layer), near)
        out_rows(layer, near * half, half)
        rs_near(rs_a)
        here("out near")
        rs_each(
            rs_a,
            norm_into(rs_a, own_x, layer, 0, g1, b1, own_m, ag_m),
            gather(ag_m),
            lambda i: here(f"norm {i}"),
        )
        here("normed")
        quarter_start(layer)
        arrive(base + 2)
        ag_near(ag_m)
        here("up")
        up_half(layer, ag_m, near)
        here("up near")
        ag_far(ag_m)
        up_half(layer, ag_m, far)
        here("up far")
        arrive(base + 3)
        here("down")
        scatter_far(
            rs_f,
            lambda i: dot_nt(both(hid, at=far_rows(i)), wd[layer]).astype(BF),
            lambda i: here(f"down {i}"),
        )
        part[half_rows(near), :] = dot_nt(hid[half_rows(near), :], wd[layer]).astype(BF)
        rs_near(rs_f)
        if layer == 0:
            quarter_pass(0)
        here("down near")

    forward_layer(0)
    rs_each(
        RS_F0,
        norm_into(RS_F0, own_m, 0, 1, g2, b2, own_x, AG_X1),
        gather(AG_X1),
        lambda i: weights_at(0, f"last norm {i}"),
    )
    forward_layer(1)

    def prefix_copy(layer, i, d):
        kt = lax.rem(k + d, KEYS)
        source = (gk, gv)[i]
        return pltpu.make_async_remote_copy(
            src_ref=source.at[pl.ds(pl.multiple_of(kt * count, count), count), :],
            dst_ref=pg.at[layer, i, :, columns],
            send_sem=pg_send.at[i, d], recv_sem=pg_recv.at[i, d],
            device_id=(r, kt), device_id_type=MESH,
        )

    def prefix_own(layer, i):
        return pltpu.make_async_copy(
            (gk, gv)[i].at[pl.ds(pl.multiple_of(k * count, count), count), :],
            pg.at[layer, i, :, columns],
            pg_recv.at[i, 0],
        )

    bits = rows.bit_length() - 1

    def row_copy(layer, b):
        bit = 1 << b
        partner = r + bit - 2 * bit * lax.rem(r // bit, 2)
        return pltpu.make_async_remote_copy(
            src_ref=pg_low.at[layer], dst_ref=pg_in.at[layer, b],
            send_sem=pgr_send.at[layer, b], recv_sem=pgr_recv.at[layer, b],
            device_id=(partner, k), device_id_type=MESH,
        )

    def row_start(layer, b):
        low = pg[layer].astype(BF)
        pg_low[layer] = low
        pg[layer] = low.astype(F32)
        row_copy(layer, b).start()

    def row_step(layer, b):
        row_copy(layer, b).wait()
        pg[layer] += pg_in[layer, b].astype(F32)
        if b + 1 < bits:
            row_start(layer, b + 1)

    def prefix_start(layer):
        for i in range(2):
            prefix_own(layer, i).start()
            for d in range(1, KEYS):
                prefix_copy(layer, i, d).start()

    def prefix_take(layer):
        for i in range(2):
            prefix_own(layer, i).wait()
            for d in range(1, KEYS):
                prefix_copy(layer, i, d).wait_recv()
        row_start(layer, 0)

    def prefix_sent(layer):
        for i in range(2):
            for d in range(1, KEYS):
                prefix_copy(layer, i, d).wait_send()

    for layer in reversed(range(LAYERS)):
        rs_gm, rs_gx = ((RS_GM0, RS_GX0), (RS_GM1, RS_GX1))[layer]
        ag_gf = (AG_GF0, AG_GF1)[layer]
        if layer == LAYERS - 1:
            forth = norm_into(RS_F1, own_m, 1, 1, g2, b2, own_x, AG_ACT)
            back = norm_back(lambda i: cot[i : i + 16, :].astype(F32), layer, 1, g2, into(ag_gf))

            def turn(i):
                forth(i)
                back(i)

            rs_each(RS_F1, turn, gather(ag_gf))
        else:
            rs_each(
                RS_GX1,
                norm_back(lambda i: own_g[i : i + 16, :] + rs_sum(RS_GX1, i), layer, 1, g2, into(ag_gf)),
                gather(ag_gf),
            )
            prefix_take(layer + 1)
        ag_near(ag_gf)
        part[half_rows(near), :] = ff_back(layer, full[ag_gf, half_rows(near), :], gelu_d[layer, half_rows(near), :])
        rs_near(rs_gm)

        def step(i):
            ag_pass(ag_gf, i)
            ag_got(ag_gf, i)
            at = far_rows(i)
            return ff_back(layer, both(full, ag_gf, at=at), both(gelu_d, layer, at=at))

        if layer == LAYERS - 1:
            quarter_pass(layer)
        scatter_far(rs_gm, step)
        if layer == 0:
            row_step(1, 0)
        gk[...] = jnp.zeros_like(gk)
        gv[...] = jnp.zeros_like(gv)
        quarter_got(layer)

        def keep(i, low):
            ga[i : i + 16, :] = low

        rs_each(
            rs_gm,
            norm_back(lambda i: own_g[i : i + 16, :] + rs_sum(rs_gm, i), layer, 0, g1, keep),
            go_leave(layer),
        )
        if layer == LAYERS - 1:
            for i in range(SUBS + 1):
                ag_copy(AG_ACT, i).start()
        go_wait(3 - 2 * c)
        two(functools.partial(attend_back, layer), near)
        if layer == 0:
            row_step(1, 1)
        go_wait(2)
        go_wait(1 + 2 * c)
        two(functools.partial(attend_back, layer), far)
        for d in range(1, KEYS):
            for i in range(SUBS):
                go_copy(d, i).wait_send()
        prefix_start(layer)

        def narrow(which):
            def body(i):
                i = which * half + i
                gqkv[rows_at(i, 16), wide : 2 * wide] = gk[rows_at(prefix + i, 16), :].astype(BF)
                gqkv[rows_at(i, 16), 2 * wide : 3 * wide] = gv[rows_at(prefix + i, 16), :].astype(BF)

            chunks(half, body)

        narrow(far)
        project_back(layer, block_b * own, own)
        for i in range(SUBS):
            rs_copy(rs_gx, i).start()
        project_back(layer, block_a * own, own)
        for i in range(SUBS):
            rs_mid(rs_gx, i)
        narrow(near)
        project_back(layer, near * half, half)
        rs_near(rs_gx)
        if layer == LAYERS - 1:
            ag_far(AG_ACT)
            ag_near(AG_ACT)
        else:
            for b in range(2, bits):
                row_step(1, b)
            prefix_take(0)
        prefix_sent(layer)

    act_copy = pltpu.make_async_copy(full.at[AG_ACT], low_out.at[1], loc.at[13])
    act_copy.start()

    def last(i):
        full[AG_GX, rows_at(k * own + i, 16), :] = (own_g[i : i + 16, :] + rs_sum(RS_GX0, i)).astype(BF)

    rs_each(RS_GX0, last, gather(AG_GX))
    for p in range(4 * LAYERS):
        drain(p)
    for i in range(2):
        for d in range(1, KEYS):
            pre_copy(i, d).wait_send()
    row_step(0, 0)
    ag_near(AG_GX)

    def grad_copy(which):
        return pltpu.make_async_copy(
            full.at[AG_GX, half_rows(which), :], low_out.at[0, half_rows(which), :], loc.at[14 + (which is far)]
        )

    grad_copy(near).start()
    ag_far(AG_GX)
    grad_copy(far).start()
    for b in range(1, bits):
        row_step(0, b)
    for i in range(2):
        for layer in range(LAYERS):
            prefix_out[i, layer] = pg[layer, i]
    ag_end(AG_GX)
    ag_end(AG_ACT)
    for layer in range(LAYERS):
        for i in range(3):
            quarter_copy(layer, i).wait_send()
    act_copy.wait()
    grad_copy(near).wait()
    grad_copy(far).wait()


def results(low, grads, act, gt, gpk, gpv, narrow, broad, act_held, grads_held, sems):
    parts, size = narrow.shape[:2]

    def taken(i):
        return pltpu.make_async_copy(low.at[0, i * size : (i + 1) * size, :], narrow.at[i], sems.at[0, i])

    def given(i):
        return pltpu.make_async_copy(broad.at[i], gt.at[0, i * size : (i + 1) * size, :], sems.at[1, i])

    in_act = pltpu.make_async_copy(low.at[1], act_held, sems.at[2, 0])
    out_act = pltpu.make_async_copy(act_held, act.at[0], sems.at[2, 0])
    in_grads = pltpu.make_async_copy(grads, grads_held, sems.at[2, 1])
    out_grads = [pltpu.make_async_copy(grads_held.at[i], (gpk, gpv)[i], sems.at[2, 2 + i]) for i in range(2)]
    for i in range(parts):
        taken(i).start()
    in_act.start()
    in_grads.start()
    for i in range(parts):
        taken(i).wait()
        broad[i] = narrow[i].astype(F32)
        given(i).start()
    in_act.wait()
    out_act.start()
    in_grads.wait()
    for copy in out_grads:
        copy.start()
    for i in range(parts):
        given(i).wait()
    out_act.wait()
    for copy in out_grads:
        copy.wait()


def per_device(
    tokens, cotangent, segment_ids, pad_mask, prefix_keys, prefix_values,
    w_query, w_key, w_value, w_out, w_up, w_down_t,
    norm1_gain, norm1_bias, norm2_gain, norm2_bias,
):
    rows, keys = lax.axis_size("rows"), lax.axis_size("keys")
    assert keys == KEYS and rows % (2 * KEYS) == 0 and rows & (rows - 1) == 0
    tok, width = tokens.shape[1:]
    count = prefix_keys.shape[1]
    prefix = count * keys
    local_ff = w_up.shape[2]
    wide, own, window = width // keys, tok // keys, 3 * tok // keys
    heads = wide // HEAD
    nz, bits, pieces = rows // 2, rows.bit_length() - 1, 4 * LAYERS
    vmem, anywhere = pl.BlockSpec(memory_space=pltpu.VMEM), pl.BlockSpec(memory_space=pl.ANY)
    dma = pltpu.SemaphoreType.DMA
    scratch = [
        pltpu.VMEM((LAYERS, width, 3 * wide), BF),
        pltpu.VMEM((LAYERS, width, width), BF),
        pltpu.VMEM((LAYERS, width, local_ff), BF),
        pltpu.VMEM((LAYERS, width, local_ff), BF),
        pltpu.VMEM((LAYERS, prefix, wide), BF),
        pltpu.VMEM((LAYERS, prefix, wide), BF),
        pltpu.VMEM((tok, width), BF),
        pltpu.VMEM((SCATTERS, 2, own, width), BF),
        pltpu.VMEM((SCATTERS, own, width), BF),
        pltpu.VMEM((own, width), BF),
        pltpu.VMEM((GATHERS, tok, width), BF),
        pltpu.VMEM((LAYERS, tok, 3 * wide), BF),
        pltpu.VMEM((LAYERS, keys, prefix + window, heads * own), F32),
        pltpu.VMEM((LAYERS, tok, local_ff), F32),
        pltpu.VMEM((2 * LAYERS, own, width), F32),
        pltpu.VMEM((2 * LAYERS, own, 1), F32),
        pltpu.VMEM((own, width), F32),
        pltpu.VMEM((own, width), F32),
        pltpu.VMEM((own, width), F32),
        pltpu.VMEM((own, width), BF),
        pltpu.VMEM((tok, wide), BF),
        pltpu.VMEM((tok, 3 * wide), BF),
        pltpu.VMEM((prefix + tok, wide), F32),
        pltpu.VMEM((prefix + tok, wide), F32),
        pltpu.VMEM((tok, local_ff), BF),
        pltpu.VMEM((own, width), BF),
        pltpu.VMEM((own, width), BF),
        pltpu.VMEM((tok, wide), BF),
        pltpu.VMEM((keys, window, own), F32),
        pltpu.VMEM((tok, own), F32),
        pltpu.VMEM((LAYERS, 2, count, width), F32),
        pltpu.VMEM((LAYERS, 2, count, width), BF),
        pltpu.VMEM((LAYERS, bits, 2, count, width), BF),
        dma((pieces, 2, nz + 1)),
        dma((pieces, 2, nz)),
        dma((pieces, nz)),
        dma((16,)),
        dma((2, keys)),
        dma((2, keys)),
        dma((LAYERS, 3)),
        dma((LAYERS, 3)),
        dma((keys, SUBS)),
        dma((keys, SUBS)),
        dma((2 * SUBS + 1,)),
        dma((2 * SUBS + 1,)),
        dma((2, 2 * SUBS + 1)),
        dma((2, 2 * SUBS + 1)),
        dma((2, keys)),
        dma((2, keys)),
        dma((LAYERS, bits)),
        dma((LAYERS, bits)),
    ]
    low, grads = pl.pallas_call(
        functools.partial(kernel, (rows, tok, width, local_ff)),
        out_shape=(
            jax.ShapeDtypeStruct((2, tok, width), BF),
            jax.ShapeDtypeStruct((2, LAYERS, count, width), F32),
        ),
        in_specs=[vmem, anywhere, vmem, vmem] + [anywhere] * 8 + [vmem] * 4,
        out_specs=(anywhere, vmem),
        scratch_shapes=scratch,
        compiler_params=pltpu.CompilerParams(
            collective_id=0, has_side_effects=True, vmem_limit_bytes=62 * 1024 * 1024 - 512 * 1024
        ),
    )(
        tokens[0], cotangent[0], segment_ids, pad_mask, prefix_keys, prefix_values,
        w_query, w_key, w_value, w_out, w_up, w_down_t,
        norm1_gain, norm1_bias, norm2_gain, norm2_bias,
    )
    whole = (LAYERS, count, width)
    return pl.pallas_call(
        results,
        out_shape=(
            jax.ShapeDtypeStruct((1, tok, width), BF),
            jax.ShapeDtypeStruct((1, tok, width), F32),
            jax.ShapeDtypeStruct(whole, F32),
            jax.ShapeDtypeStruct(whole, F32),
        ),
        in_specs=[anywhere] * 2,
        out_specs=(anywhere,) * 4,
        scratch_shapes=[
            pltpu.VMEM((keys, own, width), BF),
            pltpu.VMEM((keys, own, width), F32),
            pltpu.VMEM((tok, width), BF),
            pltpu.VMEM((2, *whole), F32),
            dma((3, keys)),
        ],
    )(low, grads)


def solution(mesh):
    row3 = P("rows", None, None)
    weight = P(None, "rows", None)
    return jax.shard_map(
        per_device,
        mesh=mesh,
        in_specs=(
            row3,
            row3,
            P("rows", None),
            P("rows", None),
            P(None, "keys", None),
            P(None, "keys", None),
            weight,
            weight,
            weight,
            weight,
            P(None, "rows", "keys"),
            P(None, "rows", "keys"),
            P(),
            P(),
            P(),
            P(),
        ),
        out_specs=(row3, row3, P(None, "keys", None), P(None, "keys", None)),
        check_vma=False,
    )
```

```python
import functools

import jax
import jax.numpy as jnp
from jax import lax
from jax.experimental import pallas as pl
from jax.experimental.pallas import tpu as pltpu
from jax.sharding import PartitionSpec as P

HEAD = 64
LAYERS = 2
KEYS = 4
EPSILON = 1e-05
NEGATIVE = -1000000000.0
MESH = pl.DeviceIdType.MESH
BF = jnp.bfloat16
F32 = jnp.float32

AG_M0, AG_X1, AG_M1, AG_GF1, AG_GF0, AG_GX, AG_ACT = range(7)
GATHERS = 7
RS_A0, RS_F0, RS_A1, RS_F1, RS_GM1, RS_GX1, RS_GM0, RS_GX0 = range(8)
SCATTERS = 8
GATHER_BEFORE = (None, AG_M0, AG_X1, AG_M1, AG_GF1, None, AG_GF0, None)
SUBS = 2

SCHEDULE = {
    (0, "start"): (
        ("beside", 1, 0),
        ("beside", 7, 0),
        ("along", 1, 0),
        ("beside", 2, 0),
        ("along", 0, 0),
        ("down", 1, 1),
        ("along", 4, 0),
        ("up", 1, 1),
        ("down", 0, 1),
        ("up", 0, 1),
        ("up", 1, 2),
        ("down", 1, 2),
        ("along", 2, 0),
        ("up", 0, 2),
        ("up", 1, 3),
        ("beside", 0, 0),
        ("down", 0, 2),
        ("up", 2, 1),
        ("down", 1, 3),
        ("down", 2, 1),
        ("up", 0, 3),
        ("along", 5, 0),
        ("up", 2, 2),
        ("down", 0, 3),
        ("along", 3, 0),
        ("down", 2, 2),
        ("up", 2, 3),
        ("down", 3, 1),
        ("down", 5, 1),
        ("up", 3, 1),
        ("up", 3, 2),
    ),
    (0, "attended b"): (
        ("up", 5, 2),
    ),
    (0, "out b"): (
        ("beside", 5, 0),
        ("up", 5, 1),
        ("along", 6, 0),
    ),
    (0, "out a"): (
        ("beside", 3, 0),
        ("down", 3, 2),
        ("down", 5, 2),
        ("down", 2, 3),
    ),
    (0, "norm 1"): (
        ("up", 4, 1),
        ("up", 3, 3),
        ("up", 4, 2),
        ("down", 4, 1),
    ),
    (0, "normed"): (
        ("up", 4, 3),
        ("swap", 7, 0),
    ),
    (0, "up"): (
        ("down", 3, 3),
        ("down", 4, 2),
    ),
    (0, "up far"): (
        ("along", 7, 0),
    ),
    (0, "down 0"): (
        ("beside", 4, 0),
        ("up", 6, 1),
    ),
    (0, "down 1"): (
        ("down", 5, 3),
        ("up", 5, 3),
    ),
    (0, "last norm 0"): (
        ("down", 4, 3),
        ("down", 6, 1),
    ),
    (0, "last norm 1"): (
        ("up", 6, 2),
        ("down", 6, 2),
    ),
    (1, "start"): (
        ("beside", 6, 0),
        ("down", 7, 1),
    ),
    (1, "projected near"): (
        ("up", 7, 1),
    ),
    (1, "out b"): (
        ("up", 6, 3),
    ),
    (1, "out a"): (
        ("down", 6, 3),
    ),
    (1, "norm 0"): (
        ("down", 7, 2),
    ),
    (1, "norm 1"): (
        ("up", 7, 2),
    ),
    (1, "up far"): (
        ("up", 7, 3),
        ("down", 7, 3),
    ),
}
STRAIGHT = (7,)


def dot_nn(a, b):
    return lax.dot_general(a, b, (((1,), (0,)), ((), ())), preferred_element_type=F32)


def dot_nt(a, b):
    return lax.dot_general(a, b, (((1,), (1,)), ((), ())), preferred_element_type=F32)


def dot_tn(a, b):
    return lax.dot_general(a, b, (((0,), (0,)), ((), ())), preferred_element_type=F32)


def kernel(
    dims,
    token_rows, cotangent, segments, padding, pre_k, pre_v,
    w_query, w_key, w_value, w_out, w_up, w_down,
    g1, b1, g2, b2,
    low_out, prefix_out,
    wqkv, wo, wu, wd, pk, pv,
    part, rc, ry, ys, full,
    qkv, prob, gelu_d, zhat, rinv,
    own_x, own_m, own_g, cot, att, gqkv, gk, gv, tokens, hid, ga, go_all, go, bias, codes,
    pg, pg_low, pg_in,
    w_send, w_recv, w_over, loc, pre_send, pre_recv,
    wq_send, wq_recv, go_send, go_recv,
    rs_send, rs_recv, ag_send, ag_recv, pg_send, pg_recv, pgr_send, pgr_recv,
):
    rows, tok, width, local_ff = dims
    nz = rows // 2
    wide = width // KEYS
    heads = wide // HEAD
    own = tok // KEYS
    half = tok // 2
    depth = width // rows
    count = pre_k.shape[1]
    prefix = KEYS * count
    window = 3 * own

    r = lax.axis_index("rows")
    k = lax.axis_index("keys")
    z, x = r // 2, lax.rem(r, 2)
    y, c = k // 2, lax.rem(k, 2)
    sib = (r, k + 1 - 2 * c)
    across = (r, lax.rem(k + 2, KEYS))
    beside = (r + 1 - 2 * x, k)
    far, near = 1 - y, y

    def level(d):
        return lax.rem(z + d, nz)

    barrier = pltpu.get_barrier_semaphore()

    def greet(d, carry):
        pl.semaphore_signal(barrier, inc=1, device_id=(level(d) * 2 + x, k), device_id_type=MESH)
        return carry

    lax.fori_loop(1, nz, greet, 0)
    pl.semaphore_signal(barrier, inc=1, device_id=beside, device_id_type=MESH)
    for d in range(1, KEYS):
        pl.semaphore_signal(barrier, inc=1, device_id=(r, lax.rem(k + d, KEYS)), device_id_type=MESH)

    group = nz // KEYS

    def spot(ref, layer, at):
        return ref.at[layer, pl.ds(pl.multiple_of(at * depth, depth), depth), :]

    def slot(p, zz, xx):
        layer, kind = divmod(p, 4)
        at = zz * 2 + xx
        return spot((wqkv, wo, wu, wd)[kind], layer, at)

    def active(p, zz):
        return None if p % 4 != 1 else (zz // group) == k

    def guarded(condition, action):
        if condition is None:
            action()
        else:
            pl.when(condition)(action)

    columns = pl.ds(pl.multiple_of(k * wide, wide), wide)

    def own_copies(p):
        layer, kind = divmod(p, 4)
        if kind == 0:
            place = pl.ds(pl.multiple_of(r * depth, depth), depth)
            return [
                pltpu.make_async_copy(
                    w.at[layer, :, columns], wqkv.at[layer, place, i * wide : (i + 1) * wide], loc.at[6 * layer + i]
                )
                for i, w in enumerate((w_query, w_key, w_value))
            ]
        source = (None, w_out, w_up, w_down)[kind]
        return [pltpu.make_async_copy(source.at[layer], slot(p, z, x), loc.at[6 * layer + 2 + kind])]

    def own_start(p):
        guarded(active(p, z), lambda: [copy.start() for copy in own_copies(p)] and None)

    def own_wait(p):
        guarded(active(p, z), lambda: [copy.wait() for copy in own_copies(p)] and None)

    def push(p, zz, xx, send_sem, target):
        place = slot(p, zz, xx)
        return pltpu.make_async_remote_copy(
            src_ref=place, dst_ref=place, send_sem=send_sem, recv_sem=w_recv.at[p, xx, zz],
            device_id=target, device_id_type=MESH,
        )

    def straight(p):
        return p in STRAIGHT

    def up(p, zz, xx):
        return push(p, zz, xx, w_send.at[p, xx, zz], (lax.rem(z + 1, nz) * 2 + x, k))

    def down(p, zz, xx):
        sem = w_send.at[p, xx, jnp.where(zz == z, nz, zz)]
        return push(p, zz, xx, sem, (lax.rem(z + nz - 1, nz) * 2 + x, k))

    def over(p, zz):
        return push(p, zz, x, w_over.at[p, zz], beside)

    not_top, not_bottom = z < nz - 1, z > 0

    def spread_own(p, xx, action):
        pl.when(not_top)(lambda: action(up(p, z, xx)))
        pl.when(not_bottom)(lambda: action(down(p, z, xx)))

    def begin(copy):
        copy.start()

    def sent(copy):
        copy.wait_send()

    def issue(p):
        guarded(active(p, z), lambda: spread_own(p, x, begin))

    def beside_own(p):
        guarded(active(p, z), lambda: over(p, z).start())

    def swap(p):
        over_in = push(p, z, 1 - x, w_over.at[p, z], beside)
        over_in.wait_recv()
        spread_own(p, 1 - x, begin)

    def hops(group, action, sides=(True, False)):
        bounds = [1 + (nz - 1) * i // 3 for i in range(4)]

        def one(j, carry):
            if True in sides:
                pl.when(z - j >= 0)(lambda: action(jnp.maximum(z - j, 0), True))
            if False in sides:
                pl.when(z + j < nz)(lambda: action(jnp.minimum(z + j, nz - 1), False))
            return carry

        lax.fori_loop(bounds[group], bounds[group + 1], one, 0)

    def onward(p, zz, xx, below, action):
        if below:
            pl.when(not_top)(lambda: action(up(p, zz, xx)))
        else:
            pl.when(not_bottom)(lambda: action(down(p, zz, xx)))

    def passes(p, group, sides):
        def action(zz, below):
            def take():
                for xx in (x, 1 - x) if straight(p) else (x,):
                    push(p, zz, xx, w_over.at[p, zz], beside).wait_recv()
                    onward(p, zz, xx, below, begin)
                if not straight(p):
                    over(p, zz).start()

            guarded(active(p, zz), take)

        hops(group, action, sides)

    def arrive(p):
        if straight(p):
            return

        def one(zz, carry):
            guarded(active(p, zz), push(p, zz, 1 - x, w_over.at[p, zz], beside).wait_recv)
            return carry

        lax.fori_loop(0, nz, one, 0)

    def drain(p):
        def mine():
            spread_own(p, x, sent)
            if straight(p):
                spread_own(p, 1 - x, sent)
            over(p, z).wait_send()

        guarded(active(p, z), mine)

        def action(zz, below):
            def passed():
                for xx in (x, 1 - x) if straight(p) else (x,):
                    onward(p, zz, xx, below, sent)
                if not straight(p):
                    over(p, zz).wait_send()

            guarded(active(p, zz), passed)

        for group_at in range(3):
            hops(group_at, action)

    def pre_copy(i, d):
        kt = lax.rem(k + d, KEYS)
        source, target = ((pre_k, pk), (pre_v, pv))[i]
        return pltpu.make_async_remote_copy(
            src_ref=source.at[:, :, pl.ds(pl.multiple_of(kt * wide, wide), wide)],
            dst_ref=target.at[:, pl.ds(pl.multiple_of(k * count, count), count), :],
            send_sem=pre_send.at[i, d], recv_sem=pre_recv.at[i, d], device_id=(r, kt), device_id_type=MESH,
        )

    def pre_own(i):
        source, target = ((pre_k, pk), (pre_v, pv))[i]
        return pltpu.make_async_copy(
            source.at[:, :, columns],
            target.at[:, pl.ds(pl.multiple_of(k * count, count), count), :],
            pre_recv.at[i, 0],
        )

    own_block = pl.ds(pl.multiple_of(k * own, own), own)
    cot_copy = pltpu.make_async_copy(cotangent.at[own_block, :], cot, loc.at[12])

    for p in range(4 * LAYERS):
        own_start(p)
    cot_copy.start()
    token_copy = pltpu.make_async_copy(token_rows, tokens, loc.at[13])
    token_copy.start()
    for i in range(2):
        pre_own(i).start()

    visible_code = jnp.where(padding[...] == 1, segments[...], -1).astype(F32)
    codes[...] = jnp.broadcast_to(visible_code, (own, tok)).T

    def mask_of(i, carry):
        queries = segments[:, pl.ds(pl.multiple_of(i * own, own), own)].astype(F32)
        keys_code = codes[pl.ds(pl.multiple_of(jnp.clip(i - 1, 0, KEYS - 3) * own, own), window), :]
        bias[i, 0:prefix, :] = jnp.zeros((prefix, own), F32)
        bias[i, prefix : prefix + window, :] = jnp.where(keys_code == queries, 0.0, NEGATIVE)
        return carry

    lax.fori_loop(0, KEYS, mask_of, 0)

    def widen(i, carry):
        at = pl.multiple_of(i * 16, 16)
        own_x[pl.ds(at, 16), :] = tokens[pl.ds(k * own + at, 16), :].astype(F32)
        return carry

    token_copy.wait()
    lax.fori_loop(0, own // 16, widen, 0)
    pl.semaphore_wait(barrier, nz - 1 + 1 + KEYS - 1)
    own_wait(0)
    for i in range(2):
        for d in range(1, KEYS):
            pre_copy(i, d).start()
    for p in range(1, 4 * LAYERS):
        own_wait(p)
    cot_copy.wait()

    sub = own // SUBS
    block_a, block_b = 2 * far + c, 2 * far + 1 - c

    def rows_at(at, size):
        return pl.ds(pl.multiple_of(at, 16), size)

    def rs_copy(n, i):
        if i < SUBS:
            source, target = part.at[rows_at(block_b * own + i * sub, sub), :], rc.at[n, 0, i * sub : (i + 1) * sub, :]
        elif i == SUBS:
            source, target = part.at[rows_at((2 * near + 1 - c) * own, own), :], rc.at[n, 1]
        else:
            at = slice((i - SUBS - 1) * sub, (i - SUBS) * sub)
            source, target = ys.at[at, :], ry.at[n, at, :]
        return pltpu.make_async_remote_copy(
            src_ref=source, dst_ref=target, send_sem=rs_send.at[i], recv_sem=rs_recv.at[i],
            device_id=sib if i <= SUBS else across, device_id_type=MESH,
        )

    def chunks(total, body, size=16):
        def one(i, carry):
            body(pl.multiple_of(i * size, size))
            return carry

        lax.fori_loop(0, total // size, one, 0)

    def rs_mid(n, i):
        rs_copy(n, i).wait_recv()
        for at in range(i * sub, (i + 1) * sub, 16):
            mine = part[rows_at(block_a * own + at, 16), :].astype(F32)
            ys[at : at + 16, :] = (mine + rc[n, 0, at : at + 16, :].astype(F32)).astype(BF)
        rs_copy(n, SUBS + 1 + i).start()

    def rs_near(n):
        rs_copy(n, SUBS).start()

    def rs_sum(n, at):
        mine = part[rows_at(k * own + at, 16), :].astype(F32) + rc[n, 1, at : at + 16, :].astype(F32)
        return mine + ry[n, at : at + 16, :].astype(F32)

    def rs_each(n, body, leave, between=lambda i: None):
        if GATHER_BEFORE[n] is not None:
            ag_end(GATHER_BEFORE[n])
        rs_copy(n, SUBS).wait_recv()
        for i in range(SUBS):
            between(i)
            rs_copy(n, SUBS + 1 + i).wait_recv()
            for at in range(i * sub, (i + 1) * sub, 16):
                body(at)
            leave(i)
        rs_end(n)

    def gather(n):
        def leave(i):
            ag_copy(n, i).start()
            if i == SUBS - 1:
                ag_copy(n, SUBS).start()

        return leave

    def rs_end(n):
        for i in range(2 * SUBS + 1):
            rs_copy(n, i).wait_send()

    def ag_copy(n, i):
        if i < SUBS:
            place, device = full.at[n, rows_at(k * own + i * sub, sub), :], across
        elif i == SUBS:
            place, device = full.at[n, rows_at(k * own, own), :], sib
        else:
            place, device = full.at[n, rows_at(block_a * own + (i - SUBS - 1) * sub, sub), :], sib
        return pltpu.make_async_remote_copy(
            src_ref=place, dst_ref=place, send_sem=ag_send.at[n // AG_ACT, i], recv_sem=ag_recv.at[n // AG_ACT, i],
            device_id=device, device_id_type=MESH,
        )

    def ag_end(n):
        for i in range(2 * SUBS + 1):
            ag_copy(n, i).wait_send()

    def ag_near(n):
        ag_copy(n, SUBS).wait_recv()

    def ag_pass(n, i):
        ag_copy(n, i).wait_recv()
        ag_copy(n, SUBS + 1 + i).start()

    def ag_got(n, i):
        ag_copy(n, SUBS + 1 + i).wait_recv()

    def ag_far(n):
        for i in range(SUBS):
            ag_pass(n, i)
        for i in range(SUBS):
            ag_got(n, i)

    def half_rows(which):
        return pl.ds(pl.multiple_of(which * half, half), half)

    def far_rows(i):
        return rows_at(block_a * own + i * sub, sub), rows_at(block_b * own + i * sub, sub)

    def both(ref, *lead, at):
        return jnp.concatenate([ref[(*lead, rows, slice(None))] for rows in at], axis=0)

    def project(layer, source, which):
        hr = half_rows(which)
        xin = source[hr, :]
        for i in range(3):
            at = slice(i * wide, (i + 1) * wide)
            val = dot_nn(xin, wqkv[layer, :, at])
            qkv[layer, hr, at] = (val * HEAD**-0.5 if i == 0 else val).astype(BF)

    lane_head = lax.broadcasted_iota(jnp.int32, (1, wide), 1) // HEAD
    masks = [jnp.where(lane_head == h, 1.0, 0.0).astype(BF) for h in range(heads)]

    def stacked(value):
        return jnp.concatenate([value * mask for mask in masks], axis=0)

    def place_of(i):
        return pl.multiple_of(i * own, own)

    def window_of(i):
        return pl.multiple_of(jnp.clip(i - 1, 0, KEYS - 3) * own, own)

    def unstacked(value):
        parts = [value[h * HEAD : (h + 1) * HEAD, h * own : (h + 1) * own] for h in range(heads)]
        return jnp.concatenate(parts, axis=0).T

    def seen(layer, start):
        span = pl.ds(start, window)
        return (
            jnp.concatenate([pk[layer], qkv[layer, span, wide : 2 * wide]], axis=0),
            jnp.concatenate([pv[layer], qkv[layer, span, 2 * wide : 3 * wide]], axis=0),
        )

    def attend(layer, i):
        q4 = stacked(qkv[layer, pl.ds(place_of(i), own), 0:wide])
        key_rows, value_rows = seen(layer, window_of(i))
        s = dot_nt(key_rows, q4) + jnp.concatenate([bias[i]] * heads, axis=1)
        e = jnp.exp(s - jnp.max(s, axis=0, keepdims=True))
        p = e * (1.0 / jnp.sum(e, axis=0, keepdims=True))
        prob[layer, i] = p
        att[pl.ds(place_of(i), own), :] = unstacked(dot_tn(value_rows, p.astype(BF))).astype(BF)

    def attend_back(layer, i):
        at = pl.ds(place_of(i), own)
        q4 = stacked(qkv[layer, at, 0:wide])
        go4 = stacked(go[at, :])
        start = window_of(i)
        key_rows, value_rows = seen(layer, start)
        p = prob[layer, i]
        gp = dot_nt(value_rows, go4)
        dsum = jnp.sum(p * gp, axis=0, keepdims=True)
        gs = (p * (gp - dsum)).astype(BF)
        places = pl.ds(prefix + start, window)
        gk_here, gv_here = dot_nn(gs, q4), dot_nn(p.astype(BF), go4)
        gk[0:prefix, :] += gk_here[:prefix]
        gk[places, :] += gk_here[prefix:]
        gv[0:prefix, :] += gv_here[:prefix]
        gv[places, :] += gv_here[prefix:]
        gqkv[at, 0:wide] = (unstacked(dot_tn(key_rows, gs)).astype(BF).astype(F32) * HEAD**-0.5).astype(BF)

    def two(body, which):
        def one(i, carry):
            body(2 * which + i)
            return carry

        lax.fori_loop(0, 2, one, 0)

    def out_rows(layer, at, size):
        rows_here = rows_at(at, size)
        part[rows_here, :] = dot_nn(att[rows_here, :], wo[layer, columns, :]).astype(BF)

    def up_half(layer, n, which):
        hr = half_rows(which)
        u = dot_nn(full[n, hr, :], wu[layer])
        for at in range(0, half, 16):
            v = u[at : at + 16]
            phi_sum = 0.5 * (1.0 + lax.erf(v * 0.7071067811865476))
            density = jnp.exp(v * v * -0.5) * 0.3989422804014327
            here = rows_at(which * half + at, 16)
            hid[here, :] = (v * phi_sum).astype(BF)
            gelu_d[layer, here, :] = phi_sum + v * density

    def ff_back(layer, gradient, slope):
        gu = (dot_nn(gradient, wd[layer]) * slope).astype(BF)
        return dot_nt(gu, wu[layer]).astype(BF)

    def scatter_far(n, step, before=lambda i: None, early=False):
        for i in range(SUBS):
            before(i)
            if early and i > 0:
                rs_mid(n, i - 1)
            value = step(i)
            at_a, at_b = far_rows(i)
            part[at_b, :] = value[sub:]
            rs_copy(n, i).start()
            part[at_a, :] = value[:sub]
            if not early and i > 0:
                rs_mid(n, i - 1)
        rs_mid(n, SUBS - 1)

    def project_back(layer, at, size):
        rows_here = rows_at(at, size)
        part[rows_here, :] = dot_nt(gqkv[rows_here, :], wqkv[layer]).astype(BF)

    def norm_into(n, residual, layer, which, gain, shift, result, target):
        index = 2 * layer + which
        g, b = gain[layer : layer + 1, :], shift[layer : layer + 1, :]

        def body(i):
            value = residual[i : i + 16, :] + rs_sum(n, i)
            centre = value - jnp.mean(value, axis=-1, keepdims=True)
            inv = lax.rsqrt(jnp.mean(centre * centre, axis=-1, keepdims=True) + EPSILON)
            hat = centre * inv
            done = hat * g + b
            zhat[index, i : i + 16, :] = hat
            rinv[index, i : i + 16, :] = inv
            result[i : i + 16, :] = done
            full[target, rows_at(k * own + i, 16), :] = done.astype(BF)

        return body

    def into(n):
        def store(i, low):
            full[n, rows_at(k * own + i, 16), :] = low

        return store

    def norm_back(read, layer, which, gain, store):
        index = 2 * layer + which
        g = gain[layer : layer + 1, :]

        def body(i):
            scaled = read(i) * g
            hat = zhat[index, i : i + 16, :]
            inv = rinv[index, i : i + 16, :]
            first = jnp.mean(scaled, axis=-1, keepdims=True)
            second = jnp.mean(scaled * hat, axis=-1, keepdims=True)
            result = inv * (scaled - first - hat * second)
            own_g[i : i + 16, :] = result
            store(i, result.astype(BF))

        return body

    quarter = width // KEYS

    def quarter_copy(layer, i):
        at = (k, k, lax.rem(k + 2, KEYS))[i]
        place = wo.at[layer, pl.ds(pl.multiple_of(at * quarter, quarter), quarter), :]
        return pltpu.make_async_remote_copy(
            src_ref=place, dst_ref=place, send_sem=wq_send.at[layer, i], recv_sem=wq_recv.at[layer, i],
            device_id=(across, sib, sib)[i], device_id_type=MESH,
        )

    def quarter_start(layer):
        quarter_copy(layer, 0).start()
        quarter_copy(layer, 1).start()

    def quarter_pass(layer):
        quarter_copy(layer, 0).wait_recv()
        quarter_copy(layer, 2).start()

    def quarter_got(layer):
        quarter_copy(layer, 1).wait_recv()
        quarter_copy(layer, 2).wait_recv()

    def go_copy(d, i):
        kt = lax.rem(k + d, KEYS)
        return pltpu.make_async_remote_copy(
            src_ref=go_all.at[i * sub : (i + 1) * sub, pl.ds(pl.multiple_of(kt * wide, wide), wide)],
            dst_ref=go.at[rows_at(k * own + i * sub, sub), :],
            send_sem=go_send.at[d, i], recv_sem=go_recv.at[d, i], device_id=(r, kt), device_id_type=MESH,
        )

    def go_leave(layer):
        def leave(i):
            at = slice(i * sub, (i + 1) * sub)
            go_all[at, :] = dot_nt(ga[at, :], wo[layer]).astype(BF)
            for d in (2, *range(1, KEYS, 2)):
                go_copy(d, i).start()
            go[rows_at(k * own + i * sub, sub), :] = go_all[at, columns]

        return leave

    def go_wait(d):
        for i in range(SUBS):
            go_copy(d, i).wait_recv()

    def weights_at(layer, point):
        for kind, p, distance in SCHEDULE.get((layer, point), ()):
            if kind == "along":
                issue(p)
            elif kind == "beside":
                beside_own(p)
            elif kind == "swap":
                swap(p)
            else:
                passes(p, distance - 1, (kind == "up",))

    def forward_layer(layer):
        base = 4 * layer
        rs_a, rs_f = ((RS_A0, RS_F0), (RS_A1, RS_F1))[layer]
        ag_m = (AG_M0, AG_M1)[layer]
        source = tokens if layer == 0 else full.at[AG_X1]
        here = functools.partial(weights_at, layer)
        here("start")
        arrive(base)
        if layer > 0:
            ag_near(AG_X1)
        project(layer, source, near)
        here("projected near")
        if layer == 0:
            for i in range(2):
                pre_own(i).wait()
                for d in range(1, KEYS):
                    pre_copy(i, d).wait_recv()
        if layer > 0:
            ag_far(AG_X1)
        project(layer, source, far)
        here("projected")
        attend(layer, block_b)
        here("attended b")
        arrive(base + 1)
        out_rows(layer, block_b * own, own)
        for i in range(SUBS):
            rs_copy(rs_a, i).start()
        here("out b")
        attend(layer, block_a)
        out_rows(layer, block_a * own, own)
        for i in range(SUBS):
            rs_mid(rs_a, i)
        here("out a")
        two(functools.partial(attend, layer), near)
        out_rows(layer, near * half, half)
        rs_near(rs_a)
        here("out near")
        rs_each(
            rs_a,
            norm_into(rs_a, own_x, layer, 0, g1, b1, own_m, ag_m),
            gather(ag_m),
            lambda i: here(f"norm {i}"),
        )
        here("normed")
        quarter_start(layer)
        arrive(base + 2)
        ag_near(ag_m)
        here("up")
        up_half(layer, ag_m, near)
        here("up near")
        ag_far(ag_m)
        up_half(layer, ag_m, far)
        here("up far")
        arrive(base + 3)
        here("down")
        scatter_far(
            rs_f,
            lambda i: dot_nt(both(hid, at=far_rows(i)), wd[layer]).astype(BF),
            lambda i: here(f"down {i}"),
        )
        part[half_rows(near), :] = dot_nt(hid[half_rows(near), :], wd[layer]).astype(BF)
        rs_near(rs_f)
        if layer == 0:
            quarter_pass(0)
        here("down near")

    forward_layer(0)
    rs_each(
        RS_F0,
        norm_into(RS_F0, own_m, 0, 1, g2, b2, own_x, AG_X1),
        gather(AG_X1),
        lambda i: weights_at(0, f"last norm {i}"),
    )
    forward_layer(1)

    def prefix_copy(layer, i, d):
        kt = lax.rem(k + d, KEYS)
        source = (gk, gv)[i]
        return pltpu.make_async_remote_copy(
            src_ref=source.at[pl.ds(pl.multiple_of(kt * count, count), count), :],
            dst_ref=pg.at[layer, i, :, columns],
            send_sem=pg_send.at[i, d], recv_sem=pg_recv.at[i, d],
            device_id=(r, kt), device_id_type=MESH,
        )

    def prefix_own(layer, i):
        return pltpu.make_async_copy(
            (gk, gv)[i].at[pl.ds(pl.multiple_of(k * count, count), count), :],
            pg.at[layer, i, :, columns],
            pg_recv.at[i, 0],
        )

    bits = rows.bit_length() - 1

    def row_copy(layer, b):
        bit = 1 << b
        partner = r + bit - 2 * bit * lax.rem(r // bit, 2)
        return pltpu.make_async_remote_copy(
            src_ref=pg_low.at[layer], dst_ref=pg_in.at[layer, b],
            send_sem=pgr_send.at[layer, b], recv_sem=pgr_recv.at[layer, b],
            device_id=(partner, k), device_id_type=MESH,
        )

    def row_start(layer, b):
        low = pg[layer].astype(BF)
        pg_low[layer] = low
        pg[layer] = low.astype(F32)
        row_copy(layer, b).start()

    def row_step(layer, b):
        row_copy(layer, b).wait()
        pg[layer] += pg_in[layer, b].astype(F32)
        if b + 1 < bits:
            row_start(layer, b + 1)

    def prefix_start(layer):
        for i in range(2):
            prefix_own(layer, i).start()
            for d in range(1, KEYS):
                prefix_copy(layer, i, d).start()

    def prefix_take(layer):
        for i in range(2):
            prefix_own(layer, i).wait()
            for d in range(1, KEYS):
                prefix_copy(layer, i, d).wait_recv()
        row_start(layer, 0)

    def prefix_sent(layer):
        for i in range(2):
            for d in range(1, KEYS):
                prefix_copy(layer, i, d).wait_send()

    for layer in reversed(range(LAYERS)):
        rs_gm, rs_gx = ((RS_GM0, RS_GX0), (RS_GM1, RS_GX1))[layer]
        ag_gf = (AG_GF0, AG_GF1)[layer]
        if layer == LAYERS - 1:
            forth = norm_into(RS_F1, own_m, 1, 1, g2, b2, own_x, AG_ACT)
            back = norm_back(lambda i: cot[i : i + 16, :].astype(F32), layer, 1, g2, into(ag_gf))

            def turn(i):
                forth(i)
                back(i)

            rs_each(RS_F1, turn, gather(ag_gf))
        else:
            rs_each(
                RS_GX1,
                norm_back(lambda i: own_g[i : i + 16, :] + rs_sum(RS_GX1, i), layer, 1, g2, into(ag_gf)),
                gather(ag_gf),
            )
            prefix_take(layer + 1)
        ag_near(ag_gf)
        part[half_rows(near), :] = ff_back(layer, full[ag_gf, half_rows(near), :], gelu_d[layer, half_rows(near), :])
        rs_near(rs_gm)

        def step(i):
            ag_got(ag_gf, i)
            at = far_rows(i)
            return ff_back(layer, both(full, ag_gf, at=at), both(gelu_d, layer, at=at))

        if layer == LAYERS - 1:
            quarter_pass(layer)
        scatter_far(rs_gm, step, lambda i: ag_pass(ag_gf, i), early=True)
        if layer == 0:
            row_step(1, 0)
        gk[...] = jnp.zeros_like(gk)
        gv[...] = jnp.zeros_like(gv)
        quarter_got(layer)

        def keep(i, low):
            ga[i : i + 16, :] = low

        rs_each(
            rs_gm,
            norm_back(lambda i: own_g[i : i + 16, :] + rs_sum(rs_gm, i), layer, 0, g1, keep),
            go_leave(layer),
        )
        if layer == LAYERS - 1:
            for i in range(SUBS + 1):
                ag_copy(AG_ACT, i).start()
        go_wait(3 - 2 * c)
        two(functools.partial(attend_back, layer), near)
        if layer == 0:
            row_step(1, 1)
        go_wait(2)
        go_wait(1 + 2 * c)
        two(functools.partial(attend_back, layer), far)
        for d in range(1, KEYS):
            for i in range(SUBS):
                go_copy(d, i).wait_send()
        prefix_start(layer)

        def narrow(which):
            def body(i):
                i = which * half + i
                gqkv[rows_at(i, 16), wide : 2 * wide] = gk[rows_at(prefix + i, 16), :].astype(BF)
                gqkv[rows_at(i, 16), 2 * wide : 3 * wide] = gv[rows_at(prefix + i, 16), :].astype(BF)

            chunks(half, body)

        narrow(far)
        project_back(layer, block_b * own, own)
        for i in range(SUBS):
            rs_copy(rs_gx, i).start()
        project_back(layer, block_a * own, own)
        for i in range(SUBS):
            rs_mid(rs_gx, i)
        narrow(near)
        project_back(layer, near * half, half)
        rs_near(rs_gx)
        if layer == LAYERS - 1:
            ag_far(AG_ACT)
            ag_near(AG_ACT)
        else:
            for b in range(2, bits):
                row_step(1, b)
            prefix_take(0)
        prefix_sent(layer)

    act_copy = pltpu.make_async_copy(full.at[AG_ACT], low_out.at[1], loc.at[13])
    act_copy.start()

    def last(i):
        full[AG_GX, rows_at(k * own + i, 16), :] = (own_g[i : i + 16, :] + rs_sum(RS_GX0, i)).astype(BF)

    rs_each(RS_GX0, last, gather(AG_GX), lambda i: row_step(0, 0) if i == SUBS - 1 else None)
    for p in range(4 * LAYERS):
        drain(p)
    for i in range(2):
        for d in range(1, KEYS):
            pre_copy(i, d).wait_send()
    ag_near(AG_GX)

    def grad_copy(which):
        return pltpu.make_async_copy(
            full.at[AG_GX, half_rows(which), :], low_out.at[0, half_rows(which), :], loc.at[14 + (which is far)]
        )

    grad_copy(near).start()
    ag_far(AG_GX)
    grad_copy(far).start()
    for b in range(1, bits):
        row_step(0, b)
    for i in range(2):
        for layer in range(LAYERS):
            prefix_out[i, layer] = pg[layer, i]
    ag_end(AG_GX)
    ag_end(AG_ACT)
    for layer in range(LAYERS):
        for i in range(3):
            quarter_copy(layer, i).wait_send()
    act_copy.wait()
    grad_copy(near).wait()
    grad_copy(far).wait()


def results(low, grads, act, gt, gpk, gpv, narrow, broad, act_held, grads_held, sems):
    parts, size = narrow.shape[:2]

    def taken(i):
        return pltpu.make_async_copy(low.at[0, i * size : (i + 1) * size, :], narrow.at[i], sems.at[0, i])

    def given(i):
        return pltpu.make_async_copy(broad.at[i], gt.at[0, i * size : (i + 1) * size, :], sems.at[1, i])

    in_act = pltpu.make_async_copy(low.at[1], act_held, sems.at[2, 0])
    out_act = pltpu.make_async_copy(act_held, act.at[0], sems.at[2, 0])
    in_grads = pltpu.make_async_copy(grads, grads_held, sems.at[2, 1])
    out_grads = [pltpu.make_async_copy(grads_held.at[i], (gpk, gpv)[i], sems.at[2, 2 + i]) for i in range(2)]
    for i in range(parts):
        taken(i).start()
    in_act.start()
    in_grads.start()
    for i in range(parts):
        taken(i).wait()
        broad[i] = narrow[i].astype(F32)
        given(i).start()
    in_act.wait()
    out_act.start()
    in_grads.wait()
    for copy in out_grads:
        copy.start()
    for i in range(parts):
        given(i).wait()
    out_act.wait()
    for copy in out_grads:
        copy.wait()


def per_device(
    tokens, cotangent, segment_ids, pad_mask, prefix_keys, prefix_values,
    w_query, w_key, w_value, w_out, w_up, w_down_t,
    norm1_gain, norm1_bias, norm2_gain, norm2_bias,
):
    rows, keys = lax.axis_size("rows"), lax.axis_size("keys")
    assert keys == KEYS and rows % (2 * KEYS) == 0 and rows & (rows - 1) == 0
    tok, width = tokens.shape[1:]
    count = prefix_keys.shape[1]
    prefix = count * keys
    local_ff = w_up.shape[2]
    wide, own, window = width // keys, tok // keys, 3 * tok // keys
    heads = wide // HEAD
    nz, bits, pieces = rows // 2, rows.bit_length() - 1, 4 * LAYERS
    vmem, anywhere = pl.BlockSpec(memory_space=pltpu.VMEM), pl.BlockSpec(memory_space=pl.ANY)
    dma = pltpu.SemaphoreType.DMA
    scratch = [
        pltpu.VMEM((LAYERS, width, 3 * wide), BF),
        pltpu.VMEM((LAYERS, width, width), BF),
        pltpu.VMEM((LAYERS, width, local_ff), BF),
        pltpu.VMEM((LAYERS, width, local_ff), BF),
        pltpu.VMEM((LAYERS, prefix, wide), BF),
        pltpu.VMEM((LAYERS, prefix, wide), BF),
        pltpu.VMEM((tok, width), BF),
        pltpu.VMEM((SCATTERS, 2, own, width), BF),
        pltpu.VMEM((SCATTERS, own, width), BF),
        pltpu.VMEM((own, width), BF),
        pltpu.VMEM((GATHERS, tok, width), BF),
        pltpu.VMEM((LAYERS, tok, 3 * wide), BF),
        pltpu.VMEM((LAYERS, keys, prefix + window, heads * own), F32),
        pltpu.VMEM((LAYERS, tok, local_ff), F32),
        pltpu.VMEM((2 * LAYERS, own, width), F32),
        pltpu.VMEM((2 * LAYERS, own, 1), F32),
        pltpu.VMEM((own, width), F32),
        pltpu.VMEM((own, width), F32),
        pltpu.VMEM((own, width), F32),
        pltpu.VMEM((own, width), BF),
        pltpu.VMEM((tok, wide), BF),
        pltpu.VMEM((tok, 3 * wide), BF),
        pltpu.VMEM((prefix + tok, wide), F32),
        pltpu.VMEM((prefix + tok, wide), F32),
        pltpu.VMEM((tok, width), BF),
        pltpu.VMEM((tok, local_ff), BF),
        pltpu.VMEM((own, width), BF),
        pltpu.VMEM((own, width), BF),
        pltpu.VMEM((tok, wide), BF),
        pltpu.VMEM((keys, prefix + window, own), F32),
        pltpu.VMEM((tok, own), F32),
        pltpu.VMEM((LAYERS, 2, count, width), F32),
        pltpu.VMEM((LAYERS, 2, count, width), BF),
        pltpu.VMEM((LAYERS, bits, 2, count, width), BF),
        dma((pieces, 2, nz + 1)),
        dma((pieces, 2, nz)),
        dma((pieces, nz)),
        dma((16,)),
        dma((2, keys)),
        dma((2, keys)),
        dma((LAYERS, 3)),
        dma((LAYERS, 3)),
        dma((keys, SUBS)),
        dma((keys, SUBS)),
        dma((2 * SUBS + 1,)),
        dma((2 * SUBS + 1,)),
        dma((2, 2 * SUBS + 1)),
        dma((2, 2 * SUBS + 1)),
        dma((2, keys)),
        dma((2, keys)),
        dma((LAYERS, bits)),
        dma((LAYERS, bits)),
    ]
    low, grads = pl.pallas_call(
        functools.partial(kernel, (rows, tok, width, local_ff)),
        out_shape=(
            jax.ShapeDtypeStruct((2, tok, width), BF),
            jax.ShapeDtypeStruct((2, LAYERS, count, width), F32),
        ),
        in_specs=[anywhere, anywhere, vmem, vmem] + [anywhere] * 8 + [vmem] * 4,
        out_specs=(anywhere, vmem),
        scratch_shapes=scratch,
        compiler_params=pltpu.CompilerParams(
            collective_id=0, has_side_effects=True, vmem_limit_bytes=62 * 1024 * 1024 - 512 * 1024
        ),
    )(
        tokens[0], cotangent[0], segment_ids, pad_mask, prefix_keys, prefix_values,
        w_query, w_key, w_value, w_out, w_up, w_down_t,
        norm1_gain, norm1_bias, norm2_gain, norm2_bias,
    )
    whole = (LAYERS, count, width)
    return pl.pallas_call(
        results,
        out_shape=(
            jax.ShapeDtypeStruct((1, tok, width), BF),
            jax.ShapeDtypeStruct((1, tok, width), F32),
            jax.ShapeDtypeStruct(whole, F32),
            jax.ShapeDtypeStruct(whole, F32),
        ),
        in_specs=[anywhere] * 2,
        out_specs=(anywhere,) * 4,
        scratch_shapes=[
            pltpu.VMEM((keys, own, width), BF),
            pltpu.VMEM((keys, own, width), F32),
            pltpu.VMEM((tok, width), BF),
            pltpu.VMEM((2, *whole), F32),
            dma((3, keys)),
        ],
    )(low, grads)


def solution(mesh):
    row3 = P("rows", None, None)
    weight = P(None, "rows", None)
    return jax.shard_map(
        per_device,
        mesh=mesh,
        in_specs=(
            row3,
            row3,
            P("rows", None),
            P("rows", None),
            P(None, "keys", None),
            P(None, "keys", None),
            weight,
            weight,
            weight,
            weight,
            P(None, "rows", "keys"),
            P(None, "rows", "keys"),
            P(),
            P(),
            P(),
            P(),
        ),
        out_specs=(row3, row3, P(None, "keys", None), P(None, "keys", None)),
        check_vma=False,
    )
```

```python
import functools

import jax
import jax.numpy as jnp
from jax import lax
from jax.experimental import pallas as pl
from jax.experimental.pallas import tpu as pltpu
from jax.sharding import PartitionSpec as P

HEAD = 64
LAYERS = 2
KEYS = 4
EPSILON = 1e-05
NEGATIVE = -1000000000.0
MESH = pl.DeviceIdType.MESH
BF = jnp.bfloat16
F32 = jnp.float32

AG_M0, AG_X1, AG_M1, AG_GF1, AG_GF0, AG_GX, AG_ACT = range(7)
GATHERS = 7
RS_A0, RS_F0, RS_A1, RS_F1, RS_GM1, RS_GX1, RS_GM0, RS_GX0 = range(8)
SCATTERS = 8
GATHER_BEFORE = (None, AG_M0, AG_X1, AG_M1, AG_GF1, None, AG_GF0, None)
SUBS = 2

SCHEDULE = {
    (0, "start"): (
        ("beside", 1, 0),
        ("beside", 7, 0),
        ("along", 1, 0),
        ("beside", 2, 0),
        ("along", 0, 0),
        ("down", 1, 1),
        ("along", 4, 0),
        ("up", 1, 1),
        ("down", 0, 1),
        ("up", 0, 1),
        ("up", 1, 2),
        ("down", 1, 2),
        ("along", 2, 0),
        ("up", 0, 2),
        ("up", 1, 3),
        ("beside", 0, 0),
        ("down", 0, 2),
        ("up", 2, 1),
        ("down", 1, 3),
        ("down", 2, 1),
        ("up", 0, 3),
        ("along", 5, 0),
        ("up", 2, 2),
        ("down", 0, 3),
        ("along", 3, 0),
        ("down", 2, 2),
        ("up", 2, 3),
        ("down", 3, 1),
        ("down", 5, 1),
        ("up", 3, 1),
        ("up", 3, 2),
    ),
    (0, "attended b"): (
        ("up", 5, 2),
    ),
    (0, "out b"): (
        ("beside", 5, 0),
        ("up", 5, 1),
        ("along", 6, 0),
    ),
    (0, "out a"): (
        ("beside", 3, 0),
        ("down", 3, 2),
        ("down", 5, 2),
        ("down", 2, 3),
    ),
    (0, "norm 1"): (
        ("up", 4, 1),
        ("up", 3, 3),
        ("up", 4, 2),
        ("down", 4, 1),
    ),
    (0, "normed"): (
        ("up", 4, 3),
        ("swap", 7, 0),
    ),
    (0, "up"): (
        ("down", 3, 3),
        ("down", 4, 2),
    ),
    (0, "up far"): (
        ("along", 7, 0),
    ),
    (0, "down 0"): (
        ("beside", 4, 0),
        ("up", 6, 1),
    ),
    (0, "down 1"): (
        ("down", 5, 3),
        ("up", 5, 3),
    ),
    (0, "last norm 0"): (
        ("down", 4, 3),
        ("down", 6, 1),
    ),
    (0, "last norm 1"): (
        ("up", 6, 2),
        ("down", 6, 2),
    ),
    (1, "start"): (
        ("beside", 6, 0),
        ("down", 7, 1),
    ),
    (1, "projected near"): (
        ("up", 7, 1),
    ),
    (1, "out b"): (
        ("up", 6, 3),
    ),
    (1, "out a"): (
        ("down", 6, 3),
    ),
    (1, "norm 0"): (
        ("down", 7, 2),
    ),
    (1, "norm 1"): (
        ("up", 7, 2),
    ),
    (1, "up far"): (
        ("up", 7, 3),
        ("down", 7, 3),
    ),
}
STRAIGHT = (7,)


def dot_nn(a, b):
    return lax.dot_general(a, b, (((1,), (0,)), ((), ())), preferred_element_type=F32)


def dot_nt(a, b):
    return lax.dot_general(a, b, (((1,), (1,)), ((), ())), preferred_element_type=F32)


def dot_tn(a, b):
    return lax.dot_general(a, b, (((0,), (0,)), ((), ())), preferred_element_type=F32)


def kernel(
    dims,
    token_rows, cotangent, segments, padding, pre_k, pre_v,
    w_query, w_key, w_value, w_out, w_up, w_down,
    g1, b1, g2, b2,
    low_out, prefix_out,
    wqkv, wo, wu, wd, pk, pv,
    part, rc, ry, ys, full,
    qkv, prob, gelu_d, zhat, rinv,
    own_x, own_m, own_g, cot, att, gqkv, gk, gv, tokens, hid, ga, go_all, go, bias, codes,
    pg, pg_low, pg_in,
    w_send, w_recv, w_over, loc, pre_send, pre_recv,
    wq_send, wq_recv, go_send, go_recv,
    rs_send, rs_recv, ag_send, ag_recv, pg_send, pg_recv, pgr_send, pgr_recv,
):
    rows, tok, width, local_ff = dims
    nz = rows // 2
    wide = width // KEYS
    heads = wide // HEAD
    own = tok // KEYS
    half = tok // 2
    depth = width // rows
    count = pre_k.shape[1]
    prefix = KEYS * count
    window = 3 * own

    r = lax.axis_index("rows")
    k = lax.axis_index("keys")
    z, x = r // 2, lax.rem(r, 2)
    y, c = k // 2, lax.rem(k, 2)
    sib = (r, k + 1 - 2 * c)
    across = (r, lax.rem(k + 2, KEYS))
    beside = (r + 1 - 2 * x, k)
    far, near = 1 - y, y

    barrier = pltpu.get_barrier_semaphore()

    def greet(zz):
        pl.semaphore_signal(barrier, inc=1, device_id=(zz * 2 + x, k), device_id_type=MESH)

    not_top, not_bottom = z < nz - 1, z > 0
    pl.when(not_top)(lambda: greet(lax.rem(z + 1, nz)))
    pl.when(not_bottom)(lambda: greet(lax.rem(z + nz - 1, nz)))
    far_partners = [1 << b for b in range(1, nz.bit_length() - 1)]
    for bit in far_partners:
        greet(z + bit - 2 * bit * lax.rem(z // bit, 2))
    pl.semaphore_signal(barrier, inc=1, device_id=beside, device_id_type=MESH)
    for d in range(1, KEYS):
        pl.semaphore_signal(barrier, inc=1, device_id=(r, lax.rem(k + d, KEYS)), device_id_type=MESH)

    group = nz // KEYS

    def spot(ref, layer, at):
        return ref.at[layer, pl.ds(pl.multiple_of(at * depth, depth), depth), :]

    def slot(p, zz, xx):
        layer, kind = divmod(p, 4)
        at = zz * 2 + xx
        return spot((wqkv, wo, wu, wd)[kind], layer, at)

    def active(p, zz):
        return None if p % 4 != 1 else (zz // group) == k

    def guarded(condition, action):
        if condition is None:
            action()
        else:
            pl.when(condition)(action)

    columns = pl.ds(pl.multiple_of(k * wide, wide), wide)

    def own_copies(p):
        layer, kind = divmod(p, 4)
        if kind == 0:
            place = pl.ds(pl.multiple_of(r * depth, depth), depth)
            return [
                pltpu.make_async_copy(
                    w.at[layer, :, columns], wqkv.at[layer, place, i * wide : (i + 1) * wide], loc.at[6 * layer + i]
                )
                for i, w in enumerate((w_query, w_key, w_value))
            ]
        source = (None, w_out, w_up, w_down)[kind]
        return [pltpu.make_async_copy(source.at[layer], slot(p, z, x), loc.at[6 * layer + 2 + kind])]

    def own_start(p):
        guarded(active(p, z), lambda: [copy.start() for copy in own_copies(p)] and None)

    def own_wait(p):
        guarded(active(p, z), lambda: [copy.wait() for copy in own_copies(p)] and None)

    def push(p, zz, xx, send_sem, target):
        place = slot(p, zz, xx)
        return pltpu.make_async_remote_copy(
            src_ref=place, dst_ref=place, send_sem=send_sem, recv_sem=w_recv.at[p, xx, zz],
            device_id=target, device_id_type=MESH,
        )

    def straight(p):
        return p in STRAIGHT

    def up(p, zz, xx):
        return push(p, zz, xx, w_send.at[p, xx, zz], (lax.rem(z + 1, nz) * 2 + x, k))

    def down(p, zz, xx):
        sem = w_send.at[p, xx, jnp.where(zz == z, nz, zz)]
        return push(p, zz, xx, sem, (lax.rem(z + nz - 1, nz) * 2 + x, k))

    def over(p, zz):
        return push(p, zz, x, w_over.at[p, zz], beside)

    def spread_own(p, xx, action):
        pl.when(not_top)(lambda: action(up(p, z, xx)))
        pl.when(not_bottom)(lambda: action(down(p, z, xx)))

    def begin(copy):
        copy.start()

    def sent(copy):
        copy.wait_send()

    def issue(p):
        guarded(active(p, z), lambda: spread_own(p, x, begin))

    def beside_own(p):
        guarded(active(p, z), lambda: over(p, z).start())

    def swap(p):
        over_in = push(p, z, 1 - x, w_over.at[p, z], beside)
        over_in.wait_recv()
        spread_own(p, 1 - x, begin)

    def hops(group, action, sides=(True, False)):
        bounds = [1 + (nz - 1) * i // 3 for i in range(4)]

        def one(j, carry):
            if True in sides:
                pl.when(z - j >= 0)(lambda: action(jnp.maximum(z - j, 0), True))
            if False in sides:
                pl.when(z + j < nz)(lambda: action(jnp.minimum(z + j, nz - 1), False))
            return carry

        lax.fori_loop(bounds[group], bounds[group + 1], one, 0)

    def onward(p, zz, xx, below, action):
        if below:
            pl.when(not_top)(lambda: action(up(p, zz, xx)))
        else:
            pl.when(not_bottom)(lambda: action(down(p, zz, xx)))

    def passes(p, group, sides):
        def action(zz, below):
            def take():
                for xx in (x, 1 - x) if straight(p) else (x,):
                    push(p, zz, xx, w_over.at[p, zz], beside).wait_recv()
                    onward(p, zz, xx, below, begin)
                if not straight(p):
                    over(p, zz).start()

            guarded(active(p, zz), take)

        hops(group, action, sides)

    def arrive(p):
        if straight(p):
            return

        def one(zz, carry):
            guarded(active(p, zz), push(p, zz, 1 - x, w_over.at[p, zz], beside).wait_recv)
            return carry

        lax.fori_loop(0, nz, one, 0)

    def drain(p):
        def mine():
            spread_own(p, x, sent)
            if straight(p):
                spread_own(p, 1 - x, sent)
            over(p, z).wait_send()

        guarded(active(p, z), mine)

        def action(zz, below):
            def passed():
                for xx in (x, 1 - x) if straight(p) else (x,):
                    onward(p, zz, xx, below, sent)
                if not straight(p):
                    over(p, zz).wait_send()

            guarded(active(p, zz), passed)

        for group_at in range(3):
            hops(group_at, action)

    def pre_copy(i, d):
        kt = lax.rem(k + d, KEYS)
        source, target = ((pre_k, pk), (pre_v, pv))[i]
        return pltpu.make_async_remote_copy(
            src_ref=source.at[:, :, pl.ds(pl.multiple_of(kt * wide, wide), wide)],
            dst_ref=target.at[:, pl.ds(pl.multiple_of(k * count, count), count), :],
            send_sem=pre_send.at[i, d], recv_sem=pre_recv.at[i, d], device_id=(r, kt), device_id_type=MESH,
        )

    def pre_own(i):
        source, target = ((pre_k, pk), (pre_v, pv))[i]
        return pltpu.make_async_copy(
            source.at[:, :, columns],
            target.at[:, pl.ds(pl.multiple_of(k * count, count), count), :],
            pre_recv.at[i, 0],
        )

    own_block = pl.ds(pl.multiple_of(k * own, own), own)
    cot_copy = pltpu.make_async_copy(cotangent.at[own_block, :], cot, loc.at[12])

    for p in range(4 * LAYERS):
        own_start(p)
    cot_copy.start()
    token_copy = pltpu.make_async_copy(token_rows, tokens, loc.at[13])
    token_copy.start()
    for i in range(2):
        pre_own(i).start()

    visible_code = jnp.where(padding[...] == 1, segments[...], -1).astype(F32)
    codes[...] = jnp.broadcast_to(visible_code, (own, tok)).T

    def mask_of(i, carry):
        queries = segments[:, pl.ds(pl.multiple_of(i * own, own), own)].astype(F32)
        keys_code = codes[pl.ds(pl.multiple_of(jnp.clip(i - 1, 0, KEYS - 3) * own, own), window), :]
        bias[i, 0:prefix, :] = jnp.zeros((prefix, own), F32)
        bias[i, prefix : prefix + window, :] = jnp.where(keys_code == queries, 0.0, NEGATIVE)
        return carry

    lax.fori_loop(0, KEYS, mask_of, 0)

    def widen(i, carry):
        at = pl.multiple_of(i * 16, 16)
        own_x[pl.ds(at, 16), :] = tokens[pl.ds(k * own + at, 16), :].astype(F32)
        return carry

    token_copy.wait()
    lax.fori_loop(0, own // 16, widen, 0)
    ends = jnp.where(z == 0, 1, 0) + jnp.where(z == nz - 1, 1, 0)
    pl.semaphore_wait(barrier, 2 - ends + len(far_partners) + 1 + KEYS - 1)
    own_wait(0)
    for i in range(2):
        for d in range(1, KEYS):
            pre_copy(i, d).start()
    for p in range(1, 4 * LAYERS):
        own_wait(p)
    cot_copy.wait()

    sub = own // SUBS
    block_a, block_b = 2 * far + c, 2 * far + 1 - c

    def rows_at(at, size):
        return pl.ds(pl.multiple_of(at, 16), size)

    def rs_copy(n, i):
        if i < SUBS:
            source, target = part.at[rows_at(block_b * own + i * sub, sub), :], rc.at[n, 0, i * sub : (i + 1) * sub, :]
        elif i == SUBS:
            source, target = part.at[rows_at((2 * near + 1 - c) * own, own), :], rc.at[n, 1]
        else:
            at = slice((i - SUBS - 1) * sub, (i - SUBS) * sub)
            source, target = ys.at[at, :], ry.at[n, at, :]
        return pltpu.make_async_remote_copy(
            src_ref=source, dst_ref=target, send_sem=rs_send.at[i], recv_sem=rs_recv.at[i],
            device_id=sib if i <= SUBS else across, device_id_type=MESH,
        )

    def chunks(total, body, size=16):
        def one(i, carry):
            body(pl.multiple_of(i * size, size))
            return carry

        lax.fori_loop(0, total // size, one, 0)

    def rs_mid(n, i):
        rs_copy(n, i).wait_recv()
        for at in range(i * sub, (i + 1) * sub, 16):
            mine = part[rows_at(block_a * own + at, 16), :].astype(F32)
            ys[at : at + 16, :] = (mine + rc[n, 0, at : at + 16, :].astype(F32)).astype(BF)
        rs_copy(n, SUBS + 1 + i).start()

    def rs_near(n):
        rs_copy(n, SUBS).start()

    def rs_sum(n, at):
        mine = part[rows_at(k * own + at, 16), :].astype(F32) + rc[n, 1, at : at + 16, :].astype(F32)
        return mine + ry[n, at : at + 16, :].astype(F32)

    def rs_each(n, body, leave, between=lambda i: None):
        if GATHER_BEFORE[n] is not None:
            ag_end(GATHER_BEFORE[n])
        rs_copy(n, SUBS).wait_recv()
        for i in range(SUBS):
            between(i)
            rs_copy(n, SUBS + 1 + i).wait_recv()
            for at in range(i * sub, (i + 1) * sub, 16):
                body(at)
            leave(i)
        rs_end(n)

    def gather(n):
        def leave(i):
            ag_copy(n, i).start()
            if i == SUBS - 1:
                ag_copy(n, SUBS).start()

        return leave

    def rs_end(n):
        for i in range(2 * SUBS + 1):
            rs_copy(n, i).wait_send()

    def ag_copy(n, i):
        if i < SUBS:
            place, device = full.at[n, rows_at(k * own + i * sub, sub), :], across
        elif i == SUBS:
            place, device = full.at[n, rows_at(k * own, own), :], sib
        else:
            place, device = full.at[n, rows_at(block_a * own + (i - SUBS - 1) * sub, sub), :], sib
        return pltpu.make_async_remote_copy(
            src_ref=place, dst_ref=place, send_sem=ag_send.at[n // AG_ACT, i], recv_sem=ag_recv.at[n // AG_ACT, i],
            device_id=device, device_id_type=MESH,
        )

    def ag_end(n):
        for i in range(2 * SUBS + 1):
            ag_copy(n, i).wait_send()

    def ag_near(n):
        ag_copy(n, SUBS).wait_recv()

    def ag_pass(n, i):
        ag_copy(n, i).wait_recv()
        ag_copy(n, SUBS + 1 + i).start()

    def ag_got(n, i):
        ag_copy(n, SUBS + 1 + i).wait_recv()

    def ag_far(n, between=lambda: None):
        for i in range(SUBS):
            ag_pass(n, i)
            if i == 0:
                between()
        for i in range(SUBS):
            ag_got(n, i)

    def half_rows(which):
        return pl.ds(pl.multiple_of(which * half, half), half)

    def far_rows(i):
        return rows_at(block_a * own + i * sub, sub), rows_at(block_b * own + i * sub, sub)

    def both(ref, *lead, at):
        return jnp.concatenate([ref[(*lead, rows, slice(None))] for rows in at], axis=0)

    def project(layer, source, which):
        hr = half_rows(which)
        xin = source[hr, :]
        for i in range(3):
            at = slice(i * wide, (i + 1) * wide)
            val = dot_nn(xin, wqkv[layer, :, at])
            qkv[layer, hr, at] = (val * HEAD**-0.5 if i == 0 else val).astype(BF)

    lane_head = lax.broadcasted_iota(jnp.int32, (1, wide), 1) // HEAD
    masks = [jnp.where(lane_head == h, 1.0, 0.0).astype(BF) for h in range(heads)]

    def stacked(value):
        return jnp.concatenate([value * mask for mask in masks], axis=0)

    def place_of(i):
        return pl.multiple_of(i * own, own)

    def window_of(i):
        return pl.multiple_of(jnp.clip(i - 1, 0, KEYS - 3) * own, own)

    def unstacked(value):
        parts = [value[h * HEAD : (h + 1) * HEAD, h * own : (h + 1) * own] for h in range(heads)]
        return jnp.concatenate(parts, axis=0).T

    def seen(layer, start):
        span = pl.ds(start, window)
        return (
            jnp.concatenate([pk[layer], qkv[layer, span, wide : 2 * wide]], axis=0),
            jnp.concatenate([pv[layer], qkv[layer, span, 2 * wide : 3 * wide]], axis=0),
        )

    def attend(layer, i):
        q4 = stacked(qkv[layer, pl.ds(place_of(i), own), 0:wide])
        key_rows, value_rows = seen(layer, window_of(i))
        s = dot_nt(key_rows, q4) + jnp.concatenate([bias[i]] * heads, axis=1)
        e = jnp.exp(s - jnp.max(s, axis=0, keepdims=True))
        p = e * (1.0 / jnp.sum(e, axis=0, keepdims=True))
        prob[layer, i] = p
        att[pl.ds(place_of(i), own), :] = unstacked(dot_tn(value_rows, p.astype(BF))).astype(BF)

    def attend_back(layer, i):
        at = pl.ds(place_of(i), own)
        q4 = stacked(qkv[layer, at, 0:wide])
        go4 = stacked(go[at, :])
        start = window_of(i)
        key_rows, value_rows = seen(layer, start)
        p = prob[layer, i]
        gp = dot_nt(value_rows, go4)
        dsum = jnp.sum(p * gp, axis=0, keepdims=True)
        gs = (p * (gp - dsum)).astype(BF)
        places = pl.ds(prefix + start, window)
        gk_here, gv_here = dot_nn(gs, q4), dot_nn(p.astype(BF), go4)
        gk[0:prefix, :] += gk_here[:prefix]
        gk[places, :] += gk_here[prefix:]
        gv[0:prefix, :] += gv_here[:prefix]
        gv[places, :] += gv_here[prefix:]
        gqkv[at, 0:wide] = (unstacked(dot_tn(key_rows, gs)).astype(BF).astype(F32) * HEAD**-0.5).astype(BF)

    def two(body, which):
        def one(i, carry):
            body(2 * which + i)
            return carry

        lax.fori_loop(0, 2, one, 0)

    def out_rows(layer, at, size):
        rows_here = rows_at(at, size)
        part[rows_here, :] = dot_nn(att[rows_here, :], wo[layer, columns, :]).astype(BF)

    def up_half(layer, n, which):
        hr = half_rows(which)
        u = dot_nn(full[n, hr, :], wu[layer])
        for at in range(0, half, 16):
            v = u[at : at + 16]
            phi_sum = 0.5 * (1.0 + lax.erf(v * 0.7071067811865476))
            density = jnp.exp(v * v * -0.5) * 0.3989422804014327
            here = rows_at(which * half + at, 16)
            hid[here, :] = (v * phi_sum).astype(BF)
            gelu_d[layer, here, :] = phi_sum + v * density

    def ff_back(layer, gradient, slope):
        gu = (dot_nn(gradient, wd[layer]) * slope).astype(BF)
        return dot_nt(gu, wu[layer]).astype(BF)

    def scatter_far(n, step, before=lambda i: None, early=False):
        for i in range(SUBS):
            before(i)
            if early and i > 0:
                rs_mid(n, i - 1)
            value = step(i)
            at_a, at_b = far_rows(i)
            part[at_b, :] = value[sub:]
            rs_copy(n, i).start()
            part[at_a, :] = value[:sub]
            if not early and i > 0:
                rs_mid(n, i - 1)
        rs_mid(n, SUBS - 1)

    def project_back(layer, at, size):
        rows_here = rows_at(at, size)
        part[rows_here, :] = dot_nt(gqkv[rows_here, :], wqkv[layer]).astype(BF)

    def norm_into(n, residual, layer, which, gain, shift, result, target):
        index = 2 * layer + which
        g, b = gain[layer : layer + 1, :], shift[layer : layer + 1, :]

        def body(i):
            value = residual[i : i + 16, :] + rs_sum(n, i)
            centre = value - jnp.mean(value, axis=-1, keepdims=True)
            inv = lax.rsqrt(jnp.mean(centre * centre, axis=-1, keepdims=True) + EPSILON)
            hat = centre * inv
            done = hat * g + b
            zhat[index, i : i + 16, :] = hat
            rinv[index, i : i + 16, :] = inv
            result[i : i + 16, :] = done
            full[target, rows_at(k * own + i, 16), :] = done.astype(BF)

        return body

    def into(n):
        def store(i, low):
            full[n, rows_at(k * own + i, 16), :] = low

        return store

    def norm_back(read, layer, which, gain, store):
        index = 2 * layer + which
        g = gain[layer : layer + 1, :]

        def body(i):
            scaled = read(i) * g
            hat = zhat[index, i : i + 16, :]
            inv = rinv[index, i : i + 16, :]
            first = jnp.mean(scaled, axis=-1, keepdims=True)
            second = jnp.mean(scaled * hat, axis=-1, keepdims=True)
            result = inv * (scaled - first - hat * second)
            own_g[i : i + 16, :] = result
            store(i, result.astype(BF))

        return body

    quarter = width // KEYS

    def quarter_copy(layer, i):
        at = (k, k, lax.rem(k + 2, KEYS))[i]
        place = wo.at[layer, pl.ds(pl.multiple_of(at * quarter, quarter), quarter), :]
        return pltpu.make_async_remote_copy(
            src_ref=place, dst_ref=place, send_sem=wq_send.at[layer, i], recv_sem=wq_recv.at[layer, i],
            device_id=(across, sib, sib)[i], device_id_type=MESH,
        )

    def quarter_start(layer):
        quarter_copy(layer, 0).start()
        quarter_copy(layer, 1).start()

    def quarter_pass(layer):
        quarter_copy(layer, 0).wait_recv()
        quarter_copy(layer, 2).start()

    def quarter_got(layer):
        quarter_copy(layer, 1).wait_recv()
        quarter_copy(layer, 2).wait_recv()

    def go_copy(d, i):
        kt = lax.rem(k + d, KEYS)
        return pltpu.make_async_remote_copy(
            src_ref=go_all.at[i * sub : (i + 1) * sub, pl.ds(pl.multiple_of(kt * wide, wide), wide)],
            dst_ref=go.at[rows_at(k * own + i * sub, sub), :],
            send_sem=go_send.at[d, i], recv_sem=go_recv.at[d, i], device_id=(r, kt), device_id_type=MESH,
        )

    def go_leave(layer):
        def leave(i):
            at = slice(i * sub, (i + 1) * sub)
            go_all[at, :] = dot_nt(ga[at, :], wo[layer]).astype(BF)
            for d in (2, *range(1, KEYS, 2)):
                go_copy(d, i).start()
            go[rows_at(k * own + i * sub, sub), :] = go_all[at, columns]

        return leave

    def go_wait(d):
        for i in range(SUBS):
            go_copy(d, i).wait_recv()

    def weights_at(layer, point):
        for kind, p, distance in SCHEDULE.get((layer, point), ()):
            if kind == "along":
                issue(p)
            elif kind == "beside":
                beside_own(p)
            elif kind == "swap":
                swap(p)
            else:
                passes(p, distance - 1, (kind == "up",))

    def forward_layer(layer):
        base = 4 * layer
        rs_a, rs_f = ((RS_A0, RS_F0), (RS_A1, RS_F1))[layer]
        ag_m = (AG_M0, AG_M1)[layer]
        source = tokens if layer == 0 else full.at[AG_X1]
        here = functools.partial(weights_at, layer)
        here("start")
        arrive(base)
        if layer > 0:
            ag_near(AG_X1)
        project(layer, source, near)
        here("projected near")
        if layer == 0:
            for i in range(2):
                pre_own(i).wait()
                for d in range(1, KEYS):
                    pre_copy(i, d).wait_recv()
        if layer > 0:
            ag_far(AG_X1)
        project(layer, source, far)
        here("projected")
        attend(layer, block_b)
        here("attended b")
        arrive(base + 1)
        out_rows(layer, block_b * own, own)
        for i in range(SUBS):
            rs_copy(rs_a, i).start()
        here("out b")
        attend(layer, block_a)
        out_rows(layer, block_a * own, own)
        for i in range(SUBS):
            rs_mid(rs_a, i)
        here("out a")
        two(functools.partial(attend, layer), near)
        out_rows(layer, near * half, half)
        rs_near(rs_a)
        here("out near")
        rs_each(
            rs_a,
            norm_into(rs_a, own_x, layer, 0, g1, b1, own_m, ag_m),
            gather(ag_m),
            lambda i: here(f"norm {i}"),
        )
        here("normed")
        quarter_start(layer)
        arrive(base + 2)
        ag_near(ag_m)
        here("up")
        up_half(layer, ag_m, near)
        here("up near")
        ag_far(ag_m)
        up_half(layer, ag_m, far)
        here("up far")
        arrive(base + 3)
        here("down")
        scatter_far(
            rs_f,
            lambda i: dot_nt(both(hid, at=far_rows(i)), wd[layer]).astype(BF),
            lambda i: here(f"down {i}"),
        )
        part[half_rows(near), :] = dot_nt(hid[half_rows(near), :], wd[layer]).astype(BF)
        rs_near(rs_f)
        if layer == 0:
            quarter_pass(0)
        here("down near")

    forward_layer(0)
    rs_each(
        RS_F0,
        norm_into(RS_F0, own_m, 0, 1, g2, b2, own_x, AG_X1),
        gather(AG_X1),
        lambda i: weights_at(0, f"last norm {i}"),
    )
    forward_layer(1)

    def prefix_copy(layer, i, d):
        kt = lax.rem(k + d, KEYS)
        source = (gk, gv)[i]
        return pltpu.make_async_remote_copy(
            src_ref=source.at[pl.ds(pl.multiple_of(kt * count, count), count), :],
            dst_ref=pg.at[layer, i, :, columns],
            send_sem=pg_send.at[i, d], recv_sem=pg_recv.at[i, d],
            device_id=(r, kt), device_id_type=MESH,
        )

    def prefix_own(layer, i):
        return pltpu.make_async_copy(
            (gk, gv)[i].at[pl.ds(pl.multiple_of(k * count, count), count), :],
            pg.at[layer, i, :, columns],
            pg_recv.at[i, 0],
        )

    bits = rows.bit_length() - 1

    def row_copy(layer, b):
        bit = 1 << b
        partner = r + bit - 2 * bit * lax.rem(r // bit, 2)
        return pltpu.make_async_remote_copy(
            src_ref=pg_low.at[layer], dst_ref=pg_in.at[layer, b],
            send_sem=pgr_send.at[layer, b], recv_sem=pgr_recv.at[layer, b],
            device_id=(partner, k), device_id_type=MESH,
        )

    def row_start(layer, b):
        low = pg[layer].astype(BF)
        pg_low[layer] = low
        pg[layer] = low.astype(F32)
        row_copy(layer, b).start()

    def row_step(layer, b):
        row_copy(layer, b).wait()
        pg[layer] += pg_in[layer, b].astype(F32)
        if b + 1 < bits:
            row_start(layer, b + 1)

    def prefix_start(layer):
        for i in range(2):
            prefix_own(layer, i).start()
            for d in range(1, KEYS):
                prefix_copy(layer, i, d).start()

    def prefix_take(layer):
        for i in range(2):
            prefix_own(layer, i).wait()
            for d in range(1, KEYS):
                prefix_copy(layer, i, d).wait_recv()
        row_start(layer, 0)

    def prefix_sent(layer):
        for i in range(2):
            for d in range(1, KEYS):
                prefix_copy(layer, i, d).wait_send()

    for layer in reversed(range(LAYERS)):
        rs_gm, rs_gx = ((RS_GM0, RS_GX0), (RS_GM1, RS_GX1))[layer]
        ag_gf = (AG_GF0, AG_GF1)[layer]
        if layer == LAYERS - 1:
            forth = norm_into(RS_F1, own_m, 1, 1, g2, b2, own_x, AG_ACT)
            back = norm_back(lambda i: cot[i : i + 16, :].astype(F32), layer, 1, g2, into(ag_gf))

            def turn(i):
                forth(i)
                back(i)

            rs_each(RS_F1, turn, gather(ag_gf))
        else:
            rs_each(
                RS_GX1,
                norm_back(lambda i: own_g[i : i + 16, :] + rs_sum(RS_GX1, i), layer, 1, g2, into(ag_gf)),
                gather(ag_gf),
            )
            prefix_take(layer + 1)
        ag_near(ag_gf)
        part[half_rows(near), :] = ff_back(layer, full[ag_gf, half_rows(near), :], gelu_d[layer, half_rows(near), :])
        rs_near(rs_gm)

        def step(i):
            ag_got(ag_gf, i)
            at = far_rows(i)
            return ff_back(layer, both(full, ag_gf, at=at), both(gelu_d, layer, at=at))

        if layer == LAYERS - 1:
            quarter_pass(layer)
        scatter_far(rs_gm, step, lambda i: ag_pass(ag_gf, i), early=True)
        if layer == 0:
            row_step(1, 0)
        gk[...] = jnp.zeros_like(gk)
        gv[...] = jnp.zeros_like(gv)
        quarter_got(layer)

        def keep(i, low):
            ga[i : i + 16, :] = low

        rs_each(
            rs_gm,
            norm_back(lambda i: own_g[i : i + 16, :] + rs_sum(rs_gm, i), layer, 0, g1, keep),
            go_leave(layer),
        )
        if layer == LAYERS - 1:
            for i in range(SUBS + 1):
                ag_copy(AG_ACT, i).start()
        go_wait(3 - 2 * c)
        two(functools.partial(attend_back, layer), near)
        if layer == 0:
            row_step(1, 1)
        go_wait(2)
        go_wait(1 + 2 * c)
        two(functools.partial(attend_back, layer), far)
        for d in range(1, KEYS):
            for i in range(SUBS):
                go_copy(d, i).wait_send()
        prefix_start(layer)

        def narrow(which):
            def body(i):
                i = which * half + i
                gqkv[rows_at(i, 16), wide : 2 * wide] = gk[rows_at(prefix + i, 16), :].astype(BF)
                gqkv[rows_at(i, 16), 2 * wide : 3 * wide] = gv[rows_at(prefix + i, 16), :].astype(BF)

            chunks(half, body)

        narrow(far)
        project_back(layer, block_b * own, own)
        for i in range(SUBS):
            rs_copy(rs_gx, i).start()
        project_back(layer, block_a * own, own)
        for i in range(SUBS):
            rs_mid(rs_gx, i)
        narrow(near)
        project_back(layer, near * half, half)
        rs_near(rs_gx)
        if layer == LAYERS - 1:
            ag_far(AG_ACT)
            ag_near(AG_ACT)
        else:
            for b in range(2, bits):
                row_step(1, b)
            prefix_take(0)
        prefix_sent(layer)

    act_copy = pltpu.make_async_copy(full.at[AG_ACT], low_out.at[1], loc.at[13])
    act_copy.start()

    def last(i):
        full[AG_GX, rows_at(k * own + i, 16), :] = (own_g[i : i + 16, :] + rs_sum(RS_GX0, i)).astype(BF)

    rs_each(RS_GX0, last, gather(AG_GX), lambda i: row_step(0, 0) if i == SUBS - 1 else None)
    for p in range(4 * LAYERS):
        drain(p)
    for i in range(2):
        for d in range(1, KEYS):
            pre_copy(i, d).wait_send()
    ag_near(AG_GX)

    def grad_copy(which):
        return pltpu.make_async_copy(
            full.at[AG_GX, half_rows(which), :], low_out.at[0, half_rows(which), :], loc.at[14 + (which is far)]
        )

    grad_copy(near).start()
    ag_far(AG_GX, lambda: row_step(0, 1))
    grad_copy(far).start()
    for b in range(2, bits):
        row_step(0, b)
    for i in range(2):
        for layer in range(LAYERS):
            prefix_out[i, layer] = pg[layer, i]
    ag_end(AG_GX)
    ag_end(AG_ACT)
    for layer in range(LAYERS):
        for i in range(3):
            quarter_copy(layer, i).wait_send()
    act_copy.wait()
    grad_copy(near).wait()
    grad_copy(far).wait()


def results(low, grads, act, gt, gpk, gpv, narrow, broad, act_held, grads_held, sems):
    parts, size = narrow.shape[:2]

    def taken(i):
        return pltpu.make_async_copy(low.at[0, i * size : (i + 1) * size, :], narrow.at[i], sems.at[0, i])

    def given(i):
        return pltpu.make_async_copy(broad.at[i], gt.at[0, i * size : (i + 1) * size, :], sems.at[1, i])

    in_act = pltpu.make_async_copy(low.at[1], act_held, sems.at[2, 0])
    out_act = pltpu.make_async_copy(act_held, act.at[0], sems.at[2, 0])
    in_grads = pltpu.make_async_copy(grads, grads_held, sems.at[2, 1])
    out_grads = [pltpu.make_async_copy(grads_held.at[i], (gpk, gpv)[i], sems.at[2, 2 + i]) for i in range(2)]
    for i in range(parts):
        taken(i).start()
    in_act.start()
    in_grads.start()
    for i in range(parts):
        taken(i).wait()
        broad[i] = narrow[i].astype(F32)
        given(i).start()
    in_act.wait()
    out_act.start()
    in_grads.wait()
    for copy in out_grads:
        copy.start()
    for i in range(parts):
        given(i).wait()
    out_act.wait()
    for copy in out_grads:
        copy.wait()


def per_device(
    tokens, cotangent, segment_ids, pad_mask, prefix_keys, prefix_values,
    w_query, w_key, w_value, w_out, w_up, w_down_t,
    norm1_gain, norm1_bias, norm2_gain, norm2_bias,
):
    rows, keys = lax.axis_size("rows"), lax.axis_size("keys")
    assert keys == KEYS and rows % (2 * KEYS) == 0 and rows & (rows - 1) == 0
    tok, width = tokens.shape[1:]
    count = prefix_keys.shape[1]
    prefix = count * keys
    local_ff = w_up.shape[2]
    wide, own, window = width // keys, tok // keys, 3 * tok // keys
    heads = wide // HEAD
    nz, bits, pieces = rows // 2, rows.bit_length() - 1, 4 * LAYERS
    vmem, anywhere = pl.BlockSpec(memory_space=pltpu.VMEM), pl.BlockSpec(memory_space=pl.ANY)
    dma = pltpu.SemaphoreType.DMA
    scratch = [
        pltpu.VMEM((LAYERS, width, 3 * wide), BF),
        pltpu.VMEM((LAYERS, width, width), BF),
        pltpu.VMEM((LAYERS, width, local_ff), BF),
        pltpu.VMEM((LAYERS, width, local_ff), BF),
        pltpu.VMEM((LAYERS, prefix, wide), BF),
        pltpu.VMEM((LAYERS, prefix, wide), BF),
        pltpu.VMEM((tok, width), BF),
        pltpu.VMEM((SCATTERS, 2, own, width), BF),
        pltpu.VMEM((SCATTERS, own, width), BF),
        pltpu.VMEM((own, width), BF),
        pltpu.VMEM((GATHERS, tok, width), BF),
        pltpu.VMEM((LAYERS, tok, 3 * wide), BF),
        pltpu.VMEM((LAYERS, keys, prefix + window, heads * own), F32),
        pltpu.VMEM((LAYERS, tok, local_ff), F32),
        pltpu.VMEM((2 * LAYERS, own, width), F32),
        pltpu.VMEM((2 * LAYERS, own, 1), F32),
        pltpu.VMEM((own, width), F32),
        pltpu.VMEM((own, width), F32),
        pltpu.VMEM((own, width), F32),
        pltpu.VMEM((own, width), BF),
        pltpu.VMEM((tok, wide), BF),
        pltpu.VMEM((tok, 3 * wide), BF),
        pltpu.VMEM((prefix + tok, wide), F32),
        pltpu.VMEM((prefix + tok, wide), F32),
        pltpu.VMEM((tok, width), BF),
        pltpu.VMEM((tok, local_ff), BF),
        pltpu.VMEM((own, width), BF),
        pltpu.VMEM((own, width), BF),
        pltpu.VMEM((tok, wide), BF),
        pltpu.VMEM((keys, prefix + window, own), F32),
        pltpu.VMEM((tok, own), F32),
        pltpu.VMEM((LAYERS, 2, count, width), F32),
        pltpu.VMEM((LAYERS, 2, count, width), BF),
        pltpu.VMEM((LAYERS, bits, 2, count, width), BF),
        dma((pieces, 2, nz + 1)),
        dma((pieces, 2, nz)),
        dma((pieces, nz)),
        dma((16,)),
        dma((2, keys)),
        dma((2, keys)),
        dma((LAYERS, 3)),
        dma((LAYERS, 3)),
        dma((keys, SUBS)),
        dma((keys, SUBS)),
        dma((2 * SUBS + 1,)),
        dma((2 * SUBS + 1,)),
        dma((2, 2 * SUBS + 1)),
        dma((2, 2 * SUBS + 1)),
        dma((2, keys)),
        dma((2, keys)),
        dma((LAYERS, bits)),
        dma((LAYERS, bits)),
    ]
    low, grads = pl.pallas_call(
        functools.partial(kernel, (rows, tok, width, local_ff)),
        out_shape=(
            jax.ShapeDtypeStruct((2, tok, width), BF),
            jax.ShapeDtypeStruct((2, LAYERS, count, width), F32),
        ),
        in_specs=[anywhere, anywhere, vmem, vmem] + [anywhere] * 8 + [vmem] * 4,
        out_specs=(anywhere, vmem),
        scratch_shapes=scratch,
        compiler_params=pltpu.CompilerParams(
            collective_id=0, has_side_effects=True, vmem_limit_bytes=62 * 1024 * 1024 - 512 * 1024
        ),
    )(
        tokens[0], cotangent[0], segment_ids, pad_mask, prefix_keys, prefix_values,
        w_query, w_key, w_value, w_out, w_up, w_down_t,
        norm1_gain, norm1_bias, norm2_gain, norm2_bias,
    )
    whole = (LAYERS, count, width)
    return pl.pallas_call(
        results,
        out_shape=(
            jax.ShapeDtypeStruct((1, tok, width), BF),
            jax.ShapeDtypeStruct((1, tok, width), F32),
            jax.ShapeDtypeStruct(whole, F32),
            jax.ShapeDtypeStruct(whole, F32),
        ),
        in_specs=[anywhere] * 2,
        out_specs=(anywhere,) * 4,
        scratch_shapes=[
            pltpu.VMEM((2 * keys, own // 2, width), BF),
            pltpu.VMEM((2 * keys, own // 2, width), F32),
            pltpu.VMEM((tok, width), BF),
            pltpu.VMEM((2, *whole), F32),
            dma((3, 2 * keys)),
        ],
    )(low, grads)


def solution(mesh):
    row3 = P("rows", None, None)
    weight = P(None, "rows", None)
    return jax.shard_map(
        per_device,
        mesh=mesh,
        in_specs=(
            row3,
            row3,
            P("rows", None),
            P("rows", None),
            P(None, "keys", None),
            P(None, "keys", None),
            weight,
            weight,
            weight,
            weight,
            P(None, "rows", "keys"),
            P(None, "rows", "keys"),
            P(),
            P(),
            P(),
            P(),
        ),
        out_specs=(row3, row3, P(None, "keys", None), P(None, "keys", None)),
        check_vma=False,
    )
```

```python
import functools

import jax
import jax.numpy as jnp
from jax import lax
from jax.experimental import pallas as pl
from jax.experimental.pallas import tpu as pltpu
from jax.sharding import PartitionSpec as P

HEAD = 64
LAYERS = 2
KEYS = 4
EPSILON = 1e-05
NEGATIVE = -1000000000.0
MESH = pl.DeviceIdType.MESH
BF = jnp.bfloat16
F32 = jnp.float32

AG_M0, AG_X1, AG_M1, AG_GF1, AG_GF0, AG_GX, AG_ACT = range(7)
GATHERS = 7
RS_A0, RS_F0, RS_A1, RS_F1, RS_GM1, RS_GX1, RS_GM0, RS_GX0 = range(8)
SCATTERS = 8
GATHER_BEFORE = (None, AG_M0, AG_X1, AG_M1, AG_GF1, None, AG_GF0, None)
SUBS = 2

SCHEDULE = {
    (0, "start"): (
        ("beside", 1, 0),
        ("beside", 7, 0),
        ("along", 1, 0),
        ("beside", 2, 0),
        ("along", 0, 0),
        ("down", 1, 1),
        ("along", 4, 0),
        ("up", 1, 1),
        ("down", 0, 1),
        ("up", 0, 1),
        ("up", 1, 2),
        ("down", 1, 2),
        ("along", 2, 0),
        ("up", 0, 2),
        ("up", 1, 3),
        ("beside", 0, 0),
        ("down", 0, 2),
        ("up", 2, 1),
        ("down", 1, 3),
        ("down", 2, 1),
        ("up", 0, 3),
        ("along", 5, 0),
        ("up", 2, 2),
        ("down", 0, 3),
        ("along", 3, 0),
        ("down", 2, 2),
        ("up", 2, 3),
        ("down", 3, 1),
        ("down", 5, 1),
        ("up", 3, 1),
        ("up", 3, 2),
    ),
    (0, "attended b"): (
        ("up", 5, 2),
    ),
    (0, "out b"): (
        ("beside", 5, 0),
        ("up", 5, 1),
        ("along", 6, 0),
    ),
    (0, "out a"): (
        ("beside", 3, 0),
        ("down", 3, 2),
        ("down", 5, 2),
        ("down", 2, 3),
    ),
    (0, "norm 1"): (
        ("up", 4, 1),
        ("up", 3, 3),
        ("up", 4, 2),
        ("down", 4, 1),
    ),
    (0, "normed"): (
        ("up", 4, 3),
        ("swap", 7, 0),
    ),
    (0, "up"): (
        ("down", 3, 3),
        ("down", 4, 2),
    ),
    (0, "up far"): (
        ("along", 7, 0),
    ),
    (0, "down 0"): (
        ("beside", 4, 0),
        ("up", 6, 1),
    ),
    (0, "down 1"): (
        ("down", 5, 3),
        ("up", 5, 3),
    ),
    (0, "last norm 0"): (
        ("down", 4, 3),
        ("down", 6, 1),
    ),
    (0, "last norm 1"): (
        ("up", 6, 2),
        ("down", 6, 2),
    ),
    (1, "start"): (
        ("beside", 6, 0),
        ("down", 7, 1),
    ),
    (1, "projected near"): (
        ("up", 7, 1),
    ),
    (1, "out b"): (
        ("up", 6, 3),
    ),
    (1, "out a"): (
        ("down", 6, 3),
    ),
    (1, "norm 0"): (
        ("down", 7, 2),
    ),
    (1, "norm 1"): (
        ("up", 7, 2),
    ),
    (1, "up far"): (
        ("up", 7, 3),
        ("down", 7, 3),
    ),
}
STRAIGHT = (7,)


def dot_nn(a, b):
    return lax.dot_general(a, b, (((1,), (0,)), ((), ())), preferred_element_type=F32)


def dot_nt(a, b):
    return lax.dot_general(a, b, (((1,), (1,)), ((), ())), preferred_element_type=F32)


def dot_tn(a, b):
    return lax.dot_general(a, b, (((0,), (0,)), ((), ())), preferred_element_type=F32)


def kernel(
    dims,
    token_rows, cotangent, segments, padding, pre_k, pre_v,
    w_query, w_key, w_value, w_out, w_up, w_down,
    g1, b1, g2, b2,
    low_out, prefix_out,
    wqkv, wo, wu, wd, pk, pv,
    part, rc, ry, ys, full,
    qkv, prob, gelu_d, zhat, rinv,
    own_x, own_m, own_g, cot, att, gqkv, gk, gv, tokens, hid, ga, go_all, go, bias, codes,
    pg, pg_low, pg_in,
    w_send, w_recv, w_over, loc, pre_send, pre_recv,
    wq_send, wq_recv, go_send, go_recv,
    rs_send, rs_recv, ag_send, ag_recv, pg_send, pg_recv, pgr_send, pgr_recv,
):
    rows, tok, width, local_ff = dims
    nz = rows // 2
    wide = width // KEYS
    heads = wide // HEAD
    own = tok // KEYS
    half = tok // 2
    depth = width // rows
    count = pre_k.shape[1]
    prefix = KEYS * count
    window = 3 * own

    r = lax.axis_index("rows")
    k = lax.axis_index("keys")
    z, x = r // 2, lax.rem(r, 2)
    y, c = k // 2, lax.rem(k, 2)
    sib = (r, k + 1 - 2 * c)
    across = (r, lax.rem(k + 2, KEYS))
    beside = (r + 1 - 2 * x, k)
    far, near = 1 - y, y

    barrier = pltpu.get_barrier_semaphore()

    def greet(zz):
        pl.semaphore_signal(barrier, inc=1, device_id=(zz * 2 + x, k), device_id_type=MESH)

    not_top, not_bottom = z < nz - 1, z > 0
    pl.when(not_top)(lambda: greet(lax.rem(z + 1, nz)))
    pl.when(not_bottom)(lambda: greet(lax.rem(z + nz - 1, nz)))
    far_partners = [1 << b for b in range(1, nz.bit_length() - 1)]
    for bit in far_partners:
        greet(z + bit - 2 * bit * lax.rem(z // bit, 2))
    pl.semaphore_signal(barrier, inc=1, device_id=beside, device_id_type=MESH)
    for d in range(1, KEYS):
        pl.semaphore_signal(barrier, inc=1, device_id=(r, lax.rem(k + d, KEYS)), device_id_type=MESH)

    group = nz // KEYS

    def spot(ref, layer, at):
        return ref.at[layer, pl.ds(pl.multiple_of(at * depth, depth), depth), :]

    def slot(p, zz, xx):
        layer, kind = divmod(p, 4)
        at = zz * 2 + xx
        return spot((wqkv, wo, wu, wd)[kind], layer, at)

    def active(p, zz):
        return None if p % 4 != 1 else (zz // group) == k

    def guarded(condition, action):
        if condition is None:
            action()
        else:
            pl.when(condition)(action)

    columns = pl.ds(pl.multiple_of(k * wide, wide), wide)

    def own_copies(p):
        layer, kind = divmod(p, 4)
        if kind == 0:
            place = pl.ds(pl.multiple_of(r * depth, depth), depth)
            return [
                pltpu.make_async_copy(
                    w.at[layer, :, columns], wqkv.at[layer, place, i * wide : (i + 1) * wide], loc.at[6 * layer + i]
                )
                for i, w in enumerate((w_query, w_key, w_value))
            ]
        source = (None, w_out, w_up, w_down)[kind]
        return [pltpu.make_async_copy(source.at[layer], slot(p, z, x), loc.at[6 * layer + 2 + kind])]

    def own_start(p):
        guarded(active(p, z), lambda: [copy.start() for copy in own_copies(p)] and None)

    def own_wait(p):
        guarded(active(p, z), lambda: [copy.wait() for copy in own_copies(p)] and None)

    def push(p, zz, xx, send_sem, target):
        place = slot(p, zz, xx)
        return pltpu.make_async_remote_copy(
            src_ref=place, dst_ref=place, send_sem=send_sem, recv_sem=w_recv.at[p, xx, zz],
            device_id=target, device_id_type=MESH,
        )

    def straight(p):
        return p in STRAIGHT

    def up(p, zz, xx):
        return push(p, zz, xx, w_send.at[p, xx, zz], (lax.rem(z + 1, nz) * 2 + x, k))

    def down(p, zz, xx):
        sem = w_send.at[p, xx, jnp.where(zz == z, nz, zz)]
        return push(p, zz, xx, sem, (lax.rem(z + nz - 1, nz) * 2 + x, k))

    def over(p, zz):
        return push(p, zz, x, w_over.at[p, zz], beside)

    def spread_own(p, xx, action):
        pl.when(not_top)(lambda: action(up(p, z, xx)))
        pl.when(not_bottom)(lambda: action(down(p, z, xx)))

    def begin(copy):
        copy.start()

    def sent(copy):
        copy.wait_send()

    def issue(p):
        guarded(active(p, z), lambda: spread_own(p, x, begin))

    def beside_own(p):
        guarded(active(p, z), lambda: over(p, z).start())

    def swap(p):
        over_in = push(p, z, 1 - x, w_over.at[p, z], beside)
        over_in.wait_recv()
        spread_own(p, 1 - x, begin)

    def hops(group, action, sides=(True, False)):
        bounds = [1 + (nz - 1) * i // 3 for i in range(4)]

        def one(j, carry):
            if True in sides:
                pl.when(z - j >= 0)(lambda: action(jnp.maximum(z - j, 0), True))
            if False in sides:
                pl.when(z + j < nz)(lambda: action(jnp.minimum(z + j, nz - 1), False))
            return carry

        lax.fori_loop(bounds[group], bounds[group + 1], one, 0)

    def onward(p, zz, xx, below, action):
        if below:
            pl.when(not_top)(lambda: action(up(p, zz, xx)))
        else:
            pl.when(not_bottom)(lambda: action(down(p, zz, xx)))

    def passes(p, group, sides):
        def action(zz, below):
            def take():
                for xx in (x, 1 - x) if straight(p) else (x,):
                    push(p, zz, xx, w_over.at[p, zz], beside).wait_recv()
                    onward(p, zz, xx, below, begin)
                if not straight(p):
                    over(p, zz).start()

            guarded(active(p, zz), take)

        hops(group, action, sides)

    def arrive(p):
        if straight(p):
            return

        def one(zz, carry):
            guarded(active(p, zz), push(p, zz, 1 - x, w_over.at[p, zz], beside).wait_recv)
            return carry

        lax.fori_loop(0, nz, one, 0)

    def drain(p):
        def mine():
            spread_own(p, x, sent)
            if straight(p):
                spread_own(p, 1 - x, sent)
            over(p, z).wait_send()

        guarded(active(p, z), mine)

        def action(zz, below):
            def passed():
                for xx in (x, 1 - x) if straight(p) else (x,):
                    onward(p, zz, xx, below, sent)
                if not straight(p):
                    over(p, zz).wait_send()

            guarded(active(p, zz), passed)

        for group_at in range(3):
            hops(group_at, action)

    def pre_copy(i, d):
        kt = lax.rem(k + d, KEYS)
        source, target = ((pre_k, pk), (pre_v, pv))[i]
        return pltpu.make_async_remote_copy(
            src_ref=source.at[:, :, pl.ds(pl.multiple_of(kt * wide, wide), wide)],
            dst_ref=target.at[:, pl.ds(pl.multiple_of(k * count, count), count), :],
            send_sem=pre_send.at[i, d], recv_sem=pre_recv.at[i, d], device_id=(r, kt), device_id_type=MESH,
        )

    def pre_own(i):
        source, target = ((pre_k, pk), (pre_v, pv))[i]
        return pltpu.make_async_copy(
            source.at[:, :, columns],
            target.at[:, pl.ds(pl.multiple_of(k * count, count), count), :],
            pre_recv.at[i, 0],
        )

    own_block = pl.ds(pl.multiple_of(k * own, own), own)
    cot_copy = pltpu.make_async_copy(cotangent.at[own_block, :], cot, loc.at[12])

    for p in range(4 * LAYERS):
        own_start(p)
    cot_copy.start()
    token_copy = pltpu.make_async_copy(token_rows, tokens, loc.at[13])
    token_copy.start()
    for i in range(2):
        pre_own(i).start()

    visible_code = jnp.where(padding[...] == 1, segments[...], -1).astype(F32)
    codes[...] = jnp.broadcast_to(visible_code, (own, tok)).T

    def mask_of(i, carry):
        queries = segments[:, pl.ds(pl.multiple_of(i * own, own), own)].astype(F32)
        keys_code = codes[pl.ds(pl.multiple_of(jnp.clip(i - 1, 0, KEYS - 3) * own, own), window), :]
        bias[i, 0:prefix, :] = jnp.zeros((prefix, own), F32)
        bias[i, prefix : prefix + window, :] = jnp.where(keys_code == queries, 0.0, NEGATIVE)
        return carry

    lax.fori_loop(0, KEYS, mask_of, 0)

    def widen(i, carry):
        at = pl.multiple_of(i * 16, 16)
        own_x[pl.ds(at, 16), :] = tokens[pl.ds(k * own + at, 16), :].astype(F32)
        return carry

    token_copy.wait()
    lax.fori_loop(0, own // 16, widen, 0)
    ends = jnp.where(z == 0, 1, 0) + jnp.where(z == nz - 1, 1, 0)
    pl.semaphore_wait(barrier, 2 - ends + len(far_partners) + 1 + KEYS - 1)
    own_wait(0)
    for i in range(2):
        for d in range(1, KEYS):
            pre_copy(i, d).start()
    for p in range(1, 4 * LAYERS):
        own_wait(p)
    cot_copy.wait()

    sub = own // SUBS
    block_a, block_b = 2 * far + c, 2 * far + 1 - c

    def rows_at(at, size):
        return pl.ds(pl.multiple_of(at, 16), size)

    def rs_copy(n, i):
        if i < SUBS:
            source, target = part.at[rows_at(block_b * own + i * sub, sub), :], rc.at[n, 0, i * sub : (i + 1) * sub, :]
        elif i == SUBS:
            source, target = part.at[rows_at((2 * near + 1 - c) * own, own), :], rc.at[n, 1]
        else:
            at = slice((i - SUBS - 1) * sub, (i - SUBS) * sub)
            source, target = ys.at[at, :], ry.at[n, at, :]
        return pltpu.make_async_remote_copy(
            src_ref=source, dst_ref=target, send_sem=rs_send.at[i], recv_sem=rs_recv.at[i],
            device_id=sib if i <= SUBS else across, device_id_type=MESH,
        )

    def chunks(total, body, size=16):
        def one(i, carry):
            body(pl.multiple_of(i * size, size))
            return carry

        lax.fori_loop(0, total // size, one, 0)

    def rs_mid(n, i):
        rs_copy(n, i).wait_recv()
        for at in range(i * sub, (i + 1) * sub, 16):
            mine = part[rows_at(block_a * own + at, 16), :].astype(F32)
            ys[at : at + 16, :] = (mine + rc[n, 0, at : at + 16, :].astype(F32)).astype(BF)
        rs_copy(n, SUBS + 1 + i).start()

    def rs_near(n):
        rs_copy(n, SUBS).start()

    def rs_sum(n, at):
        mine = part[rows_at(k * own + at, 16), :].astype(F32) + rc[n, 1, at : at + 16, :].astype(F32)
        return mine + ry[n, at : at + 16, :].astype(F32)

    def rs_each(n, body, leave, between=lambda i: None):
        if GATHER_BEFORE[n] is not None:
            ag_end(GATHER_BEFORE[n])
        rs_copy(n, SUBS).wait_recv()
        for i in range(SUBS):
            between(i)
            rs_copy(n, SUBS + 1 + i).wait_recv()
            for at in range(i * sub, (i + 1) * sub, 16):
                body(at)
            leave(i)
        rs_end(n)

    def gather(n):
        def leave(i):
            ag_copy(n, i).start()
            if i == SUBS - 1:
                ag_copy(n, SUBS).start()

        return leave

    def rs_end(n):
        for i in range(2 * SUBS + 1):
            rs_copy(n, i).wait_send()

    def ag_copy(n, i):
        if i < SUBS:
            place, device = full.at[n, rows_at(k * own + i * sub, sub), :], across
        elif i == SUBS:
            place, device = full.at[n, rows_at(k * own, own), :], sib
        else:
            place, device = full.at[n, rows_at(block_a * own + (i - SUBS - 1) * sub, sub), :], sib
        return pltpu.make_async_remote_copy(
            src_ref=place, dst_ref=place, send_sem=ag_send.at[n // AG_ACT, i], recv_sem=ag_recv.at[n // AG_ACT, i],
            device_id=device, device_id_type=MESH,
        )

    def ag_end(n):
        for i in range(2 * SUBS + 1):
            ag_copy(n, i).wait_send()

    def ag_near(n):
        ag_copy(n, SUBS).wait_recv()

    def ag_pass(n, i):
        ag_copy(n, i).wait_recv()
        ag_copy(n, SUBS + 1 + i).start()

    def ag_got(n, i):
        ag_copy(n, SUBS + 1 + i).wait_recv()

    def ag_far(n, between=lambda: None):
        for i in range(SUBS):
            ag_pass(n, i)
            if i == 0:
                between()
        for i in range(SUBS):
            ag_got(n, i)

    def half_rows(which):
        return pl.ds(pl.multiple_of(which * half, half), half)

    def far_rows(i):
        return rows_at(block_a * own + i * sub, sub), rows_at(block_b * own + i * sub, sub)

    def both(ref, *lead, at):
        return jnp.concatenate([ref[(*lead, rows, slice(None))] for rows in at], axis=0)

    def project(layer, source, which):
        hr = half_rows(which)
        xin = source[hr, :]
        for i in range(3):
            at = slice(i * wide, (i + 1) * wide)
            val = dot_nn(xin, wqkv[layer, :, at])
            qkv[layer, hr, at] = (val * HEAD**-0.5 if i == 0 else val).astype(BF)

    lane_head = lax.broadcasted_iota(jnp.int32, (1, wide), 1) // HEAD
    masks = [jnp.where(lane_head == h, 1.0, 0.0).astype(BF) for h in range(heads)]

    def stacked(value):
        return jnp.concatenate([value * mask for mask in masks], axis=0)

    def place_of(i):
        return pl.multiple_of(i * own, own)

    def window_of(i):
        return pl.multiple_of(jnp.clip(i - 1, 0, KEYS - 3) * own, own)

    def unstacked(value):
        parts = [value[h * HEAD : (h + 1) * HEAD, h * own : (h + 1) * own] for h in range(heads)]
        return jnp.concatenate(parts, axis=0).T

    def seen(layer, start):
        span = pl.ds(start, window)
        return (
            jnp.concatenate([pk[layer], qkv[layer, span, wide : 2 * wide]], axis=0),
            jnp.concatenate([pv[layer], qkv[layer, span, 2 * wide : 3 * wide]], axis=0),
        )

    def attend(layer, i):
        q4 = stacked(qkv[layer, pl.ds(place_of(i), own), 0:wide])
        key_rows, value_rows = seen(layer, window_of(i))
        s = dot_nt(key_rows, q4) + jnp.concatenate([bias[i]] * heads, axis=1)
        e = jnp.exp(s - jnp.max(s, axis=0, keepdims=True))
        p = e * (1.0 / jnp.sum(e, axis=0, keepdims=True))
        prob[layer, i] = p
        att[pl.ds(place_of(i), own), :] = unstacked(dot_tn(value_rows, p.astype(BF))).astype(BF)

    def attend_back(layer, i):
        at = pl.ds(place_of(i), own)
        q4 = stacked(qkv[layer, at, 0:wide])
        go4 = stacked(go[at, :])
        start = window_of(i)
        key_rows, value_rows = seen(layer, start)
        p = prob[layer, i]
        gp = dot_nt(value_rows, go4)
        dsum = jnp.sum(p * gp, axis=0, keepdims=True)
        gs = (p * (gp - dsum)).astype(BF)
        places = pl.ds(prefix + start, window)
        gk_here, gv_here = dot_nn(gs, q4), dot_nn(p.astype(BF), go4)
        gk[0:prefix, :] += gk_here[:prefix]
        gk[places, :] += gk_here[prefix:]
        gv[0:prefix, :] += gv_here[:prefix]
        gv[places, :] += gv_here[prefix:]
        gqkv[at, 0:wide] = (unstacked(dot_tn(key_rows, gs)).astype(BF).astype(F32) * HEAD**-0.5).astype(BF)

    def two(body, which):
        def one(i, carry):
            body(2 * which + i)
            return carry

        lax.fori_loop(0, 2, one, 0)

    def out_rows(layer, at, size):
        rows_here = rows_at(at, size)
        part[rows_here, :] = dot_nn(att[rows_here, :], wo[layer, columns, :]).astype(BF)

    def up_half(layer, n, which):
        hr = half_rows(which)
        u = dot_nn(full[n, hr, :], wu[layer])
        for at in range(0, half, 16):
            v = u[at : at + 16]
            phi_sum = 0.5 * (1.0 + lax.erf(v * 0.7071067811865476))
            density = jnp.exp(v * v * -0.5) * 0.3989422804014327
            here = rows_at(which * half + at, 16)
            hid[here, :] = (v * phi_sum).astype(BF)
            gelu_d[layer, here, :] = phi_sum + v * density

    def ff_back(layer, gradient, slope):
        gu = (dot_nn(gradient, wd[layer]) * slope).astype(BF)
        return dot_nt(gu, wu[layer]).astype(BF)

    def scatter_far(n, step, before=lambda i: None, early=False):
        for i in range(SUBS):
            before(i)
            if early and i > 0:
                rs_mid(n, i - 1)
            value = step(i)
            at_a, at_b = far_rows(i)
            part[at_b, :] = value[sub:]
            rs_copy(n, i).start()
            part[at_a, :] = value[:sub]
            if not early and i > 0:
                rs_mid(n, i - 1)
        rs_mid(n, SUBS - 1)

    def project_back(layer, at, size):
        rows_here = rows_at(at, size)
        part[rows_here, :] = dot_nt(gqkv[rows_here, :], wqkv[layer]).astype(BF)

    def norm_into(n, residual, layer, which, gain, shift, result, target):
        index = 2 * layer + which
        g, b = gain[layer : layer + 1, :], shift[layer : layer + 1, :]

        def body(i):
            value = residual[i : i + 16, :] + rs_sum(n, i)
            centre = value - jnp.mean(value, axis=-1, keepdims=True)
            inv = lax.rsqrt(jnp.mean(centre * centre, axis=-1, keepdims=True) + EPSILON)
            hat = centre * inv
            done = hat * g + b
            zhat[index, i : i + 16, :] = hat
            rinv[index, i : i + 16, :] = inv
            result[i : i + 16, :] = done
            full[target, rows_at(k * own + i, 16), :] = done.astype(BF)

        return body

    def into(n):
        def store(i, low):
            full[n, rows_at(k * own + i, 16), :] = low

        return store

    def norm_back(read, layer, which, gain, store):
        index = 2 * layer + which
        g = gain[layer : layer + 1, :]

        def body(i):
            scaled = read(i) * g
            hat = zhat[index, i : i + 16, :]
            inv = rinv[index, i : i + 16, :]
            first = jnp.mean(scaled, axis=-1, keepdims=True)
            second = jnp.mean(scaled * hat, axis=-1, keepdims=True)
            result = inv * (scaled - first - hat * second)
            own_g[i : i + 16, :] = result
            store(i, result.astype(BF))

        return body

    quarter = width // KEYS

    def quarter_copy(layer, i):
        at = (k, k, k, lax.rem(k + 2, KEYS))[i] * quarter + (quarter // 2 if i == 1 else 0)
        place = wo.at[layer, rows_at(at, quarter // 2 if i < 2 else quarter), :]
        return pltpu.make_async_remote_copy(
            src_ref=place, dst_ref=place, send_sem=wq_send.at[layer, i], recv_sem=wq_recv.at[layer, i],
            device_id=(across, across, sib, sib)[i], device_id_type=MESH,
        )

    def quarter_pass(layer):
        quarter_copy(layer, 0).wait_recv()
        quarter_copy(layer, 1).wait_recv()
        quarter_copy(layer, 3).start()

    def quarter_got(layer):
        quarter_copy(layer, 2).wait_recv()
        quarter_copy(layer, 3).wait_recv()

    def go_copy(d, i):
        kt = lax.rem(k + d, KEYS)
        return pltpu.make_async_remote_copy(
            src_ref=go_all.at[i * sub : (i + 1) * sub, pl.ds(pl.multiple_of(kt * wide, wide), wide)],
            dst_ref=go.at[rows_at(k * own + i * sub, sub), :],
            send_sem=go_send.at[d, i], recv_sem=go_recv.at[d, i], device_id=(r, kt), device_id_type=MESH,
        )

    def go_leave(layer):
        def leave(i):
            at = slice(i * sub, (i + 1) * sub)
            go_all[at, :] = dot_nt(ga[at, :], wo[layer]).astype(BF)
            for d in (2, *range(1, KEYS, 2)):
                go_copy(d, i).start()
            go[rows_at(k * own + i * sub, sub), :] = go_all[at, columns]

        return leave

    def go_wait(d):
        for i in range(SUBS):
            go_copy(d, i).wait_recv()

    def weights_at(layer, point):
        for kind, p, distance in SCHEDULE.get((layer, point), ()):
            if kind == "along":
                issue(p)
            elif kind == "beside":
                beside_own(p)
            elif kind == "swap":
                swap(p)
            else:
                passes(p, distance - 1, (kind == "up",))

    def forward_layer(layer):
        base = 4 * layer
        rs_a, rs_f = ((RS_A0, RS_F0), (RS_A1, RS_F1))[layer]
        ag_m = (AG_M0, AG_M1)[layer]
        source = tokens if layer == 0 else full.at[AG_X1]
        here = functools.partial(weights_at, layer)
        here("start")
        arrive(base)
        if layer > 0:
            arrive(base + 1)
            quarter_copy(layer, 0).start()
            ag_near(AG_X1)
        project(layer, source, near)
        here("projected near")
        if layer == 0:
            for i in range(2):
                pre_own(i).wait()
                for d in range(1, KEYS):
                    pre_copy(i, d).wait_recv()
        if layer > 0:
            ag_far(AG_X1)
        project(layer, source, far)
        here("projected")
        attend(layer, block_b)
        here("attended b")
        if layer == 0:
            arrive(base + 1)
        out_rows(layer, block_b * own, own)
        for i in range(SUBS):
            rs_copy(rs_a, i).start()
        here("out b")
        attend(layer, block_a)
        out_rows(layer, block_a * own, own)
        for i in range(SUBS):
            rs_mid(rs_a, i)
        here("out a")
        two(functools.partial(attend, layer), near)
        out_rows(layer, near * half, half)
        rs_near(rs_a)
        here("out near")
        rs_each(
            rs_a,
            norm_into(rs_a, own_x, layer, 0, g1, b1, own_m, ag_m),
            gather(ag_m),
            lambda i: here(f"norm {i}"),
        )
        here("normed")
        if layer == 0:
            quarter_copy(layer, 0).start()
        quarter_copy(layer, 1).start()
        quarter_copy(layer, 2).start()
        arrive(base + 2)
        ag_near(ag_m)
        here("up")
        up_half(layer, ag_m, near)
        here("up near")
        ag_far(ag_m)
        up_half(layer, ag_m, far)
        here("up far")
        arrive(base + 3)
        here("down")
        scatter_far(
            rs_f,
            lambda i: dot_nt(both(hid, at=far_rows(i)), wd[layer]).astype(BF),
            lambda i: here(f"down {i}"),
        )
        part[half_rows(near), :] = dot_nt(hid[half_rows(near), :], wd[layer]).astype(BF)
        rs_near(rs_f)
        if layer == 0:
            quarter_pass(0)
        here("down near")

    forward_layer(0)
    rs_each(
        RS_F0,
        norm_into(RS_F0, own_m, 0, 1, g2, b2, own_x, AG_X1),
        gather(AG_X1),
        lambda i: weights_at(0, f"last norm {i}"),
    )
    forward_layer(1)

    def prefix_copy(layer, i, d):
        kt = lax.rem(k + d, KEYS)
        source = (gk, gv)[i]
        return pltpu.make_async_remote_copy(
            src_ref=source.at[pl.ds(pl.multiple_of(kt * count, count), count), :],
            dst_ref=pg.at[layer, i, :, columns],
            send_sem=pg_send.at[i, d], recv_sem=pg_recv.at[i, d],
            device_id=(r, kt), device_id_type=MESH,
        )

    def prefix_own(layer, i):
        return pltpu.make_async_copy(
            (gk, gv)[i].at[pl.ds(pl.multiple_of(k * count, count), count), :],
            pg.at[layer, i, :, columns],
            pg_recv.at[i, 0],
        )

    bits = rows.bit_length() - 1

    def row_copy(layer, b):
        bit = 1 << b
        partner = r + bit - 2 * bit * lax.rem(r // bit, 2)
        return pltpu.make_async_remote_copy(
            src_ref=pg_low.at[layer], dst_ref=pg_in.at[layer, b],
            send_sem=pgr_send.at[layer, b], recv_sem=pgr_recv.at[layer, b],
            device_id=(partner, k), device_id_type=MESH,
        )

    def row_start(layer, b):
        low = pg[layer].astype(BF)
        pg_low[layer] = low
        pg[layer] = low.astype(F32)
        row_copy(layer, b).start()

    def row_step(layer, b):
        row_copy(layer, b).wait()
        pg[layer] += pg_in[layer, b].astype(F32)
        if b + 1 < bits:
            row_start(layer, b + 1)

    def prefix_start(layer):
        for i in range(2):
            prefix_own(layer, i).start()
            for d in range(1, KEYS):
                prefix_copy(layer, i, d).start()

    def prefix_take(layer):
        for i in range(2):
            prefix_own(layer, i).wait()
            for d in range(1, KEYS):
                prefix_copy(layer, i, d).wait_recv()
        row_start(layer, 0)

    def prefix_sent(layer):
        for i in range(2):
            for d in range(1, KEYS):
                prefix_copy(layer, i, d).wait_send()

    for layer in reversed(range(LAYERS)):
        rs_gm, rs_gx = ((RS_GM0, RS_GX0), (RS_GM1, RS_GX1))[layer]
        ag_gf = (AG_GF0, AG_GF1)[layer]
        if layer == LAYERS - 1:
            forth = norm_into(RS_F1, own_m, 1, 1, g2, b2, own_x, AG_ACT)
            back = norm_back(lambda i: cot[i : i + 16, :].astype(F32), layer, 1, g2, into(ag_gf))

            def turn(i):
                forth(i)
                back(i)

            rs_each(RS_F1, turn, gather(ag_gf))
        else:
            rs_each(
                RS_GX1,
                norm_back(lambda i: own_g[i : i + 16, :] + rs_sum(RS_GX1, i), layer, 1, g2, into(ag_gf)),
                gather(ag_gf),
            )
            prefix_take(layer + 1)
        ag_near(ag_gf)
        part[half_rows(near), :] = ff_back(layer, full[ag_gf, half_rows(near), :], gelu_d[layer, half_rows(near), :])
        rs_near(rs_gm)

        def step(i):
            ag_got(ag_gf, i)
            at = far_rows(i)
            return ff_back(layer, both(full, ag_gf, at=at), both(gelu_d, layer, at=at))

        if layer == LAYERS - 1:
            quarter_pass(layer)
        scatter_far(rs_gm, step, lambda i: ag_pass(ag_gf, i), early=True)
        if layer == 0:
            row_step(1, 0)
        gk[...] = jnp.zeros_like(gk)
        gv[...] = jnp.zeros_like(gv)
        quarter_got(layer)

        def keep(i, low):
            ga[i : i + 16, :] = low

        rs_each(
            rs_gm,
            norm_back(lambda i: own_g[i : i + 16, :] + rs_sum(rs_gm, i), layer, 0, g1, keep),
            go_leave(layer),
        )
        if layer == LAYERS - 1:
            for i in range(SUBS + 1):
                ag_copy(AG_ACT, i).start()
        go_wait(3 - 2 * c)
        two(functools.partial(attend_back, layer), near)
        if layer == 0:
            row_step(1, 1)
        go_wait(2)
        go_wait(1 + 2 * c)
        two(functools.partial(attend_back, layer), far)
        for d in range(1, KEYS):
            for i in range(SUBS):
                go_copy(d, i).wait_send()
        prefix_start(layer)

        def narrow(which):
            def body(i):
                i = which * half + i
                gqkv[rows_at(i, 16), wide : 2 * wide] = gk[rows_at(prefix + i, 16), :].astype(BF)
                gqkv[rows_at(i, 16), 2 * wide : 3 * wide] = gv[rows_at(prefix + i, 16), :].astype(BF)

            chunks(half, body)

        narrow(far)
        project_back(layer, block_b * own, own)
        for i in range(SUBS):
            rs_copy(rs_gx, i).start()
        project_back(layer, block_a * own, own)
        for i in range(SUBS):
            rs_mid(rs_gx, i)
        narrow(near)
        project_back(layer, near * half, half)
        rs_near(rs_gx)
        if layer == LAYERS - 1:
            ag_far(AG_ACT)
            ag_near(AG_ACT)
        else:
            for b in range(2, bits):
                row_step(1, b)
            prefix_take(0)
        prefix_sent(layer)

    act_copy = pltpu.make_async_copy(full.at[AG_ACT], low_out.at[1], loc.at[13])
    act_copy.start()

    def last(i):
        full[AG_GX, rows_at(k * own + i, 16), :] = (own_g[i : i + 16, :] + rs_sum(RS_GX0, i)).astype(BF)

    rs_each(RS_GX0, last, gather(AG_GX), lambda i: row_step(0, 0) if i == SUBS - 1 else None)
    for p in range(4 * LAYERS):
        drain(p)
    for i in range(2):
        for d in range(1, KEYS):
            pre_copy(i, d).wait_send()
    ag_near(AG_GX)

    def grad_copy(which):
        return pltpu.make_async_copy(
            full.at[AG_GX, half_rows(which), :], low_out.at[0, half_rows(which), :], loc.at[14 + (which is far)]
        )

    grad_copy(near).start()
    ag_far(AG_GX, lambda: row_step(0, 1))
    grad_copy(far).start()
    for b in range(2, bits):
        row_step(0, b)
    for i in range(2):
        for layer in range(LAYERS):
            prefix_out[i, layer] = pg[layer, i]
    ag_end(AG_GX)
    ag_end(AG_ACT)
    for layer in range(LAYERS):
        for i in range(4):
            quarter_copy(layer, i).wait_send()
    act_copy.wait()
    grad_copy(near).wait()
    grad_copy(far).wait()


def results(low, grads, act, gt, gpk, gpv, narrow, broad, act_held, grads_held, sems):
    parts, size = narrow.shape[:2]

    def taken(i):
        return pltpu.make_async_copy(low.at[0, i * size : (i + 1) * size, :], narrow.at[i], sems.at[0, i])

    def given(i):
        return pltpu.make_async_copy(broad.at[i], gt.at[0, i * size : (i + 1) * size, :], sems.at[1, i])

    in_act = pltpu.make_async_copy(low.at[1], act_held, sems.at[2, 0])
    out_act = pltpu.make_async_copy(act_held, act.at[0], sems.at[2, 0])
    in_grads = pltpu.make_async_copy(grads, grads_held, sems.at[2, 1])
    out_grads = [pltpu.make_async_copy(grads_held.at[i], (gpk, gpv)[i], sems.at[2, 2 + i]) for i in range(2)]
    for i in range(parts):
        taken(i).start()
    in_act.start()
    in_grads.start()
    for i in range(parts):
        taken(i).wait()
        broad[i] = narrow[i].astype(F32)
        given(i).start()
    in_act.wait()
    out_act.start()
    in_grads.wait()
    for copy in out_grads:
        copy.start()
    for i in range(parts):
        given(i).wait()
    out_act.wait()
    for copy in out_grads:
        copy.wait()


def per_device(
    tokens, cotangent, segment_ids, pad_mask, prefix_keys, prefix_values,
    w_query, w_key, w_value, w_out, w_up, w_down_t,
    norm1_gain, norm1_bias, norm2_gain, norm2_bias,
):
    rows, keys = lax.axis_size("rows"), lax.axis_size("keys")
    assert keys == KEYS and rows % (2 * KEYS) == 0 and rows & (rows - 1) == 0
    tok, width = tokens.shape[1:]
    count = prefix_keys.shape[1]
    prefix = count * keys
    local_ff = w_up.shape[2]
    wide, own, window = width // keys, tok // keys, 3 * tok // keys
    heads = wide // HEAD
    nz, bits, pieces = rows // 2, rows.bit_length() - 1, 4 * LAYERS
    vmem, anywhere = pl.BlockSpec(memory_space=pltpu.VMEM), pl.BlockSpec(memory_space=pl.ANY)
    dma = pltpu.SemaphoreType.DMA
    scratch = [
        pltpu.VMEM((LAYERS, width, 3 * wide), BF),
        pltpu.VMEM((LAYERS, width, width), BF),
        pltpu.VMEM((LAYERS, width, local_ff), BF),
        pltpu.VMEM((LAYERS, width, local_ff), BF),
        pltpu.VMEM((LAYERS, prefix, wide), BF),
        pltpu.VMEM((LAYERS, prefix, wide), BF),
        pltpu.VMEM((tok, width), BF),
        pltpu.VMEM((SCATTERS, 2, own, width), BF),
        pltpu.VMEM((SCATTERS, own, width), BF),
        pltpu.VMEM((own, width), BF),
        pltpu.VMEM((GATHERS, tok, width), BF),
        pltpu.VMEM((LAYERS, tok, 3 * wide), BF),
        pltpu.VMEM((LAYERS, keys, prefix + window, heads * own), F32),
        pltpu.VMEM((LAYERS, tok, local_ff), F32),
        pltpu.VMEM((2 * LAYERS, own, width), F32),
        pltpu.VMEM((2 * LAYERS, own, 1), F32),
        pltpu.VMEM((own, width), F32),
        pltpu.VMEM((own, width), F32),
        pltpu.VMEM((own, width), F32),
        pltpu.VMEM((own, width), BF),
        pltpu.VMEM((tok, wide), BF),
        pltpu.VMEM((tok, 3 * wide), BF),
        pltpu.VMEM((prefix + tok, wide), F32),
        pltpu.VMEM((prefix + tok, wide), F32),
        pltpu.VMEM((tok, width), BF),
        pltpu.VMEM((tok, local_ff), BF),
        pltpu.VMEM((own, width), BF),
        pltpu.VMEM((own, width), BF),
        pltpu.VMEM((tok, wide), BF),
        pltpu.VMEM((keys, prefix + window, own), F32),
        pltpu.VMEM((tok, own), F32),
        pltpu.VMEM((LAYERS, 2, count, width), F32),
        pltpu.VMEM((LAYERS, 2, count, width), BF),
        pltpu.VMEM((LAYERS, bits, 2, count, width), BF),
        dma((pieces, 2, nz + 1)),
        dma((pieces, 2, nz)),
        dma((pieces, nz)),
        dma((16,)),
        dma((2, keys)),
        dma((2, keys)),
        dma((LAYERS, 4)),
        dma((LAYERS, 4)),
        dma((keys, SUBS)),
        dma((keys, SUBS)),
        dma((2 * SUBS + 1,)),
        dma((2 * SUBS + 1,)),
        dma((2, 2 * SUBS + 1)),
        dma((2, 2 * SUBS + 1)),
        dma((2, keys)),
        dma((2, keys)),
        dma((LAYERS, bits)),
        dma((LAYERS, bits)),
    ]
    low, grads = pl.pallas_call(
        functools.partial(kernel, (rows, tok, width, local_ff)),
        out_shape=(
            jax.ShapeDtypeStruct((2, tok, width), BF),
            jax.ShapeDtypeStruct((2, LAYERS, count, width), F32),
        ),
        in_specs=[anywhere, anywhere, vmem, vmem] + [anywhere] * 8 + [vmem] * 4,
        out_specs=(anywhere, vmem),
        scratch_shapes=scratch,
        compiler_params=pltpu.CompilerParams(
            collective_id=0, has_side_effects=True, vmem_limit_bytes=62 * 1024 * 1024 - 512 * 1024
        ),
    )(
        tokens[0], cotangent[0], segment_ids, pad_mask, prefix_keys, prefix_values,
        w_query, w_key, w_value, w_out, w_up, w_down_t,
        norm1_gain, norm1_bias, norm2_gain, norm2_bias,
    )
    whole = (LAYERS, count, width)
    return pl.pallas_call(
        results,
        out_shape=(
            jax.ShapeDtypeStruct((1, tok, width), BF),
            jax.ShapeDtypeStruct((1, tok, width), F32),
            jax.ShapeDtypeStruct(whole, F32),
            jax.ShapeDtypeStruct(whole, F32),
        ),
        in_specs=[anywhere] * 2,
        out_specs=(anywhere,) * 4,
        scratch_shapes=[
            pltpu.VMEM((2 * keys, own // 2, width), BF),
            pltpu.VMEM((2 * keys, own // 2, width), F32),
            pltpu.VMEM((tok, width), BF),
            pltpu.VMEM((2, *whole), F32),
            dma((3, 2 * keys)),
        ],
    )(low, grads)


def solution(mesh):
    row3 = P("rows", None, None)
    weight = P(None, "rows", None)
    return jax.shard_map(
        per_device,
        mesh=mesh,
        in_specs=(
            row3,
            row3,
            P("rows", None),
            P("rows", None),
            P(None, "keys", None),
            P(None, "keys", None),
            weight,
            weight,
            weight,
            weight,
            P(None, "rows", "keys"),
            P(None, "rows", "keys"),
            P(),
            P(),
            P(),
            P(),
        ),
        out_specs=(row3, row3, P(None, "keys", None), P(None, "keys", None)),
        check_vma=False,
    )
```

```python
import functools

import jax
import jax.numpy as jnp
from jax import lax
from jax.experimental import pallas as pl
from jax.experimental.pallas import tpu as pltpu
from jax.sharding import PartitionSpec as P

HEAD = 64
LAYERS = 2
KEYS = 4
EPSILON = 1e-05
NEGATIVE = -1000000000.0
MESH = pl.DeviceIdType.MESH
BF = jnp.bfloat16
F32 = jnp.float32

AG_M0, AG_X1, AG_M1, AG_GF1, AG_GF0, AG_GX, AG_ACT = range(7)
GATHERS = 7
RS_A0, RS_F0, RS_A1, RS_F1, RS_GM1, RS_GX1, RS_GM0, RS_GX0 = range(8)
SCATTERS = 8
GATHER_BEFORE = (None, AG_M0, AG_X1, AG_M1, AG_GF1, None, AG_GF0, None)
SUBS = 2

SCHEDULE = {
    (0, "start"): (
        ("beside", 1, 0),
        ("beside", 7, 0),
        ("along", 1, 0),
        ("beside", 2, 0),
        ("along", 0, 0),
        ("down", 1, 1),
        ("along", 4, 0),
        ("up", 1, 1),
        ("down", 0, 1),
        ("up", 0, 1),
        ("up", 1, 2),
        ("down", 1, 2),
        ("along", 2, 0),
        ("up", 0, 2),
        ("up", 1, 3),
        ("beside", 0, 0),
        ("down", 0, 2),
        ("up", 2, 1),
        ("down", 1, 3),
        ("down", 2, 1),
        ("up", 0, 3),
        ("along", 5, 0),
        ("up", 2, 2),
        ("down", 0, 3),
        ("along", 3, 0),
        ("down", 2, 2),
        ("up", 2, 3),
        ("down", 3, 1),
        ("down", 5, 1),
        ("up", 3, 1),
        ("up", 3, 2),
    ),
    (0, "attended b"): (
        ("up", 5, 2),
    ),
    (0, "out b"): (
        ("beside", 5, 0),
        ("up", 5, 1),
        ("along", 6, 0),
    ),
    (0, "out a"): (
        ("beside", 3, 0),
        ("down", 3, 2),
        ("down", 5, 2),
        ("down", 2, 3),
    ),
    (0, "norm 1"): (
        ("up", 4, 1),
        ("up", 3, 3),
        ("up", 4, 2),
        ("down", 4, 1),
    ),
    (0, "normed"): (
        ("up", 4, 3),
        ("swap", 7, 0),
    ),
    (0, "up"): (
        ("down", 3, 3),
        ("down", 4, 2),
    ),
    (0, "up far"): (
        ("along", 7, 0),
    ),
    (0, "down 0"): (
        ("beside", 4, 0),
        ("up", 6, 1),
    ),
    (0, "down 1"): (
        ("down", 5, 3),
        ("up", 5, 3),
    ),
    (0, "last norm 0"): (
        ("down", 4, 3),
        ("down", 6, 1),
    ),
    (0, "last norm 1"): (
        ("up", 6, 2),
        ("down", 6, 2),
    ),
    (1, "start"): (
        ("beside", 6, 0),
        ("down", 7, 1),
    ),
    (1, "projected near"): (
        ("up", 7, 1),
    ),
    (1, "out b"): (
        ("up", 6, 3),
    ),
    (1, "out a"): (
        ("down", 6, 3),
    ),
    (1, "norm 0"): (
        ("down", 7, 2),
    ),
    (1, "norm 1"): (
        ("up", 7, 2),
    ),
    (1, "up far"): (
        ("up", 7, 3),
        ("down", 7, 3),
    ),
}
STRAIGHT = (7,)


def dot_nn(a, b):
    return lax.dot_general(a, b, (((1,), (0,)), ((), ())), preferred_element_type=F32)


def dot_nt(a, b):
    return lax.dot_general(a, b, (((1,), (1,)), ((), ())), preferred_element_type=F32)


def dot_tn(a, b):
    return lax.dot_general(a, b, (((0,), (0,)), ((), ())), preferred_element_type=F32)


def kernel(
    dims,
    token_rows, cotangent, segments, padding, pre_k, pre_v,
    w_query, w_key, w_value, w_out, w_up, w_down,
    g1, b1, g2, b2,
    low_out, prefix_out,
    wqkv, wo, wu, wd, pk, pv,
    part, rc, ry, ys, full,
    qkv, prob, gelu_d, zhat, rinv,
    own_x, own_m, own_g, cot, att, gqkv, gk, gv, tokens, hid, ga, go_all, go, bias, codes,
    pg, pg_low, pg_in,
    w_send, w_recv, w_over, loc, pre_send, pre_recv,
    wq_send, wq_recv, go_send, go_recv,
    rs_send, rs_recv, ag_send, ag_recv, pg_send, pg_recv, pgr_send, pgr_recv,
):
    rows, tok, width, local_ff = dims
    nz = rows // 2
    wide = width // KEYS
    heads = wide // HEAD
    own = tok // KEYS
    half = tok // 2
    depth = width // rows
    count = pre_k.shape[1]
    prefix = KEYS * count
    window = 3 * own

    r = lax.axis_index("rows")
    k = lax.axis_index("keys")
    z, x = r // 2, lax.rem(r, 2)
    y, c = k // 2, lax.rem(k, 2)
    sib = (r, k + 1 - 2 * c)
    across = (r, lax.rem(k + 2, KEYS))
    beside = (r + 1 - 2 * x, k)
    far, near = 1 - y, y

    barrier = pltpu.get_barrier_semaphore()

    def greet(zz):
        pl.semaphore_signal(barrier, inc=1, device_id=(zz * 2 + x, k), device_id_type=MESH)

    not_top, not_bottom = z < nz - 1, z > 0
    pl.when(not_top)(lambda: greet(lax.rem(z + 1, nz)))
    pl.when(not_bottom)(lambda: greet(lax.rem(z + nz - 1, nz)))
    far_partners = [1 << b for b in range(1, nz.bit_length() - 1)]
    for bit in far_partners:
        greet(z + bit - 2 * bit * lax.rem(z // bit, 2))
    pl.semaphore_signal(barrier, inc=1, device_id=beside, device_id_type=MESH)
    for d in range(1, KEYS):
        pl.semaphore_signal(barrier, inc=1, device_id=(r, lax.rem(k + d, KEYS)), device_id_type=MESH)

    group = nz // KEYS

    def spot(ref, layer, at):
        return ref.at[layer, pl.ds(pl.multiple_of(at * depth, depth), depth), :]

    def slot(p, zz, xx):
        layer, kind = divmod(p, 4)
        at = zz * 2 + xx
        return spot((wqkv, wo, wu, wd)[kind], layer, at)

    def active(p, zz):
        return None if p % 4 != 1 else (zz // group) == k

    def guarded(condition, action):
        if condition is None:
            action()
        else:
            pl.when(condition)(action)

    columns = pl.ds(pl.multiple_of(k * wide, wide), wide)

    def own_copies(p):
        layer, kind = divmod(p, 4)
        if kind == 0:
            place = pl.ds(pl.multiple_of(r * depth, depth), depth)
            return [
                pltpu.make_async_copy(
                    w.at[layer, :, columns], wqkv.at[layer, place, i * wide : (i + 1) * wide], loc.at[6 * layer + i]
                )
                for i, w in enumerate((w_query, w_key, w_value))
            ]
        source = (None, w_out, w_up, w_down)[kind]
        return [pltpu.make_async_copy(source.at[layer], slot(p, z, x), loc.at[6 * layer + 2 + kind])]

    def own_start(p):
        guarded(active(p, z), lambda: [copy.start() for copy in own_copies(p)] and None)

    def own_wait(p):
        guarded(active(p, z), lambda: [copy.wait() for copy in own_copies(p)] and None)

    def push(p, zz, xx, send_sem, target):
        place = slot(p, zz, xx)
        return pltpu.make_async_remote_copy(
            src_ref=place, dst_ref=place, send_sem=send_sem, recv_sem=w_recv.at[p, xx, zz],
            device_id=target, device_id_type=MESH,
        )

    def straight(p):
        return p in STRAIGHT

    def up(p, zz, xx):
        return push(p, zz, xx, w_send.at[p if xx is x else 4 * LAYERS, zz], (lax.rem(z + 1, nz) * 2 + x, k))

    def down(p, zz, xx):
        sem = w_send.at[p if xx is x else 4 * LAYERS, jnp.where(zz == z, nz, zz)]
        return push(p, zz, xx, sem, (lax.rem(z + nz - 1, nz) * 2 + x, k))

    def over(p, zz):
        return push(p, zz, x, w_over.at[p, zz], beside)

    def spread_own(p, xx, action):
        pl.when(not_top)(lambda: action(up(p, z, xx)))
        pl.when(not_bottom)(lambda: action(down(p, z, xx)))

    def begin(copy):
        copy.start()

    def sent(copy):
        copy.wait_send()

    def issue(p):
        guarded(active(p, z), lambda: spread_own(p, x, begin))

    def beside_own(p):
        guarded(active(p, z), lambda: over(p, z).start())

    def swap(p):
        over_in = push(p, z, 1 - x, w_over.at[p, z], beside)
        over_in.wait_recv()
        spread_own(p, 1 - x, begin)

    def hops(group, action, sides=(True, False)):
        bounds = [1 + (nz - 1) * i // 3 for i in range(4)]

        def one(j, carry):
            if True in sides:
                pl.when(z - j >= 0)(lambda: action(jnp.maximum(z - j, 0), True))
            if False in sides:
                pl.when(z + j < nz)(lambda: action(jnp.minimum(z + j, nz - 1), False))
            return carry

        lax.fori_loop(bounds[group], bounds[group + 1], one, 0)

    def onward(p, zz, xx, below, action):
        if below:
            pl.when(not_top)(lambda: action(up(p, zz, xx)))
        else:
            pl.when(not_bottom)(lambda: action(down(p, zz, xx)))

    def passes(p, group, sides):
        def action(zz, below):
            def take():
                for xx in (x, 1 - x) if straight(p) else (x,):
                    push(p, zz, xx, w_over.at[p, zz], beside).wait_recv()
                    onward(p, zz, xx, below, begin)
                if not straight(p):
                    over(p, zz).start()

            guarded(active(p, zz), take)

        hops(group, action, sides)

    def arrive(p):
        if straight(p):
            return

        def one(zz, carry):
            guarded(active(p, zz), push(p, zz, 1 - x, w_over.at[p, zz], beside).wait_recv)
            return carry

        lax.fori_loop(0, nz, one, 0)

    def drain(p):
        def mine():
            spread_own(p, x, sent)
            if straight(p):
                spread_own(p, 1 - x, sent)
            over(p, z).wait_send()

        guarded(active(p, z), mine)

        def action(zz, below):
            def passed():
                for xx in (x, 1 - x) if straight(p) else (x,):
                    onward(p, zz, xx, below, sent)
                if not straight(p):
                    over(p, zz).wait_send()

            guarded(active(p, zz), passed)

        for group_at in range(3):
            hops(group_at, action)

    def pre_copy(i, d):
        kt = lax.rem(k + d, KEYS)
        source, target = ((pre_k, pk), (pre_v, pv))[i]
        return pltpu.make_async_remote_copy(
            src_ref=source.at[:, :, pl.ds(pl.multiple_of(kt * wide, wide), wide)],
            dst_ref=target.at[:, pl.ds(pl.multiple_of(k * count, count), count), :],
            send_sem=pre_send.at[i, d], recv_sem=pre_recv.at[i, d], device_id=(r, kt), device_id_type=MESH,
        )

    def pre_own(i):
        source, target = ((pre_k, pk), (pre_v, pv))[i]
        return pltpu.make_async_copy(
            source.at[:, :, columns],
            target.at[:, pl.ds(pl.multiple_of(k * count, count), count), :],
            pre_recv.at[i, 0],
        )

    own_block = pl.ds(pl.multiple_of(k * own, own), own)
    cot_copy = pltpu.make_async_copy(cotangent.at[own_block, :], cot, loc.at[12])

    for p in range(4 * LAYERS):
        own_start(p)
    cot_copy.start()
    token_copy = pltpu.make_async_copy(token_rows, tokens, loc.at[13])
    token_copy.start()
    for i in range(2):
        pre_own(i).start()

    visible_code = jnp.where(padding[...] == 1, segments[...], -1).astype(F32)
    codes[...] = jnp.broadcast_to(visible_code, (own, tok)).T

    def mask_of(i, carry):
        queries = segments[:, pl.ds(pl.multiple_of(i * own, own), own)].astype(F32)
        keys_code = codes[pl.ds(pl.multiple_of(jnp.clip(i - 1, 0, KEYS - 3) * own, own), window), :]
        bias[i, 0:prefix, :] = jnp.zeros((prefix, own), F32)
        bias[i, prefix : prefix + window, :] = jnp.where(keys_code == queries, 0.0, NEGATIVE)
        return carry

    lax.fori_loop(0, KEYS, mask_of, 0)

    def widen(i, carry):
        at = pl.multiple_of(i * 16, 16)
        own_x[pl.ds(at, 16), :] = tokens[pl.ds(k * own + at, 16), :].astype(F32)
        return carry

    token_copy.wait()
    lax.fori_loop(0, own // 16, widen, 0)
    ends = jnp.where(z == 0, 1, 0) + jnp.where(z == nz - 1, 1, 0)
    pl.semaphore_wait(barrier, 2 - ends + len(far_partners) + 1 + KEYS - 1)
    own_wait(0)
    for i in range(2):
        for d in range(1, KEYS):
            pre_copy(i, d).start()
    for p in range(1, 4 * LAYERS):
        own_wait(p)
    cot_copy.wait()

    sub = own // SUBS
    block_a, block_b = 2 * far + c, 2 * far + 1 - c

    def rows_at(at, size):
        return pl.ds(pl.multiple_of(at, 16), size)

    def rs_copy(n, i):
        if i < SUBS:
            source, target = part.at[rows_at(block_b * own + i * sub, sub), :], rc.at[n, 0, i * sub : (i + 1) * sub, :]
        elif i == SUBS:
            source, target = part.at[rows_at((2 * near + 1 - c) * own, own), :], rc.at[n, 1]
        else:
            at = slice((i - SUBS - 1) * sub, (i - SUBS) * sub)
            source, target = ys.at[at, :], ry.at[n, at, :]
        return pltpu.make_async_remote_copy(
            src_ref=source, dst_ref=target, send_sem=rs_send.at[i], recv_sem=rs_recv.at[i],
            device_id=sib if i <= SUBS else across, device_id_type=MESH,
        )

    def chunks(total, body, size=16):
        def one(i, carry):
            body(pl.multiple_of(i * size, size))
            return carry

        lax.fori_loop(0, total // size, one, 0)

    def rs_mid(n, i):
        rs_copy(n, i).wait_recv()
        for at in range(i * sub, (i + 1) * sub, 16):
            mine = part[rows_at(block_a * own + at, 16), :].astype(F32)
            ys[at : at + 16, :] = (mine + rc[n, 0, at : at + 16, :].astype(F32)).astype(BF)
        rs_copy(n, SUBS + 1 + i).start()

    def rs_near(n):
        rs_copy(n, SUBS).start()

    def rs_sum(n, at):
        mine = part[rows_at(k * own + at, 16), :].astype(F32) + rc[n, 1, at : at + 16, :].astype(F32)
        return mine + ry[n, at : at + 16, :].astype(F32)

    def rs_each(n, body, leave, between=lambda i: None):
        if GATHER_BEFORE[n] is not None:
            ag_end(GATHER_BEFORE[n])
        rs_copy(n, SUBS).wait_recv()
        for i in range(SUBS):
            between(i)
            rs_copy(n, SUBS + 1 + i).wait_recv()
            for at in range(i * sub, (i + 1) * sub, 16):
                body(at)
            leave(i)
        rs_end(n)

    def gather(n):
        def leave(i):
            ag_copy(n, i).start()
            if i == SUBS - 1:
                ag_copy(n, SUBS).start()

        return leave

    def rs_end(n):
        for i in range(2 * SUBS + 1):
            rs_copy(n, i).wait_send()

    def ag_copy(n, i):
        if i < SUBS:
            place, device = full.at[n, rows_at(k * own + i * sub, sub), :], across
        elif i == SUBS:
            place, device = full.at[n, rows_at(k * own, own), :], sib
        else:
            place, device = full.at[n, rows_at(block_a * own + (i - SUBS - 1) * sub, sub), :], sib
        return pltpu.make_async_remote_copy(
            src_ref=place, dst_ref=place, send_sem=ag_send.at[n // AG_ACT, i], recv_sem=ag_recv.at[n // AG_ACT, i],
            device_id=device, device_id_type=MESH,
        )

    def ag_end(n):
        for i in range(2 * SUBS + 1):
            ag_copy(n, i).wait_send()

    def ag_near(n):
        ag_copy(n, SUBS).wait_recv()

    def ag_pass(n, i):
        ag_copy(n, i).wait_recv()
        ag_copy(n, SUBS + 1 + i).start()

    def ag_got(n, i):
        ag_copy(n, SUBS + 1 + i).wait_recv()

    def ag_far(n, between=lambda: None):
        for i in range(SUBS):
            ag_pass(n, i)
            if i == 0:
                between()
        for i in range(SUBS):
            ag_got(n, i)

    def half_rows(which):
        return pl.ds(pl.multiple_of(which * half, half), half)

    def far_rows(i):
        return rows_at(block_a * own + i * sub, sub), rows_at(block_b * own + i * sub, sub)

    def both(ref, *lead, at):
        return jnp.concatenate([ref[(*lead, rows, slice(None))] for rows in at], axis=0)

    def project(layer, source, which):
        hr = half_rows(which)
        xin = source[hr, :]
        for i in range(3):
            at = slice(i * wide, (i + 1) * wide)
            val = dot_nn(xin, wqkv[layer, :, at])
            qkv[layer, hr, at] = (val * HEAD**-0.5 if i == 0 else val).astype(BF)

    lane_head = lax.broadcasted_iota(jnp.int32, (1, wide), 1) // HEAD
    masks = [jnp.where(lane_head == h, 1.0, 0.0).astype(BF) for h in range(heads)]

    def stacked(value):
        return jnp.concatenate([value * mask for mask in masks], axis=0)

    def place_of(i):
        return pl.multiple_of(i * own, own)

    def window_of(i):
        return pl.multiple_of(jnp.clip(i - 1, 0, KEYS - 3) * own, own)

    def unstacked(value):
        parts = [value[h * HEAD : (h + 1) * HEAD, h * own : (h + 1) * own] for h in range(heads)]
        return jnp.concatenate(parts, axis=0).T

    def seen(layer, start):
        span = pl.ds(start, window)
        return (
            jnp.concatenate([pk[layer], qkv[layer, span, wide : 2 * wide]], axis=0),
            jnp.concatenate([pv[layer], qkv[layer, span, 2 * wide : 3 * wide]], axis=0),
        )

    def attend(layer, i):
        q4 = stacked(qkv[layer, pl.ds(place_of(i), own), 0:wide])
        key_rows, value_rows = seen(layer, window_of(i))
        s = dot_nt(key_rows, q4) + jnp.concatenate([bias[i]] * heads, axis=1)
        e = jnp.exp(s - jnp.max(s, axis=0, keepdims=True))
        p = e * (1.0 / jnp.sum(e, axis=0, keepdims=True))
        prob[layer, i] = p
        att[pl.ds(place_of(i), own), :] = unstacked(dot_tn(value_rows, p.astype(BF))).astype(BF)

    def attend_back(layer, i):
        at = pl.ds(place_of(i), own)
        q4 = stacked(qkv[layer, at, 0:wide])
        go4 = stacked(go[at, :])
        start = window_of(i)
        key_rows, value_rows = seen(layer, start)
        p = prob[layer, i]
        gp = dot_nt(value_rows, go4)
        dsum = jnp.sum(p * gp, axis=0, keepdims=True)
        gs = (p * (gp - dsum)).astype(BF)
        places = pl.ds(prefix + start, window)
        gk_here, gv_here = dot_nn(gs, q4), dot_nn(p.astype(BF), go4)
        gk[0:prefix, :] += gk_here[:prefix]
        gk[places, :] += gk_here[prefix:]
        gv[0:prefix, :] += gv_here[:prefix]
        gv[places, :] += gv_here[prefix:]
        gqkv[at, 0:wide] = (unstacked(dot_tn(key_rows, gs)).astype(BF).astype(F32) * HEAD**-0.5).astype(BF)

    def two(body, which):
        def one(i, carry):
            body(2 * which + i)
            return carry

        lax.fori_loop(0, 2, one, 0)

    def out_rows(layer, at, size):
        rows_here = rows_at(at, size)
        part[rows_here, :] = dot_nn(att[rows_here, :], wo[layer, columns, :]).astype(BF)

    def up_half(layer, n, which):
        hr = half_rows(which)
        u = dot_nn(full[n, hr, :], wu[layer])
        for at in range(0, half, 16):
            v = u[at : at + 16]
            phi_sum = 0.5 * (1.0 + lax.erf(v * 0.7071067811865476))
            density = jnp.exp(v * v * -0.5) * 0.3989422804014327
            here = rows_at(which * half + at, 16)
            hid[here, :] = (v * phi_sum).astype(BF)
            gelu_d[layer, here, :] = phi_sum + v * density

    def ff_back(layer, gradient, slope):
        gu = (dot_nn(gradient, wd[layer]) * slope).astype(BF)
        return dot_nt(gu, wu[layer]).astype(BF)

    def scatter_far(n, step, before=lambda i: None, early=False):
        for i in range(SUBS):
            before(i)
            if early and i > 0:
                rs_mid(n, i - 1)
            value = step(i)
            at_a, at_b = far_rows(i)
            part[at_b, :] = value[sub:]
            rs_copy(n, i).start()
            part[at_a, :] = value[:sub]
            if not early and i > 0:
                rs_mid(n, i - 1)
        rs_mid(n, SUBS - 1)

    def project_back(layer, at, size):
        rows_here = rows_at(at, size)
        part[rows_here, :] = dot_nt(gqkv[rows_here, :], wqkv[layer]).astype(BF)

    def norm_into(n, residual, layer, which, gain, shift, result, target):
        index = 2 * layer + which
        g, b = gain[layer : layer + 1, :], shift[layer : layer + 1, :]

        def body(i):
            value = residual[i : i + 16, :] + rs_sum(n, i)
            centre = value - jnp.mean(value, axis=-1, keepdims=True)
            inv = lax.rsqrt(jnp.mean(centre * centre, axis=-1, keepdims=True) + EPSILON)
            hat = centre * inv
            done = hat * g + b
            zhat[index, i : i + 16, :] = hat
            rinv[index, i : i + 16, :] = inv
            result[i : i + 16, :] = done
            full[target, rows_at(k * own + i, 16), :] = done.astype(BF)

        return body

    def into(n):
        def store(i, low):
            full[n, rows_at(k * own + i, 16), :] = low

        return store

    def norm_back(read, layer, which, gain, store):
        index = 2 * layer + which
        g = gain[layer : layer + 1, :]

        def body(i):
            scaled = read(i) * g
            hat = zhat[index, i : i + 16, :]
            inv = rinv[index, i : i + 16, :]
            first = jnp.mean(scaled, axis=-1, keepdims=True)
            second = jnp.mean(scaled * hat, axis=-1, keepdims=True)
            result = inv * (scaled - first - hat * second)
            own_g[i : i + 16, :] = result
            store(i, result.astype(BF))

        return body

    quarter = width // KEYS

    def quarter_copy(layer, i):
        at = (k, k, k, lax.rem(k + 2, KEYS))[i] * quarter + (quarter // 2 if i == 1 else 0)
        place = wo.at[layer, rows_at(at, quarter // 2 if i < 2 else quarter), :]
        return pltpu.make_async_remote_copy(
            src_ref=place, dst_ref=place, send_sem=wq_send.at[layer, i], recv_sem=wq_recv.at[layer, i],
            device_id=(across, across, sib, sib)[i], device_id_type=MESH,
        )

    def quarter_pass(layer):
        quarter_copy(layer, 0).wait_recv()
        quarter_copy(layer, 1).wait_recv()
        quarter_copy(layer, 3).start()

    def quarter_got(layer):
        quarter_copy(layer, 2).wait_recv()
        quarter_copy(layer, 3).wait_recv()

    def go_copy(d, i):
        kt = lax.rem(k + d, KEYS)
        return pltpu.make_async_remote_copy(
            src_ref=go_all.at[i * sub : (i + 1) * sub, pl.ds(pl.multiple_of(kt * wide, wide), wide)],
            dst_ref=go.at[rows_at(k * own + i * sub, sub), :],
            send_sem=go_send.at[d, i], recv_sem=go_recv.at[d, i], device_id=(r, kt), device_id_type=MESH,
        )

    def go_leave(layer):
        def leave(i):
            at = slice(i * sub, (i + 1) * sub)
            go_all[at, :] = dot_nt(ga[at, :], wo[layer]).astype(BF)
            for d in (2, *range(1, KEYS, 2)):
                go_copy(d, i).start()
            go[rows_at(k * own + i * sub, sub), :] = go_all[at, columns]

        return leave

    def go_wait(d):
        for i in range(SUBS):
            go_copy(d, i).wait_recv()

    def weights_at(layer, point):
        for kind, p, distance in SCHEDULE.get((layer, point), ()):
            if kind == "along":
                issue(p)
            elif kind == "beside":
                beside_own(p)
            elif kind == "swap":
                swap(p)
            else:
                passes(p, distance - 1, (kind == "up",))

    def forward_layer(layer):
        base = 4 * layer
        rs_a, rs_f = ((RS_A0, RS_F0), (RS_A1, RS_F1))[layer]
        ag_m = (AG_M0, AG_M1)[layer]
        source = tokens if layer == 0 else full.at[AG_X1]
        here = functools.partial(weights_at, layer)
        here("start")
        arrive(base)
        if layer > 0:
            arrive(base + 1)
            quarter_copy(layer, 0).start()
            ag_near(AG_X1)
        project(layer, source, near)
        here("projected near")
        if layer == 0:
            for i in range(2):
                pre_own(i).wait()
                for d in range(1, KEYS):
                    pre_copy(i, d).wait_recv()
        if layer > 0:
            ag_far(AG_X1)
        project(layer, source, far)
        here("projected")
        attend(layer, block_b)
        here("attended b")
        if layer == 0:
            arrive(base + 1)
        out_rows(layer, block_b * own, own)
        for i in range(SUBS):
            rs_copy(rs_a, i).start()
        here("out b")
        attend(layer, block_a)
        out_rows(layer, block_a * own, own)
        for i in range(SUBS):
            rs_mid(rs_a, i)
        here("out a")
        two(functools.partial(attend, layer), near)
        out_rows(layer, near * half, half)
        rs_near(rs_a)
        here("out near")
        rs_each(
            rs_a,
            norm_into(rs_a, own_x, layer, 0, g1, b1, own_m, ag_m),
            gather(ag_m),
            lambda i: here(f"norm {i}"),
        )
        here("normed")
        if layer == 0:
            quarter_copy(layer, 0).start()
        quarter_copy(layer, 1).start()
        quarter_copy(layer, 2).start()
        arrive(base + 2)
        ag_near(ag_m)
        here("up")
        up_half(layer, ag_m, near)
        here("up near")
        ag_far(ag_m)
        up_half(layer, ag_m, far)
        here("up far")
        arrive(base + 3)
        here("down")
        scatter_far(
            rs_f,
            lambda i: dot_nt(both(hid, at=far_rows(i)), wd[layer]).astype(BF),
            lambda i: here(f"down {i}"),
        )
        part[half_rows(near), :] = dot_nt(hid[half_rows(near), :], wd[layer]).astype(BF)
        rs_near(rs_f)
        if layer == 0:
            quarter_pass(0)
        here("down near")

    forward_layer(0)
    rs_each(
        RS_F0,
        norm_into(RS_F0, own_m, 0, 1, g2, b2, own_x, AG_X1),
        gather(AG_X1),
        lambda i: weights_at(0, f"last norm {i}"),
    )
    forward_layer(1)

    def prefix_copy(layer, i, d):
        kt = lax.rem(k + d, KEYS)
        source = (gk, gv)[i]
        return pltpu.make_async_remote_copy(
            src_ref=source.at[pl.ds(pl.multiple_of(kt * count, count), count), :],
            dst_ref=pg.at[layer, i, :, columns],
            send_sem=pg_send.at[i, d], recv_sem=pg_recv.at[i, d],
            device_id=(r, kt), device_id_type=MESH,
        )

    def prefix_own(layer, i):
        return pltpu.make_async_copy(
            (gk, gv)[i].at[pl.ds(pl.multiple_of(k * count, count), count), :],
            pg.at[layer, i, :, columns],
            pg_recv.at[i, 0],
        )

    bits = rows.bit_length() - 1

    def row_copy(layer, b):
        bit = 1 << b
        partner = r + bit - 2 * bit * lax.rem(r // bit, 2)
        return pltpu.make_async_remote_copy(
            src_ref=pg_low.at[layer], dst_ref=pg_in.at[layer, b],
            send_sem=pgr_send.at[layer, b], recv_sem=pgr_recv.at[layer, b],
            device_id=(partner, k), device_id_type=MESH,
        )

    def row_start(layer, b):
        low = pg[layer].astype(BF)
        pg_low[layer] = low
        pg[layer] = low.astype(F32)
        row_copy(layer, b).start()

    def row_step(layer, b):
        row_copy(layer, b).wait()
        pg[layer] += pg_in[layer, b].astype(F32)
        if b + 1 < bits:
            row_start(layer, b + 1)

    def prefix_start(layer):
        for i in range(2):
            prefix_own(layer, i).start()
            for d in range(1, KEYS):
                prefix_copy(layer, i, d).start()

    def prefix_take(layer):
        for i in range(2):
            prefix_own(layer, i).wait()
            for d in range(1, KEYS):
                prefix_copy(layer, i, d).wait_recv()
        row_start(layer, 0)

    def prefix_sent(layer):
        for i in range(2):
            for d in range(1, KEYS):
                prefix_copy(layer, i, d).wait_send()

    for layer in reversed(range(LAYERS)):
        rs_gm, rs_gx = ((RS_GM0, RS_GX0), (RS_GM1, RS_GX1))[layer]
        ag_gf = (AG_GF0, AG_GF1)[layer]
        if layer == LAYERS - 1:
            forth = norm_into(RS_F1, own_m, 1, 1, g2, b2, own_x, AG_ACT)
            back = norm_back(lambda i: cot[i : i + 16, :].astype(F32), layer, 1, g2, into(ag_gf))

            def turn(i):
                forth(i)
                back(i)

            rs_each(RS_F1, turn, gather(ag_gf))
        else:
            rs_each(
                RS_GX1,
                norm_back(lambda i: own_g[i : i + 16, :] + rs_sum(RS_GX1, i), layer, 1, g2, into(ag_gf)),
                gather(ag_gf),
            )
            prefix_take(layer + 1)
        ag_near(ag_gf)
        part[half_rows(near), :] = ff_back(layer, full[ag_gf, half_rows(near), :], gelu_d[layer, half_rows(near), :])
        rs_near(rs_gm)

        def step(i):
            ag_got(ag_gf, i)
            at = far_rows(i)
            return ff_back(layer, both(full, ag_gf, at=at), both(gelu_d, layer, at=at))

        if layer == LAYERS - 1:
            quarter_pass(layer)
        scatter_far(rs_gm, step, lambda i: ag_pass(ag_gf, i), early=True)
        if layer == 0:
            row_step(1, 0)
        gk[...] = jnp.zeros_like(gk)
        gv[...] = jnp.zeros_like(gv)
        quarter_got(layer)

        def keep(i, low):
            ga[i : i + 16, :] = low

        rs_each(
            rs_gm,
            norm_back(lambda i: own_g[i : i + 16, :] + rs_sum(rs_gm, i), layer, 0, g1, keep),
            go_leave(layer),
        )
        if layer == LAYERS - 1:
            for i in range(SUBS + 1):
                ag_copy(AG_ACT, i).start()
        go_wait(3 - 2 * c)
        two(functools.partial(attend_back, layer), near)
        if layer == 0:
            row_step(1, 1)
        go_wait(2)
        go_wait(1 + 2 * c)
        two(functools.partial(attend_back, layer), far)
        for d in range(1, KEYS):
            for i in range(SUBS):
                go_copy(d, i).wait_send()
        prefix_start(layer)

        def narrow(which):
            def body(i):
                i = which * half + i
                gqkv[rows_at(i, 16), wide : 2 * wide] = gk[rows_at(prefix + i, 16), :].astype(BF)
                gqkv[rows_at(i, 16), 2 * wide : 3 * wide] = gv[rows_at(prefix + i, 16), :].astype(BF)

            chunks(half, body)

        narrow(far)
        project_back(layer, block_b * own, own)
        for i in range(SUBS):
            rs_copy(rs_gx, i).start()
        project_back(layer, block_a * own, own)
        for i in range(SUBS):
            rs_mid(rs_gx, i)
        narrow(near)
        project_back(layer, near * half, half)
        rs_near(rs_gx)
        if layer == LAYERS - 1:
            ag_far(AG_ACT)
            ag_near(AG_ACT)
        else:
            for b in range(2, bits):
                row_step(1, b)
            prefix_take(0)
        prefix_sent(layer)

    act_copy = pltpu.make_async_copy(full.at[AG_ACT], low_out.at[1], loc.at[13])
    act_copy.start()

    def last(i):
        full[AG_GX, rows_at(k * own + i, 16), :] = (own_g[i : i + 16, :] + rs_sum(RS_GX0, i)).astype(BF)

    rs_each(RS_GX0, last, gather(AG_GX), lambda i: row_step(0, 0) if i == SUBS - 1 else None)
    for p in range(4 * LAYERS):
        drain(p)
    for i in range(2):
        for d in range(1, KEYS):
            pre_copy(i, d).wait_send()
    ag_near(AG_GX)

    def grad_copy(which):
        return pltpu.make_async_copy(
            full.at[AG_GX, half_rows(which), :], low_out.at[0, half_rows(which), :], loc.at[14 + (which is far)]
        )

    grad_copy(near).start()
    ag_far(AG_GX, lambda: row_step(0, 1))
    grad_copy(far).start()
    for b in range(2, bits):
        row_step(0, b)
    for i in range(2):
        for layer in range(LAYERS):
            prefix_out[i, layer] = pg[layer, i]
    ag_end(AG_GX)
    ag_end(AG_ACT)
    for layer in range(LAYERS):
        for i in range(4):
            quarter_copy(layer, i).wait_send()
    act_copy.wait()
    grad_copy(near).wait()
    grad_copy(far).wait()


def results(low, grads, act, gt, gpk, gpv, narrow, broad, act_held, grads_held, sems):
    parts, size = narrow.shape[:2]

    def taken(i):
        return pltpu.make_async_copy(low.at[0, i * size : (i + 1) * size, :], narrow.at[i], sems.at[0, i])

    def given(i):
        return pltpu.make_async_copy(broad.at[i], gt.at[0, i * size : (i + 1) * size, :], sems.at[1, i])

    in_act = pltpu.make_async_copy(low.at[1], act_held, sems.at[2, 0])
    out_act = pltpu.make_async_copy(act_held, act.at[0], sems.at[2, 0])
    in_grads = pltpu.make_async_copy(grads, grads_held, sems.at[2, 1])
    out_grads = [pltpu.make_async_copy(grads_held.at[i], (gpk, gpv)[i], sems.at[2, 2 + i]) for i in range(2)]
    for i in range(parts):
        taken(i).start()
    in_act.start()
    in_grads.start()
    for i in range(parts):
        taken(i).wait()
        broad[i] = narrow[i].astype(F32)
        given(i).start()
    in_act.wait()
    out_act.start()
    in_grads.wait()
    for copy in out_grads:
        copy.start()
    for i in range(parts):
        given(i).wait()
    out_act.wait()
    for copy in out_grads:
        copy.wait()


def per_device(
    tokens, cotangent, segment_ids, pad_mask, prefix_keys, prefix_values,
    w_query, w_key, w_value, w_out, w_up, w_down_t,
    norm1_gain, norm1_bias, norm2_gain, norm2_bias,
):
    rows, keys = lax.axis_size("rows"), lax.axis_size("keys")
    assert keys == KEYS and rows % (2 * KEYS) == 0 and rows & (rows - 1) == 0
    tok, width = tokens.shape[1:]
    count = prefix_keys.shape[1]
    prefix = count * keys
    local_ff = w_up.shape[2]
    wide, own, window = width // keys, tok // keys, 3 * tok // keys
    heads = wide // HEAD
    nz, bits, pieces = rows // 2, rows.bit_length() - 1, 4 * LAYERS
    vmem, anywhere = pl.BlockSpec(memory_space=pltpu.VMEM), pl.BlockSpec(memory_space=pl.ANY)
    dma = pltpu.SemaphoreType.DMA
    scratch = [
        pltpu.VMEM((LAYERS, width, 3 * wide), BF),
        pltpu.VMEM((LAYERS, width, width), BF),
        pltpu.VMEM((LAYERS, width, local_ff), BF),
        pltpu.VMEM((LAYERS, width, local_ff), BF),
        pltpu.VMEM((LAYERS, prefix, wide), BF),
        pltpu.VMEM((LAYERS, prefix, wide), BF),
        pltpu.VMEM((tok, width), BF),
        pltpu.VMEM((SCATTERS, 2, own, width), BF),
        pltpu.VMEM((SCATTERS, own, width), BF),
        pltpu.VMEM((own, width), BF),
        pltpu.VMEM((GATHERS, tok, width), BF),
        pltpu.VMEM((LAYERS, tok, 3 * wide), BF),
        pltpu.VMEM((LAYERS, keys, prefix + window, heads * own), F32),
        pltpu.VMEM((LAYERS, tok, local_ff), F32),
        pltpu.VMEM((2 * LAYERS, own, width), F32),
        pltpu.VMEM((2 * LAYERS, own, 1), F32),
        pltpu.VMEM((own, width), F32),
        pltpu.VMEM((own, width), F32),
        pltpu.VMEM((own, width), F32),
        pltpu.VMEM((own, width), BF),
        pltpu.VMEM((tok, wide), BF),
        pltpu.VMEM((tok, 3 * wide), BF),
        pltpu.VMEM((prefix + tok, wide), F32),
        pltpu.VMEM((prefix + tok, wide), F32),
        pltpu.VMEM((tok, width), BF),
        pltpu.VMEM((tok, local_ff), BF),
        pltpu.VMEM((own, width), BF),
        pltpu.VMEM((own, width), BF),
        pltpu.VMEM((tok, wide), BF),
        pltpu.VMEM((keys, prefix + window, own), F32),
        pltpu.VMEM((tok, own), F32),
        pltpu.VMEM((LAYERS, 2, count, width), F32),
        pltpu.VMEM((LAYERS, 2, count, width), BF),
        pltpu.VMEM((LAYERS, bits, 2, count, width), BF),
        dma((pieces + 1, nz + 1)),
        dma((pieces, 2, nz)),
        dma((pieces, nz)),
        dma((16,)),
        dma((2, keys)),
        dma((2, keys)),
        dma((LAYERS, 4)),
        dma((LAYERS, 4)),
        dma((keys, SUBS)),
        dma((keys, SUBS)),
        dma((2 * SUBS + 1,)),
        dma((2 * SUBS + 1,)),
        dma((2, 2 * SUBS + 1)),
        dma((2, 2 * SUBS + 1)),
        dma((2, keys)),
        dma((2, keys)),
        dma((LAYERS, bits)),
        dma((LAYERS, bits)),
    ]
    low, grads = pl.pallas_call(
        functools.partial(kernel, (rows, tok, width, local_ff)),
        out_shape=(
            jax.ShapeDtypeStruct((2, tok, width), BF),
            jax.ShapeDtypeStruct((2, LAYERS, count, width), F32),
        ),
        in_specs=[anywhere, anywhere, vmem, vmem] + [anywhere] * 8 + [vmem] * 4,
        out_specs=(anywhere, vmem),
        scratch_shapes=scratch,
        compiler_params=pltpu.CompilerParams(
            collective_id=0, has_side_effects=True, vmem_limit_bytes=62 * 1024 * 1024 - 512 * 1024
        ),
    )(
        tokens[0], cotangent[0], segment_ids, pad_mask, prefix_keys, prefix_values,
        w_query, w_key, w_value, w_out, w_up, w_down_t,
        norm1_gain, norm1_bias, norm2_gain, norm2_bias,
    )
    whole = (LAYERS, count, width)
    return pl.pallas_call(
        results,
        out_shape=(
            jax.ShapeDtypeStruct((1, tok, width), BF),
            jax.ShapeDtypeStruct((1, tok, width), F32),
            jax.ShapeDtypeStruct(whole, F32),
            jax.ShapeDtypeStruct(whole, F32),
        ),
        in_specs=[anywhere] * 2,
        out_specs=(anywhere,) * 4,
        scratch_shapes=[
            pltpu.VMEM((2 * keys, own // 2, width), BF),
            pltpu.VMEM((2 * keys, own // 2, width), F32),
            pltpu.VMEM((tok, width), BF),
            pltpu.VMEM((2, *whole), F32),
            dma((3, 2 * keys)),
        ],
    )(low, grads)


def solution(mesh):
    row3 = P("rows", None, None)
    weight = P(None, "rows", None)
    return jax.shard_map(
        per_device,
        mesh=mesh,
        in_specs=(
            row3,
            row3,
            P("rows", None),
            P("rows", None),
            P(None, "keys", None),
            P(None, "keys", None),
            weight,
            weight,
            weight,
            weight,
            P(None, "rows", "keys"),
            P(None, "rows", "keys"),
            P(),
            P(),
            P(),
            P(),
        ),
        out_specs=(row3, row3, P(None, "keys", None), P(None, "keys", None)),
        check_vma=False,
    )
```
